128 devices in a mesh: ctx: 16 (over x, y_hi, core), fsdp: 8 (over y_lo, z).
Axes of the slice: x: 4, y: 4 (y_hi: 2, y_lo: 2; y = y_hi * 2 + y_lo), z: 4, core: 2. Of those that a mesh axis runs over, the one named last changes fastest.
Arguments:
- hidden: bfloat16 [8, 2048, 1024], P('fsdp', 'ctx'), may hold values from -6 to 6
- teacher: bfloat16 [8, 2048, 1024], P('fsdp', 'ctx'), may hold values from -6 to 6
- lengths: int32 [8, 5], P('fsdp'), may hold values from 1 to 1024, as said below
- tile_perm: int32 [8, 16], P('fsdp'), may hold values from 0 to 15, as said below
- routes: int32 [8, 2048, 8], P('fsdp', 'ctx'), may hold values from 0 to 31, all different within a row; in each aligned block of 128 rows (0 to 127, 128 to 255, ..., all dimensions but the last counted through in order) at most 36 rows name the same one
- norm_attn: bfloat16 [1024], P('fsdp'), may hold values from 0.5 to 1.5
- w_query: bfloat16 [1024, 1024], P('fsdp'), may hold values from -0.1875 to 0.1875
- w_key: bfloat16 [1024, 512], P('fsdp'), may hold values from -0.1875 to 0.1875
- w_value: bfloat16 [1024, 512], P('fsdp'), may hold values from -0.1875 to 0.1875
- w_out: bfloat16 [1024, 1024], P('fsdp'), may hold values from -4 to 4
- q_gain: bfloat16 [1024], P('fsdp'), may hold values from 0.5 to 1.5
- k_gain: bfloat16 [512], P('fsdp'), may hold values from 0.5 to 1.5
- norm_ffn: bfloat16 [1024], P('fsdp'), may hold values from 0.5 to 1.5
- w_router: bfloat16 [1024, 32], P('fsdp'), may hold values from -0.25 to 0.25
- w_gate: bfloat16 [32, 1024, 512], P('ctx', 'fsdp'), may hold values from -0.1875 to 0.1875
- w_up: bfloat16 [32, 1024, 512], P('ctx', 'fsdp'), may hold values from -0.1875 to 0.1875
- w_down: bfloat16 [32, 512, 1024], P('ctx', 'fsdp'), may hold values from -6 to 6
Outputs:
- output: bfloat16 [8, 2048, 1024], P('fsdp', 'ctx')
- loss: float32 [], replicated
- input_grad: float32 [8, 2048, 1024], P('fsdp', 'ctx')
- grad_norm_attn: float32 [1024], P('fsdp')
- grad_query: float32 [1024, 1024], P('fsdp')
- grad_key: float32 [1024, 512], P('fsdp')
- grad_value: float32 [1024, 512], P('fsdp')
- grad_out: float32 [1024, 1024], P('fsdp')
- grad_q_gain: float32 [1024], P('fsdp')
- grad_k_gain: float32 [512], P('fsdp')
- grad_norm_ffn: float32 [1024], P('fsdp')
- grad_router: float32 [1024, 32], P('fsdp')
- grad_gate: float32 [32, 1024, 512], P('ctx', 'fsdp')
- grad_up: float32 [32, 1024, 512], P('ctx', 'fsdp')
- grad_down: float32 [32, 512, 1024], P('ctx', 'fsdp')
The draws below stay inside these ranges and needn't reach their ends.
Inputs may be any that keep to these rules, and one draw needn't show every extreme that they name: Row g holds the 5 lengths of group g; sequence i takes ceil(length / 128) whole tiles, these counts sum to 16, and one sequence of each group is exactly 1024 long. Each row is a permutation of 0 to 15: slot s, rows s * 128 to s * 128 + 127 of the group, holds tile tile_perm[g, s] of the group's sequences laid end to end in order. `routes`: each row names 8 different experts; among the 128 rows of one device no expert is named more than 36 times.
All inputs are finite; a program needn't handle non-finite values.
Results may differ from the reference program's by a relative error of at most 0.025.
Values may be sent and summed in bfloat16 or wider, within the bound.
No kernel may reach another device: no remote copies, remote signals or barrier semaphores. Data moves between devices by JAX's collectives and lax.ppermute only.
A program may use at most 128 MiB of HBM per device.

```python
import math
import jax
import jax.numpy as jnp
import numpy as np
from jax import lax

D = 1024
HEADS = 16
KV_HEADS = 8
HEAD_DIM = 64
FF = 512
TOP = 8
EXPERTS = 32
TILE = 128
TILE_DEV = 1
SEQS = 5
TOK_DEV = 128
GROUP = 2048
TILES = 16
CAP = 36
LOSS_SCALE = 8388608
N_CTX = 16
N_FSDP = 8


def layout_pair(key):

    def one_group(group_key):
        half_tiles = TILES // 2
        keys_split = jax.random.split(group_key, 5)
        cut_points = jnp.sort(jax.random.permutation(keys_split[0], half_tiles - 1)[:SEQS - 2] + 1).astype(jnp.int32)
        bounds = jnp.concatenate([jnp.zeros((1,), jnp.int32), cut_points, jnp.full((1,), half_tiles, jnp.int32)])
        others = bounds[1:] - bounds[:-1]
        long_index = jax.random.randint(keys_split[1], (), 0, SEQS)
        seq_index = jnp.arange(SEQS)
        before = others[jnp.clip(seq_index, 0, SEQS - 2)]
        behind = others[jnp.clip(seq_index - 1, 0, SEQS - 2)]
        counts = jnp.where(seq_index < long_index, before, jnp.where(seq_index == long_index, half_tiles, behind))
        remainder = jax.random.randint(keys_split[2], (SEQS,), 1, TILE + 1)
        seq_lengths = (counts - 1) * TILE + jnp.where(seq_index == long_index, TILE, remainder)
        starts = jnp.cumsum(counts) - counts
        long_start = jnp.sum(jnp.where(seq_index == long_index, starts, 0))
        tile_ids = jnp.arange(TILES)
        is_long = (tile_ids >= long_start) & (tile_ids < long_start + half_tiles)
        tile_key = jax.random.permutation(keys_split[3], TILES) + jnp.where(is_long, 0, TILES)
        tile_order = jnp.argsort(tile_key)
        middle = TILES // TILE_DEV // 2 * TILE_DEV
        fixed_key = jnp.where(tile_ids == 0, 0, jnp.where(tile_ids == middle, 1, jnp.where(tile_ids == TILES - 1, 2, -1)))
        slot_key = jnp.where(fixed_key >= 0, fixed_key, jax.random.permutation(keys_split[4], TILES) + 3)
        slot_order = jnp.argsort(slot_key)
        slot_tiles = jnp.zeros((TILES,), jnp.int32).at[slot_order].set(tile_order.astype(jnp.int32))
        return (seq_lengths.astype(jnp.int32), slot_tiles)
    group_keys = jax.vmap(lambda number: jax.random.fold_in(key, number))(jnp.arange(N_FSDP))
    return jax.vmap(one_group)(group_keys)


def draw_lengths(key, part):
    shared = layout_pair(key)
    return shared[0]


def draw_tile_perm(key, part):
    shared = layout_pair(key)
    return shared[1]


def block_levels(rng, extent, cuts, least, largest):
    def one(axis_at, blocks):
        draws = jax.random.uniform(jax.random.fold_in(jax.random.fold_in(rng, 6), axis_at), (blocks,), jnp.float32, least / len(cuts), largest / len(cuts))
        return jnp.repeat(jnp.exp(draws), extent[axis_at] // blocks).reshape((-1,) + (1,) * (len(extent) - axis_at - 1))

    level = one(*cuts[0])
    for cut in cuts[1:]:
        level = level * one(*cut)
    return level


def routed_block(key, own, number, rows, count, top, bound, skew):
    order = jax.random.permutation(key, count)
    packed, usual = shares(count, rows * top, bound, skew, True), shares(count, rows * top, bound, skew, False)
    places = jnp.arange(count)

    def named(tallies, offset_by):
        used = int((tallies > 0).sum())
        fixed = max(1, used // 4)
        moved = fixed + (places - fixed + offset_by * (used - fixed)) % max(1, count - fixed)
        return jnp.zeros((count,), jnp.int32).at[order[jnp.where(places < fixed, places, moved)]].set(jnp.asarray(tallies, jnp.int32))

    tallies = jnp.where(number % 4 == 0, named(packed, number // 4), named(usual, number - number // 4 - 1))
    mixed = jax.random.permutation(jax.random.fold_in(own, 3), count)
    donor, receiver = mixed[0:count // 2 * 2:2], mixed[1:count // 2 * 2:2]
    slack = jnp.minimum(tallies[donor] - 1, bound - tallies[receiver]) // 2
    slack = jnp.where((donor == order[0]) | (receiver == order[0]) | (tallies[receiver] == 0), 0, jnp.maximum(slack, 0))
    moved = jax.random.randint(jax.random.fold_in(own, 4), (count // 2,), 0, 1 << 20) % (slack + 1)
    tallies = tallies.at[donor].add(-moved).at[receiver].add(moved)
    members = jnp.searchsorted(jnp.cumsum(tallies), jnp.arange(rows * top), side="right").astype(jnp.int32)
    grid = members.reshape(top, rows).T
    grid = grid[jax.random.permutation(jax.random.fold_in(own, 1), rows)]
    offset_by = jax.random.randint(jax.random.fold_in(own, 2), (rows, 1), 0, top)
    return jnp.take_along_axis(grid, (jnp.arange(top)[None, :] + offset_by) % top, axis=1)


def shares(count, total, reach, skew, full):
    portions = [(1 << 20) // math.isqrt(standing ** skew) + 1 for standing in range(1, count + 1)]
    largest = reach if full else min(reach, max(-(-total // count), total * portions[0] // sum(portions)))
    least = 1 if total - largest >= count - 1 else 0
    holding, rest = [largest] + [least] * (count - 1), total - largest - least * (count - 1)
    while rest > 0:
        candidates = [i for i in range(1, count) if holding[i] < largest] or [i for i in range(1, count) if holding[i] < reach]
        mass, remaining = sum([portions[i] for i in candidates]), rest
        for i in candidates:
            extra = min(reach - holding[i], max(1, remaining * portions[i] // mass), rest)
            holding[i] = holding[i] + extra
            rest = rest - extra
    return np.array(holding)


def normal_values(own_key, extent, scale, bound, cuts=(), kind=jnp.bfloat16):
    level = block_levels(own_key, extent, cuts, -0.22, 0.18) if cuts else 1.0
    entries = jax.random.normal(own_key, extent, jnp.float32) * scale * level
    return jnp.minimum(jnp.maximum(entries, -bound), bound).astype(kind)


def setup_inputs(seed: int = 0) -> dict:
    seeds = jax.random.split(jax.random.key(seed), 18)
    hidden = normal_values(seeds[0], (N_FSDP, GROUP, D), 1.0, 6.0, ((0, 8), (1, 16)))
    teacher = normal_values(seeds[1], (N_FSDP, GROUP, D), 1.0, 6.0, ((0, 8), (1, 16)))
    lengths = draw_lengths(jax.random.fold_in(seeds[17], 71), 0)
    tile_perm = draw_tile_perm(jax.random.fold_in(seeds[17], 71), 0)
    routes_keys = jax.random.split(jax.random.fold_in(seeds[4], 1), N_FSDP * GROUP // TOK_DEV)
    routes_turns = jax.random.permutation(jax.random.fold_in(seeds[4], 3), N_FSDP * GROUP // TOK_DEV)
    routes = jax.vmap(lambda own, number: routed_block(jax.random.fold_in(seeds[4], 2), own, number, TOK_DEV, EXPERTS, TOP, CAP, 1))(routes_keys, routes_turns).reshape((N_FSDP, GROUP, TOP))
    norm_attn = jnp.clip(1.0 + 0.1 * jax.random.normal(seeds[5], (D,), jnp.float32), 0.5, 1.5).astype(jnp.bfloat16)
    w_query = normal_values(seeds[6], (D, HEADS * HEAD_DIM), D ** -0.5, 0.1875, ((0, 8),))
    w_key = normal_values(seeds[7], (D, KV_HEADS * HEAD_DIM), D ** -0.5, 0.1875, ((0, 8),))
    w_value = normal_values(seeds[8], (D, KV_HEADS * HEAD_DIM), D ** -0.5, 0.1875, ((0, 8),))
    w_out = normal_values(seeds[9], (HEADS * HEAD_DIM, D), (8 / (HEADS * HEAD_DIM) ** 0.5), 4.0, ((0, 8),))
    q_gain = jnp.clip(1.0 + 0.1 * jax.random.normal(seeds[10], (HEADS * HEAD_DIM,), jnp.float32), 0.5, 1.5).astype(jnp.bfloat16)
    k_gain = jnp.clip(1.0 + 0.1 * jax.random.normal(seeds[11], (KV_HEADS * HEAD_DIM,), jnp.float32), 0.5, 1.5).astype(jnp.bfloat16)
    norm_ffn = jnp.clip(1.0 + 0.1 * jax.random.normal(seeds[12], (D,), jnp.float32), 0.5, 1.5).astype(jnp.bfloat16)
    w_router = normal_values(seeds[13], (D, EXPERTS), (0.5 / D ** 0.5), 0.25, ((0, 8),))
    w_gate = normal_values(seeds[14], (EXPERTS, D, FF), D ** -0.5, 0.1875, ((0, 16), (1, 8)))
    w_up = normal_values(seeds[15], (EXPERTS, D, FF), D ** -0.5, 0.1875, ((0, 16), (1, 8)))
    w_down = normal_values(seeds[16], (EXPERTS, FF, D), (16 / FF ** 0.5), 6.0, ((0, 16), (1, 8)))
    return {"hidden": hidden, "teacher": teacher, "lengths": lengths, "tile_perm": tile_perm, "routes": routes, "norm_attn": norm_attn, "w_query": w_query, "w_key": w_key, "w_value": w_value, "w_out": w_out, "q_gain": q_gain, "k_gain": k_gain, "norm_ffn": norm_ffn, "w_router": w_router, "w_gate": w_gate, "w_up": w_up, "w_down": w_down}


eps = 1e-05
theta = 10000.0
highest = lax.Precision.HIGHEST

@jax.custom_vjp
def low(v):
    return lax.optimization_barrier(v.astype(jnp.bfloat16)).astype(jnp.float32)

@jax.custom_vjp
def low_back(v):
    return v

def low_keep(v):
    return (low(v), None)

def low_pass(kept, grad):
    return (grad,)

def back_keep(v):
    return (v, None)

def back_low(kept, grad):
    return (low(grad),)
low.defvjp(low_keep, low_pass)
low_back.defvjp(back_keep, back_low)

def normalize(values, gain):
    return values * lax.rsqrt(lax.optimization_barrier(jnp.mean(values * values, -1, keepdims=True)) + eps) * gain

def rotary(values, positions):
    row_count = values.shape[0]
    per_head = values.reshape(row_count, -1, HEAD_DIM)
    half_dim = HEAD_DIM // 2
    inverse = theta ** (-jnp.arange(half_dim, dtype=jnp.float32) / half_dim)
    angles = positions.astype(jnp.float32)[:, None, None] * inverse[None, None, :]
    cos_table = jnp.cos(angles)
    sin_table = jnp.sin(angles)
    lower_half = per_head[..., :half_dim]
    upper_half = per_head[..., half_dim:]
    turned = jnp.concatenate([lower_half * cos_table - upper_half * sin_table, upper_half * cos_table + lower_half * sin_table], -1)
    return turned.reshape(row_count, -1)

def slot_table(row_ids, lengths, tile_perm):
    tile_count = (lengths + TILE - 1) // TILE
    starts = jnp.cumsum(tile_count) - tile_count
    tile_slot = row_ids // TILE
    matches = tile_slot[:, None] == jnp.arange(tile_perm.shape[0], dtype=jnp.int32)[None, :]
    canonical = lax.optimization_barrier(jnp.sum(jnp.where(matches, tile_perm[None, :], 0), 1))
    seq_ids = lax.optimization_barrier(jnp.sum((starts[None, :] <= canonical[:, None]).astype(jnp.int32), 1)) - 1
    in_sequence = seq_ids[:, None] == jnp.arange(lengths.shape[0], dtype=jnp.int32)[None, :]
    first_tile = lax.optimization_barrier(jnp.sum(jnp.where(in_sequence, starts[None, :], 0), 1))
    seq_length = lax.optimization_barrier(jnp.sum(jnp.where(in_sequence, lengths[None, :], 0), 1))
    positions = (canonical - first_tile) * TILE + row_ids % TILE
    return (seq_ids, positions, positions < seq_length)

def attention(queries, keys_in, values_in, seq_ids, positions, valid):
    block_rows = math.gcd(GROUP, 512)
    key_heads = keys_in.reshape(GROUP, KV_HEADS, HEAD_DIM)
    value_heads = values_in.reshape(GROUP, KV_HEADS, HEAD_DIM)
    factor = HEAD_DIM ** (-0.5)

    def one_block(pieces):
        query_block, query_seq, query_pos = pieces
        qheads = query_block.reshape(block_rows, KV_HEADS, HEADS // KV_HEADS, HEAD_DIM)
        raw_scores = jnp.einsum('qhgd,khd->hgqk', qheads, key_heads, precision=highest) * factor
        allowed = (query_seq[:, None] == seq_ids[None, :]) & (positions[None, :] <= query_pos[:, None]) & valid[None, :]
        scores = low_back(jnp.where(allowed[None, None], raw_scores, -1000000000.0))
        row_max = lax.optimization_barrier(jnp.max(scores, -1, keepdims=True))
        weights = jnp.exp(scores - row_max)
        totals = lax.optimization_barrier(jnp.sum(weights, -1))
        summed = jnp.einsum('hgqk,khd->qhgd', low(weights), value_heads, precision=highest)
        attended = low_back(summed) / jnp.transpose(totals, (2, 0, 1))[..., None]
        return attended.reshape(block_rows, -1)
    blocks = (queries.reshape(GROUP // block_rows, block_rows, -1), seq_ids.reshape(-1, block_rows), positions.reshape(-1, block_rows))
    return lax.map(jax.checkpoint(one_block), blocks).reshape(GROUP, -1)

def group_pass(params, inputs):
    norm_attn, w_query, w_key, w_value, w_out, q_gain, k_gain, norm_ffn, w_router, w_gate, w_up, w_down = params
    hidden_in, target, lengths, tile_perm, routes = inputs
    row_ids = jnp.arange(GROUP, dtype=jnp.int32)
    seq_ids, positions, valid = slot_table(row_ids, lengths, tile_perm)
    normed = low(normalize(hidden_in, norm_attn))
    query_lin = low_back(jnp.dot(normed, w_query, precision=highest))
    key_lin = low_back(jnp.dot(normed, w_key, precision=highest))
    values_use = low_back(low(jnp.dot(normed, w_value, precision=highest)))
    query_use = low(rotary(normalize(query_lin, q_gain), positions))
    key_use = low(rotary(normalize(key_lin, k_gain), positions))
    mixed_heads = attention(query_use, key_use, values_use, seq_ids, positions, valid)
    residual = hidden_in + low_back(jnp.dot(low(mixed_heads), w_out, precision=highest))
    post_norm = low(normalize(residual, norm_ffn))
    logits = low_back(jnp.dot(post_norm, w_router, precision=highest))
    shifted = jnp.exp(logits - lax.optimization_barrier(jnp.max(logits, -1, keepdims=True)))
    router_probs = shifted / lax.optimization_barrier(jnp.sum(shifted, -1, keepdims=True))
    pick_table = routes[:, :, None] == jnp.arange(EXPERTS, dtype=jnp.int32)[None, None, :]
    chosen = lax.optimization_barrier(jnp.sum(jnp.where(pick_table, router_probs[:, None, :], 0.0), -1))
    flat_routes = routes.reshape(-1)
    onehot = (flat_routes[:, None] == jnp.arange(EXPERTS, dtype=jnp.int32)[None, :]).astype(jnp.int32)
    slot_rank = lax.optimization_barrier(jnp.sum((jnp.cumsum(onehot, 0) - 1) * onehot, 1))
    group_room = N_CTX * CAP
    slot_index = flat_routes * group_room + slot_rank
    sources = jnp.zeros((EXPERTS * group_room,), jnp.int32).at[slot_index].set(jnp.arange(GROUP * TOP, dtype=jnp.int32) // TOP)
    slot_used = jnp.zeros((EXPERTS * group_room,), jnp.float32).at[slot_index].set(1.0)
    rows_in = (low_back(post_norm[sources]) * slot_used[:, None]).reshape(EXPERTS, group_room, D)
    gates_pre = low_back(jnp.einsum('erd,edf->erf', rows_in, w_gate, precision=highest))
    up_pre = low_back(jnp.einsum('erd,edf->erf', rows_in, w_up, precision=highest))
    activated = low(jax.nn.silu(gates_pre) * up_pre)
    expert_out = low_back(low(jnp.einsum('erf,efd->erd', activated, w_down, precision=highest)))
    returned = expert_out.reshape(-1, D)[slot_index].reshape(GROUP, TOP, D)
    result = residual + lax.optimization_barrier(jnp.sum(chosen[:, :, None] * returned, 1))
    errors = (result - target) * valid.astype(jnp.float32)[:, None]
    return (result, jnp.sum(errors * errors))

def reference(hidden, teacher, lengths, tile_perm, routes, norm_attn, w_query, w_key, w_value, w_out, q_gain, k_gain, norm_ffn, w_router, w_gate, w_up, w_down):
    params = tuple((weight.astype(jnp.float32) for weight in (norm_attn, w_query, w_key, w_value, w_out, q_gain, k_gain, norm_ffn, w_router, w_gate, w_up, w_down)))
    hidden_in = hidden.astype(jnp.float32)
    target = teacher.astype(jnp.float32)
    valid_count = jnp.sum(lengths).astype(jnp.float32)

    def forward(weights, inputs_all):

        def scan_group(carried, inputs):
            result, squares = jax.checkpoint(group_pass)(weights, inputs)
            return (carried, (result, squares))
        unused, (results, squares) = lax.scan(scan_group, jnp.zeros((), jnp.float32), (inputs_all, target, lengths, tile_perm, routes))
        return (results, jnp.sum(squares) / (valid_count * D))
    (results, loss_value), pullback = jax.vjp(forward, params, hidden_in)
    weight_grads, input_grad = pullback((jnp.zeros_like(results), jnp.asarray(LOSS_SCALE, jnp.float32)))
    return (results.astype(jnp.bfloat16), loss_value, input_grad, weight_grads[0], weight_grads[1], weight_grads[2], weight_grads[3], weight_grads[4], weight_grads[5], weight_grads[6], weight_grads[7], weight_grads[8], weight_grads[9], weight_grads[10], weight_grads[11])
```

```python
import functools

import jax
import jax.numpy as jnp
import numpy as np
from jax import lax
from jax.experimental import pallas as pl
from jax.experimental.pallas import tpu as pltpu
from jax.sharding import PartitionSpec as P

TILE = 128
HD = 64
CAP = 40
SLOTS = 16 * CAP
EPS = 1e-05
F32 = jnp.float32
BF = jnp.bfloat16

ROW_GAIN = 192
ROW_ROUTER = 208
ROWS_IN = 240
ROW_OUT = 128
ROW_GR = 192
ROW_NF = 224
ROW_LOSS = 226
ROWS_OUT = 240

CORE = [(i, i ^ 1) for i in range(16)]
YHI = [(i, i ^ 2) for i in range(16)]
XUP = [(i, (i + 4) % 16) for i in range(16)]
XDOWN = [(i, (i - 4) % 16) for i in range(16)]
XTWO = [(i, (i + 8) % 16) for i in range(16)]
YLO = [(i, i ^ 4) for i in range(8)]
ZUP = [(i, (i // 4) * 4 + (i + 1) % 4) for i in range(8)]
ZDOWN = [(i, (i // 4) * 4 + (i - 1) % 4) for i in range(8)]
ZTWO = [(i, (i // 4) * 4 + (i + 2) % 4) for i in range(8)]
PIECES = [
    (dx, dy, dc)
    for dc in (0, 1)
    for dx, dy in ((0, 0), (0, 1), (-1, 0), (1, 0), (-1, 1), (1, 1), (2, 0), (2, 1))
]


def ctx_move(value, pairs):
    return lax.ppermute(value, "ctx", pairs)


def fsdp_move(value, pairs):
    return lax.ppermute(value, "fsdp", pairs)


def dims(left, right):
    return (((left,), (right,)), ((), ()))


def dot(a, b, left=1, right=0, precision=None):
    return lax.dot_general(
        a, b, dims(left, right), preferred_element_type=F32, precision=precision
    )


def split(value):
    high = value.astype(BF)
    return high, (value - high.astype(F32)).astype(BF)


def iota(shape, axis):
    return lax.broadcasted_iota(jnp.int32, shape, axis)


def kernel_call(body, outs, args, smem=(), scratch=(), name=None, flops=0):
    specs = [
        pl.BlockSpec(memory_space=pltpu.SMEM if i in smem else pltpu.VMEM)
        for i in range(len(args))
    ]
    size = sum(int(np.prod(o.shape)) * o.dtype.itemsize for o in outs)
    size += sum(int(np.prod(a.shape)) * a.dtype.itemsize for a in args)
    return pl.pallas_call(
        body,
        out_shape=outs,
        in_specs=specs,
        out_specs=[pl.BlockSpec(memory_space=pltpu.VMEM) for _ in outs],
        scratch_shapes=list(scratch),
        compiler_params=pltpu.CompilerParams(vmem_limit_bytes=48 * 2**20),
        cost_estimate=pl.CostEstimate(flops=flops, bytes_accessed=size, transcendentals=0),
        name=name,
    )(*args)


def shape(dims_, dtype):
    return jax.ShapeDtypeStruct(dims_, dtype)


def pack_kernel(meta, wq, wk, wv, wr, na, nf, qg, kg, out):
    ctx = meta[4, 0]
    total = meta[4, 2]
    head = ctx // 2

    def rows_of(ref, pair, half):
        block = ref[:, pl.ds(pl.multiple_of(pair * 128, 128), 128)]
        pick = (iota((HD, 128), 1) == iota((HD, 128), 0) + half * HD).astype(BF)
        return dot(pick, block, 1, 1).astype(BF)

    out[0:64, :] = rows_of(wq, ctx // 2, ctx % 2)
    out[64:128, :] = rows_of(wk, head // 2, head % 2)
    out[128:192, :] = rows_of(wv, head // 2, head % 2)
    lane = iota((1, 128), 1)
    counts = jnp.where(lane == 0, total // 64, jnp.where(lane == 1, total % 64, 0))
    key_gain = jnp.concatenate([kg[...].astype(F32), jnp.zeros((1, 64), F32)], 1)
    out[192:208, :] = jnp.concatenate(
        [
            na[...].astype(F32),
            nf[...].astype(F32),
            qg[...].astype(F32),
            key_gain,
            counts.astype(F32),
            jnp.zeros((11, 128), F32),
        ],
        0,
    ).astype(BF)
    row = iota((32, 32), 0)
    expert = jnp.where(row < 16, 2 * row, 2 * row - 31)
    order = (iota((32, 32), 1) == expert).astype(BF)
    out[208:240, :] = dot(order, wr[...], 1, 1).astype(BF)


def slots_kernel(routes_t, out):
    row = iota((32, 128), 0)
    expert = jnp.where(row < 16, 2 * row, 2 * row - 31)
    named = jnp.zeros((32, 128), jnp.bool_)
    for k in range(8):
        named = named | (routes_t[k : k + 1, :] == expert)
    before = (iota((128, 128), 0) < iota((128, 128), 1)).astype(BF)
    rank = dot(named.astype(F32).astype(BF), before)
    rank = jnp.where(named, rank, -1.0)
    place = iota((1, CAP, 1), 1).astype(F32)
    out[...] = (
        (rank[:, None, :] == place).astype(F32).reshape(32 * CAP, 128).astype(BF)
    )


def project_kernel(meta, packed, *refs):
    pieces, (normed, qkv, squares) = refs[:16], refs[16:]
    ctx = meta[4, 0]
    weight = packed[0:192, :]
    gain = packed[192:208, :].astype(F32)[0:1, :]
    for (dx, dy, dc), piece in zip(PIECES, pieces):
        slot = ((ctx // 4 + dx + 4) % 4) * 4 + (((ctx // 2) % 2 + dy) % 2) * 2 + (ctx + dc) % 2
        at = pl.ds(pl.multiple_of(meta[0, slot] * TILE, TILE), TILE)
        rows = piece[...].astype(F32)
        factor = lax.rsqrt(jnp.mean(rows * rows, -1, keepdims=True) + EPS)
        low = (rows * factor * gain).astype(BF)
        normed[at, :] = low
        lin = dot(weight, low, 1, 1)
        qkv[:, at] = lin
        squares[0:1, at] = jnp.sum(lin[0:64] * lin[0:64], 0, keepdims=True)
        squares[1:2, at] = 0.5 * jnp.sum(lin[64:128] * lin[64:128], 0, keepdims=True)


def rotate(value, cos, sin):
    a, b = value[0:32], value[32:64]
    return jnp.concatenate([a * cos - b * sin, b * cos + a * sin], 0)


def diagonal_mask(meta, tile):
    room = meta[3, tile] - (tile - meta[2, tile]) * TILE
    key = iota((TILE, TILE), 0)
    return (key <= iota((TILE, TILE), 1)) & (key < room)


def strip_scores(meta, keys, query, tile):
    scores = dot(keys, query)
    last = jnp.where(diagonal_mask(meta, tile), scores[-TILE:], -1000000000.0)
    if scores.shape[0] == TILE:
        return last
    return jnp.concatenate([scores[:-TILE], last], 0)


def attend_kernel(
    meta, qkv, squares, q_gain, k_gain, cos_t, sin_t,
    out_low, out_full, stats, q_t, k_t, v_t, k_rows, v_rows,
):
    qg, kg = q_gain[...], k_gain[...]
    for tile in range(16):
        at = slice(tile * TILE, (tile + 1) * TILE)
        base = pl.ds(pl.multiple_of((tile - meta[2, tile]) * TILE, TILE), TILE)
        cos, sin = cos_t[:, base], sin_t[:, base]
        q_factor = lax.rsqrt(squares[0:1, at] * (1.0 / 1024) + EPS)
        k_factor = lax.rsqrt(squares[1:2, at] * (1.0 / 512) + EPS)
        query = rotate(qkv[0:64, at] * q_factor * qg, cos, sin)
        key = rotate(qkv[64:128, at] * k_factor * kg, cos, sin)
        value = qkv[128:192, at]
        q_t[:, at] = (query * 0.125).astype(BF)
        k_t[:, at] = key.astype(BF)
        v_t[:, at] = value.astype(BF)
        k_rows[at, :] = key.T.astype(BF)
        v_rows[at, :] = value.T.astype(BF)

    def one_tile(tile, unused):
        mine = pl.ds(pl.multiple_of(tile * TILE, TILE), TILE)
        count = tile - meta[2, tile] + 1
        slot = meta[1, tile]

        def strip(tiles):
            keys = pl.ds(pl.multiple_of((tile + 1 - tiles) * TILE, TILE), tiles * TILE)
            scores = strip_scores(meta, k_rows[keys, :], q_t[:, mine], tile)
            top = jnp.max(scores, 0, keepdims=True)
            weights = jnp.exp(scores - top)
            total = jnp.sum(weights, 0, keepdims=True)
            mixed = dot(v_t[:, keys], weights.astype(BF)) / total
            out_full[:, mine] = mixed
            out_low[pl.ds(slot, 1), :, :] = mixed.astype(BF)[None]
            stats[0:1, mine] = top
            stats[1:2, mine] = total

        for tiles in range(1, 9):
            pl.when(count == tiles)(functools.partial(strip, tiles))
        return unused

    lax.fori_loop(0, 16, one_tile, 0)


def attend_back_kernel(
    meta, moved, qkv, squares, q_gain, k_gain, cos_t, sin_t,
    out_full, stats, q_t, k_t, k_rows, v_rows,
    gq_weighted, keep, send, dots, gains, gk, gv, gain_q, gain_k,
):
    qg, kg = q_gain[...], k_gain[...]
    gk[...] = jnp.zeros_like(gk)
    gv[...] = jnp.zeros_like(gv)
    gain_q[...] = jnp.zeros_like(gain_q)
    gain_k[...] = jnp.zeros_like(gain_k)

    def turned_back(tile, value):
        base = pl.ds(pl.multiple_of((tile - meta[2, tile]) * TILE, TILE), TILE)
        return rotate(value, cos_t[:, base], -sin_t[:, base])

    def one_tile(tile, unused):
        mine = pl.ds(pl.multiple_of(tile * TILE, TILE), TILE)
        count = tile - meta[2, tile] + 1
        slot = meta[1, tile]

        def strip(tiles):
            keys = pl.ds(pl.multiple_of((tile + 1 - tiles) * TILE, TILE), tiles * TILE)
            g_out = moved[pl.ds(slot, 1), 0:64, :][0].astype(F32)
            inverse = 1.0 / stats[1:2, mine]
            g_acc = (g_out * inverse).astype(BF)
            shift = jnp.sum(g_out * out_full[:, mine], 0, keepdims=True) * inverse
            query = q_t[:, mine]
            scores = strip_scores(meta, k_rows[keys, :], query, tile)
            weights = jnp.exp(scores - stats[0:1, mine])
            g_weights = dot(v_rows[keys, :], g_acc)
            g_scores = (weights * (g_weights - shift)).astype(BF)
            gk[:, keys] += dot(query, g_scores, 1, 1)
            gv[:, keys] += dot(g_acc, weights.astype(BF), 1, 1)
            g_query = turned_back(tile, dot(k_t[:, keys], g_scores) * 0.125)
            factor = lax.rsqrt(squares[0:1, mine] * (1.0 / 1024) + EPS)
            q_norm = qkv[0:64, mine] * factor
            weighted = g_query * qg
            gq_weighted[:, mine] = weighted
            dots[0:1, mine] = jnp.sum(weighted * q_norm, 0, keepdims=True)
            gain_q[...] += g_query * q_norm

        for tiles in range(1, 9):
            pl.when(count == tiles)(functools.partial(strip, tiles))
        return unused

    lax.fori_loop(0, 16, one_tile, 0)

    odd = meta[4, 0] % 2 == 1
    for tile in range(16):
        at = slice(tile * TILE, (tile + 1) * TILE)
        g_key = turned_back(tile, gk[:, at])
        k_norm = qkv[64:128, at] * lax.rsqrt(squares[1:2, at] * (1.0 / 512) + EPS)
        dots[1:2, at] = jnp.sum(g_key * kg * k_norm, 0, keepdims=True)
        gain_k[...] += g_key * k_norm
        g_value = gv[:, at]
        keep[:, at] = jnp.where(odd, g_value, g_key)
        send[:, at] = jnp.where(odd, g_key, g_value)
    ones = jnp.ones((8, TILE), F32)
    gains[...] = jnp.concatenate(
        [
            dot(ones, gain_q[...], 1, 1, lax.Precision.HIGHEST),
            dot(ones, gain_k[...], 1, 1, lax.Precision.HIGHEST),
        ],
        1,
    )


def out_grad_kernel(moved, out_all, result):
    total = jnp.zeros((64, 1024), F32)
    for slot in range(16):
        total += dot(moved[slot, 64:128, :], out_all[slot], 1, 1)
    result[...] = total


def linear_grad_kernel(
    meta, qkv, squares, dots, gq_weighted, keep, other, k_gain, normed,
    out_grad, router_grad, ffn_gain_grad, gains, loss_parts, to_tokens, to_shards,
):
    odd = meta[4, 0] % 2 == 1
    kg = k_gain[...]
    lows = []
    for tile in range(16):
        at = slice(tile * TILE, (tile + 1) * TILE)
        q_factor = lax.rsqrt(squares[0:1, at] * (1.0 / 1024) + EPS)
        k_factor = lax.rsqrt(squares[1:2, at] * (1.0 / 512) + EPS)
        q_norm = qkv[0:64, at] * q_factor
        k_norm = qkv[64:128, at] * k_factor
        g_q = q_factor * (gq_weighted[:, at] - q_norm * (dots[0:1, at] * (1.0 / 1024)))
        both = keep[:, at] + other[:, at]
        g_k = k_factor * (both * kg - k_norm * (dots[1:2, at] * (1.0 / 512)))
        low = jnp.concatenate([g_q, jnp.where(odd, both, g_k)], 0).astype(BF)
        to_tokens[pl.ds(meta[1, tile], 1), :, :] = low[None]
        lows.append(low)
    total = dot(jnp.concatenate(lows, 1), normed[...])
    lane = iota((1, 128), 1)
    tail_rows = jnp.zeros((ROWS_OUT - ROW_LOSS - 1, 128), F32)
    loss = loss_parts[0:1, :]
    for block in range(8):
        at = slice(block * 128, (block + 1) * 128)
        to_shards[block] = jnp.concatenate(
            [
                total[:, at],
                out_grad[:, at],
                router_grad[:, at],
                ffn_gain_grad[0:1, at],
                gains[0:1, :],
                loss,
                tail_rows,
            ],
            0,
        ).astype(BF)


def input_grad_kernel(moved, weight, hidden, packed, g_resid, result):
    q_rows = jnp.concatenate([moved[h, 0:64, :] for h in range(16)], 0)
    k_rows = jnp.concatenate([moved[h, 64:128, :] for h in range(0, 16, 2)], 0)
    v_rows = jnp.concatenate([moved[h, 64:128, :] for h in range(1, 16, 2)], 0)
    g_lin = jnp.concatenate([q_rows, k_rows, v_rows], 0)
    g_normed = dot(g_lin, weight[...], 0, 1)
    rows = hidden[...].astype(F32)
    factor = lax.rsqrt(jnp.mean(rows * rows, -1, keepdims=True) + EPS)
    n = rows * factor
    gain = packed[192:208, :].astype(F32)[0:1, :]
    weighted = g_normed * gain
    result[...] = g_resid[...] + factor * (
        weighted - n * jnp.mean(weighted * n, -1, keepdims=True)
    )


def route_kernel(mixed, w_out, hidden, packed, place, outgoing, resid_out, post_out, probs):
    resid = hidden[...].astype(F32) + dot(mixed[...], w_out[...], 0, 0)
    gain = packed[192:208, :].astype(F32)[1:2, :]
    factor = lax.rsqrt(jnp.mean(resid * resid, -1, keepdims=True) + EPS)
    post = (resid * factor * gain).astype(BF)
    resid_out[...] = resid
    post_out[...] = post
    logits = dot(packed[208:240, :], post, 1, 1)
    shifted = jnp.exp(logits - jnp.max(logits, 0, keepdims=True))
    probs[...] = shifted / jnp.sum(shifted, 0, keepdims=True)
    outgoing[:, 0:1024] = dot(place[0:SLOTS, :], post).astype(BF)
    outgoing[:, 1024:2048] = dot(place[SLOTS : 2 * SLOTS, :], post).astype(BF)


def expert_weights(ref):
    gate = ref[:, 0:128, :].reshape(1024, 512)
    up = ref[:, 128:256, :].reshape(1024, 512)
    down_a = ref[:, 256:320, :].reshape(512, 512)
    down_b = ref[:, 320:384, :].reshape(512, 512)
    return gate, up, down_a, down_b


def expert_kernel(rows, weights, gate_pre, up_pre, act, result):
    gate, up, down_a, down_b = expert_weights(weights)
    x = rows[...]
    gp = dot(x, gate)
    up_value = dot(x, up)
    gate_pre[0] = gp
    up_pre[0] = up_value
    low = (gp * jax.nn.sigmoid(gp) * up_value).astype(BF)
    act[0] = low
    result[:, 0:512] = dot(low, down_a).astype(BF)
    result[:, 512:1024] = dot(low, down_b).astype(BF)


def expert_back_kernel(g_rows, weights, gate_pre, up_pre, g_gate, g_up, result):
    gate, up, down_a, down_b = expert_weights(weights)
    g = g_rows[...]
    g_act = dot(g[:, 0:512], down_a, 1, 1) + dot(g[:, 512:1024], down_b, 1, 1)
    gp, up_value = gate_pre[0], up_pre[0]
    sg = jax.nn.sigmoid(gp)
    gg = (g_act * up_value * sg * (1.0 + gp * (1.0 - sg))).astype(BF)
    gu = (g_act * (gp * sg)).astype(BF)
    g_gate[0] = gg
    g_up[0] = gu
    result[...] = (dot(gg, gate, 1, 1) + dot(gu, up, 1, 1)).astype(BF)


def expert_weight_kernel(rows, g_rows, act, g_gate, g_up, result):
    x, g = rows[...], g_rows[...]
    result[:, 0:128, :] = dot(x, g_gate[0], 0, 0).astype(BF).reshape(8, 128, 512)
    result[:, 128:256, :] = dot(x, g_up[0], 0, 0).astype(BF).reshape(8, 128, 512)
    low = act[0]
    result[:, 256:320, :] = dot(low, g[:, 0:512], 0, 0).astype(BF).reshape(8, 64, 512)
    result[:, 320:384, :] = dot(low, g[:, 512:1024], 0, 0).astype(BF).reshape(8, 64, 512)


HALF = pl.BlockSpec((SLOTS, 1024), lambda e: (0, e))
INNER = pl.BlockSpec((1, SLOTS, 512), lambda e: (e, 0, 0))
WEIGHTS = pl.BlockSpec((8, 384, 512), lambda e: (0, e, 0))


def expert_call(body, outs, out_specs, args, in_specs, name, flops):
    size = sum(int(np.prod(o.shape)) * o.dtype.itemsize for o in outs)
    size += sum(int(np.prod(a.shape)) * a.dtype.itemsize for a in args)
    return pl.pallas_call(
        body,
        grid=(2,),
        out_shape=outs,
        in_specs=in_specs,
        out_specs=out_specs,
        compiler_params=pltpu.CompilerParams(vmem_limit_bytes=56 * 2**20),
        cost_estimate=pl.CostEstimate(flops=flops, bytes_accessed=size, transcendentals=0),
        name=name,
    )(*args)


def combine_kernel(
    meta, scale, moved, place, probs, resid, teacher, post,
    result, g_result, g_rows, g_logits, router_grad, loss_parts,
):
    slot = meta[4, 0]
    tile = meta[0, slot]
    room = meta[3, tile] - (tile - meta[2, tile]) * TILE
    valid = (iota((TILE, 1), 0) < room).astype(F32)
    p = probs[...]
    chosen = place[...].astype(F32).reshape(32, CAP, 128) * p[:, None, :]
    chosen = chosen.reshape(2 * SLOTS, 128)
    high, low = split(chosen)
    total = resid[...]
    for e in (0, 1):
        at, lanes = slice(e * SLOTS, (e + 1) * SLOTS), slice(e * 1024, (e + 1) * 1024)
        total += dot(high[at], moved[:, lanes], 0, 0) + dot(low[at], moved[:, lanes], 0, 0)
    result[...] = total.astype(BF)
    errors = (total - teacher[...].astype(F32)) * valid
    squared = jnp.sum(jnp.sum(errors * errors, 0, keepdims=True), 1, keepdims=True)
    first = squared.astype(BF).astype(F32)
    second = (squared - first).astype(BF).astype(F32)
    third = squared - first - second
    lane = iota((8, 128), 1)
    loss_parts[...] = jnp.where(
        lane == 0, first, jnp.where(lane == 1, second, jnp.where(lane == 2, third, 0.0))
    )
    g = errors * scale[0, 0]
    g_result[...] = g
    g_high, g_low = split(g)
    g_probs = []
    for e in (0, 1):
        at, lanes = slice(e * SLOTS, (e + 1) * SLOTS), slice(e * 1024, (e + 1) * 1024)
        spread = dot(place[at, :], g_high) + dot(place[at, :], g_low)
        gate = jnp.sum(chosen[at], 1, keepdims=True)
        g_rows[:, lanes] = (spread * gate).astype(BF)
        g_gate = jnp.sum(spread * moved[:, lanes].astype(F32), 1, keepdims=True)
        picked = place[at, :].astype(F32) * g_gate
        g_probs.append(jnp.sum(picked.reshape(16, CAP, 128), 1))
    g_p = jnp.concatenate(g_probs, 0)
    g_z = (p * (g_p - jnp.sum(p * g_p, 0, keepdims=True))).astype(BF)
    g_logits[...] = g_z
    router_grad[...] = dot(g_z, post[...])


def resid_grad_kernel(
    moved, place, g_logits, packed, resid_in, g_result, w_out,
    g_resid_out, ffn_gain_grad, to_heads,
):
    g_post = dot(g_logits[...], packed[208:240, :], 0, 0)
    for e in (0, 1):
        at, lanes = slice(e * SLOTS, (e + 1) * SLOTS), slice(e * 1024, (e + 1) * 1024)
        g_post += dot(place[at, :], moved[:, lanes], 0, 0)
    resid = resid_in[...]
    gain = packed[192:208, :].astype(F32)[1:2, :]
    factor = lax.rsqrt(jnp.mean(resid * resid, -1, keepdims=True) + EPS)
    n = resid * factor
    ffn_gain_grad[...] = jnp.broadcast_to(jnp.sum(g_post * n, 0, keepdims=True), (8, 1024))
    weighted = g_post * gain
    g_resid = g_result[...] + factor * (
        weighted - n * jnp.mean(weighted * n, -1, keepdims=True)
    )
    g_resid_out[...] = g_resid
    low = g_resid.astype(BF)
    g_mixed = dot(w_out[...], low, 1, 1).astype(BF)
    turned = g_resid.T.astype(BF)
    for head in range(16):
        at = slice(head * 64, (head + 1) * 64)
        to_heads[head, 0:64, :] = g_mixed[at]
        to_heads[head, 64:128, :] = turned[at]


def shard_sum_kernel(blocks, result):
    total = jnp.sum(blocks[...].astype(F32), 0)
    parts = jnp.sum(total[ROW_LOSS : ROW_LOSS + 1, :], 1, keepdims=True)
    first = parts.astype(BF).astype(F32)
    second = (parts - first).astype(BF).astype(F32)
    third = parts - first - second
    lane = iota(total.shape, 1)
    pieces = jnp.where(lane == 0, first, jnp.where(lane == 1, second, third))
    use = (iota(total.shape, 0) == ROW_LOSS) & (lane < 3)
    result[...] = jnp.where(use, pieces, total).astype(BF)


def final_kernel(
    meta, divisor, near, up, down, far, wq, wk, wv, na,
    grad_q, grad_k, grad_v, grad_o, router, small, attn_gain, loss, gain_rows,
):
    x = meta[4, 0] // 4
    shard = meta[4, 1]
    summed = jnp.zeros((ROWS_OUT - ROW_GR, 128), F32)
    for ref, dx in ((near, 0), (up, 3), (down, 1), (far, 2)):
        index = (x + dx) % 4
        blocks = ref[...].astype(F32)
        wide = pl.ds(pl.multiple_of(index * 256, 256), 256)
        slim = pl.ds(pl.multiple_of(index * 128, 128), 128)
        grad_q[:, wide] = blocks[:, 0:64, :].reshape(256, 128).T
        grad_o[:, wide] = blocks[:, 128:192, :].reshape(256, 128).T
        grad_k[:, slim] = jnp.concatenate([blocks[0, 64:128], blocks[2, 64:128]], 0).T
        grad_v[:, slim] = jnp.concatenate([blocks[1, 64:128], blocks[3, 64:128]], 0).T
        tails = blocks[:, ROW_GR:, :]
        summed += tails[0] + tails[1] + tails[2] + tails[3]
        for j in range(4):
            gain_rows[pl.ds(index * 4 + j, 1), :] = tails[j, 33:34, :]
    row = iota((32, 32), 0)
    expert = jnp.where(row < 16, 2 * row, 2 * row - 31)
    order = (iota((32, 32), 1) == expert).astype(F32)
    router[...] = dot(summed[0:32], order, 0, 0, lax.Precision.HIGHEST)
    even = gain_rows[pl.ds(2 * shard, 1), :]
    odd = gain_rows[pl.ds(2 * shard + 1, 1), :]
    q_gain = jnp.concatenate([even[:, 0:64], odd[:, 0:64]], 1)
    k_gain = jnp.concatenate([(even + odd)[:, 64:128], jnp.zeros((1, 64), F32)], 1)
    small[...] = jnp.concatenate(
        [q_gain, k_gain, summed[32:33], jnp.zeros((5, 128), F32)], 0
    )
    folded = (
        jnp.sum(grad_q[...] * wq[...].astype(F32), 1, keepdims=True)
        + jnp.sum(grad_k[...] * wk[...].astype(F32), 1, keepdims=True)
        + jnp.sum(grad_v[...] * wv[...].astype(F32), 1, keepdims=True)
    )
    attn_gain[...] = folded / na[...].astype(F32)
    loss[...] = jnp.sum(summed[34:35, :], 1, keepdims=True) * divisor[0, 0]


def gather_rows(rows):
    across = ctx_move(rows, YHI)
    up, down = ctx_move(rows, XUP), ctx_move(rows, XDOWN)
    across_up, across_down = ctx_move(across, XUP), ctx_move(across, XDOWN)
    far, across_far = ctx_move(up, XUP), ctx_move(across_down, XDOWN)
    mine = [rows, across, up, down, across_up, across_down, far, across_far]
    return mine + [ctx_move(piece, CORE) for piece in mine]


def sum_ctx(value):
    value = value + ctx_move(value, CORE)
    value = value + ctx_move(value, YHI)
    up, down, far = ctx_move(value, XUP), ctx_move(value, XDOWN), ctx_move(value, XTWO)
    return value + up + down + far


def exchange(value, axis):
    return lax.all_to_all(value, axis, split_axis=0, concat_axis=0, tiled=True)


def on_device(
    hidden,
    teacher,
    lengths,
    tile_perm,
    routes,
    norm_attn,
    w_query,
    w_key,
    w_value,
    w_out,
    q_gain,
    k_gain,
    norm_ffn,
    w_router,
    w_gate,
    w_up,
    w_down,
):
    ctx = lax.axis_index("ctx")
    shard = lax.axis_index("fsdp")
    x_in = hidden[0]
    pieces = gather_rows(x_in)

    lens = lengths[0]
    perm = tile_perm[0]
    tiles = jnp.arange(16, dtype=jnp.int32)
    tile_counts = (lens + TILE - 1) // TILE
    before = jnp.tril(jnp.ones((5, 5), jnp.int32), -1)
    starts = jnp.sum(before * tile_counts[None, :], 1)
    inside = (tiles[:, None] >= starts[None, :]) & (
        tiles[:, None] < (starts + tile_counts)[None, :]
    )
    meta = jnp.stack(
        [
            perm,
            jnp.sum(jnp.where(perm[None, :] == tiles[:, None], tiles[None, :], 0), 1),
            jnp.sum(jnp.where(inside, starts[None, :], 0), 1),
            jnp.sum(jnp.where(inside, lens[None, :], 0), 1),
            jnp.where(tiles == 0, ctx, jnp.where(tiles == 1, shard, jnp.sum(lens))),
        ]
    )

    (block,) = kernel_call(
        pack_kernel,
        [shape((ROWS_IN, 128), BF)],
        [
            meta,
            w_query,
            w_key,
            w_value,
            w_router,
            norm_attn.reshape(1, 128),
            norm_ffn.reshape(1, 128),
            q_gain.reshape(1, 128),
            k_gain.reshape(1, 64),
        ],
        smem=(0,),
        name="pack",
    )
    other = fsdp_move(block, YLO)
    first = shard < 4
    pair = jnp.stack([jnp.where(first, block, other), jnp.where(first, other, block)])
    z = shard % 4
    table = jnp.zeros((2, 4, ROWS_IN, 128), BF)
    for value, dz in (
        (pair, 0),
        (fsdp_move(pair, ZUP), 3),
        (fsdp_move(pair, ZDOWN), 1),
        (fsdp_move(pair, ZTWO), 2),
    ):
        table = lax.dynamic_update_slice(table, value[:, None], (0, (z + dz) % 4, 0, 0))
    packed = jnp.transpose(table.reshape(8, ROWS_IN, 128), (1, 0, 2)).reshape(ROWS_IN, 1024)
    qg = lax.dynamic_slice(packed[ROW_GAIN + 2], (ctx * HD,), (HD,)).astype(F32).reshape(HD, 1)
    kg = (
        lax.dynamic_slice(packed[ROW_GAIN + 3], ((ctx // 2) * 128,), (HD,))
        .astype(F32)
        .reshape(HD, 1)
    )
    halves = packed[ROW_GAIN + 4].reshape(8, 128).astype(F32)
    elements = (jnp.sum(halves[:, 0]) * 64.0 + jnp.sum(halves[:, 1])) * 1024.0
    scale = (2.0 * 8388608.0 / elements).reshape(1, 1)
    divisor = (1.0 / elements).reshape(1, 1)

    frequencies = 10000.0 ** (-jnp.arange(32, dtype=F32) / 32)
    angles = frequencies[:, None] * jnp.arange(1024, dtype=F32)[None, :]
    cos_t, sin_t = jnp.cos(angles), jnp.sin(angles)
    (place,) = kernel_call(
        slots_kernel, [shape((2 * SLOTS, 128), BF)], [routes[0].T], name="slots"
    )

    out_full_weight = lax.all_gather(w_out, "fsdp", axis=0, tiled=True)
    expert_block = jnp.concatenate(
        [
            part
            for e in (0, 1)
            for part in (w_gate[e], w_up[e], w_down[e][:, :512], w_down[e][:, 512:])
        ],
        0,
    )
    experts = lax.all_gather(expert_block, "fsdp", axis=0)
    qkv_weight = lax.all_gather(
        jnp.concatenate([w_query, w_key, w_value], 1), "fsdp", axis=0, tiled=True
    )

    normed, qkv, squares = kernel_call(
        project_kernel,
        [shape((2048, 1024), BF), shape((192, 2048), F32), shape((2, 2048), F32)],
        [meta, packed] + pieces,
        smem=(0,),
        name="project",
        flops=2 * 2048 * 1024 * 192,
    )
    squares = sum_ctx(squares)
    heads_out, mixed_full, stats, q_t, k_t, v_t, k_rows, v_rows = kernel_call(
        attend_kernel,
        [
            shape((16, 64, 128), BF),
            shape((64, 2048), F32),
            shape((2, 2048), F32),
            shape((64, 2048), BF),
            shape((64, 2048), BF),
            shape((64, 2048), BF),
            shape((2048, 64), BF),
            shape((2048, 64), BF),
        ],
        [meta, qkv, squares, qg, kg, cos_t, sin_t],
        smem=(0,),
        name="attend",
        flops=54 * 4 * 128 * 128 * 64,
    )
    mixed = exchange(heads_out.reshape(1024, 128), "ctx")
    mixed_all = lax.all_gather(mixed, "ctx", axis=0)
    outgoing, resid, post, probs = kernel_call(
        route_kernel,
        [
            shape((SLOTS, 2048), BF),
            shape((128, 1024), F32),
            shape((128, 1024), BF),
            shape((32, 128), F32),
        ],
        [mixed, out_full_weight, x_in, packed, place],
        name="route",
        flops=2 * 128 * 1024 * 2400,
    )
    rows = exchange(outgoing, "ctx")
    gate_pre, up_pre, act, expert_out = expert_call(
        expert_kernel,
        [
            shape((2, SLOTS, 512), F32),
            shape((2, SLOTS, 512), F32),
            shape((2, SLOTS, 512), BF),
            shape((SLOTS, 2048), BF),
        ],
        [INNER, INNER, INNER, HALF],
        [rows, experts],
        [HALF, WEIGHTS],
        "experts",
        2 * 2 * SLOTS * 1024 * 1536,
    )
    returned = exchange(expert_out, "ctx")
    result, g_result, g_slots, g_logits, router_grad, loss_parts = kernel_call(
        combine_kernel,
        [
            shape((128, 1024), BF),
            shape((128, 1024), F32),
            shape((SLOTS, 2048), BF),
            shape((32, 128), BF),
            shape((32, 1024), F32),
            shape((8, 128), F32),
        ],
        [meta, scale, returned, place, probs, resid, teacher[0], post],
        smem=(0, 1),
        name="combine",
        flops=2 * SLOTS * 128 * 1024 * 8,
    )
    g_expert_out = exchange(g_slots, "ctx")
    g_gate, g_up, g_rows = expert_call(
        expert_back_kernel,
        [shape((2, SLOTS, 512), BF), shape((2, SLOTS, 512), BF), shape((SLOTS, 2048), BF)],
        [INNER, INNER, HALF],
        [g_expert_out, experts, gate_pre, up_pre],
        [HALF, WEIGHTS, INNER, INNER],
        "experts_back",
        2 * 2 * SLOTS * 1024 * 1536,
    )
    g_returned = exchange(g_rows, "ctx")
    (expert_grads,) = expert_call(
        expert_weight_kernel,
        [shape((8, 768, 512), BF)],
        [WEIGHTS],
        [rows, g_expert_out, act, g_gate, g_up],
        [HALF, HALF, INNER, INNER, INNER],
        "experts_weights",
        2 * 2 * SLOTS * 1024 * 1536,
    )
    expert_shard = lax.psum_scatter(
        expert_grads.reshape(8 * 768, 512), "fsdp", scatter_dimension=0, tiled=True
    )

    g_resid, ffn_gain_grad, to_heads = kernel_call(
        resid_grad_kernel,
        [shape((128, 1024), F32), shape((8, 1024), F32), shape((16, 128, 128), BF)],
        [g_returned, place, g_logits, packed, resid, g_result, out_full_weight],
        name="resid_grad",
        flops=2 * 128 * 1024 * 2400,
    )
    moved = exchange(to_heads.reshape(2048, 128), "ctx").reshape(16, 128, 128)
    gq_weighted, keep, send, dots, gains = kernel_call(
        attend_back_kernel,
        [
            shape((64, 2048), F32),
            shape((64, 2048), F32),
            shape((64, 2048), F32),
            shape((2, 2048), F32),
            shape((8, 128), F32),
        ],
        [
            meta, moved, qkv, squares, qg, kg, cos_t, sin_t,
            mixed_full, stats, q_t, k_t, k_rows, v_rows,
        ],
        smem=(0,),
        scratch=[
            pltpu.VMEM((64, 2048), F32),
            pltpu.VMEM((64, 2048), F32),
            pltpu.VMEM((64, 128), F32),
            pltpu.VMEM((64, 128), F32),
        ],
        name="attend_back",
        flops=54 * 10 * 128 * 128 * 64,
    )
    (out_grad,) = kernel_call(
        out_grad_kernel,
        [shape((64, 1024), F32)],
        [moved, mixed_all],
        name="out_grad",
        flops=2 * 2048 * 64 * 1024,
    )
    dots = sum_ctx(dots)
    received = ctx_move(send, CORE)
    to_tokens, to_shards = kernel_call(
        linear_grad_kernel,
        [shape((16, 128, 128), BF), shape((8, ROWS_OUT, 128), BF)],
        [
            meta, qkv, squares, dots, gq_weighted, keep, received, kg, normed,
            out_grad, router_grad, ffn_gain_grad, gains, loss_parts,
        ],
        smem=(0,),
        name="linear_grad",
        flops=2 * 2048 * 128 * 1024,
    )
    shards = exchange(to_shards.reshape(8 * ROWS_OUT, 128), "fsdp").reshape(8, ROWS_OUT, 128)
    (summed,) = kernel_call(
        shard_sum_kernel, [shape((ROWS_OUT, 128), BF)], [shards], name="shard_sum"
    )
    even = ctx % 2 == 0
    sibling = ctx_move(summed, CORE)
    chip = jnp.stack([jnp.where(even, summed, sibling), jnp.where(even, sibling, summed)])
    across = ctx_move(chip, YHI)
    low_y = (ctx // 2) % 2 == 0
    four = jnp.concatenate([jnp.where(low_y, chip, across), jnp.where(low_y, across, chip)])
    four_up, four_down, four_far = (
        ctx_move(four, XUP),
        ctx_move(four, XDOWN),
        ctx_move(four, XTWO),
    )
    g_lin = exchange(to_tokens.reshape(2048, 128), "ctx").reshape(16, 128, 128)
    (input_grad,) = kernel_call(
        input_grad_kernel,
        [shape((128, 1024), F32)],
        [g_lin, qkv_weight, x_in, packed, g_resid],
        name="input_grad",
        flops=2 * 128 * 2048 * 1024,
    )
    grad_q, grad_k, grad_v, grad_o, router, small, attn_gain, loss = kernel_call(
        final_kernel,
        [
            shape((128, 1024), F32),
            shape((128, 512), F32),
            shape((128, 512), F32),
            shape((128, 1024), F32),
            shape((128, 32), F32),
            shape((8, 128), F32),
            shape((128, 1), F32),
            shape((1, 1), F32),
        ],
        [
            meta, divisor, four, four_up, four_down, four_far,
            w_query, w_key, w_value, norm_attn.reshape(128, 1),
        ],
        smem=(0, 1),
        scratch=[pltpu.VMEM((16, 128), F32)],
        name="final",
    )
    by_expert = expert_shard.reshape(2, 384, 512).astype(F32)
    grad_gate = by_expert[:, 0:128]
    grad_up = by_expert[:, 128:256]
    grad_down = jnp.concatenate([by_expert[:, 256:320], by_expert[:, 320:384]], 2)
    return (
        result[None],
        loss.reshape(()),
        input_grad[None],
        attn_gain.reshape(128),
        grad_q,
        grad_k,
        grad_v,
        grad_o,
        small[0],
        small[1, :64],
        small[2],
        router,
        grad_gate,
        grad_up,
        grad_down,
    )


def solution(mesh):
    return jax.shard_map(
        on_device,
        mesh=mesh,
        in_specs=(
            P("fsdp", "ctx", None),
            P("fsdp", "ctx", None),
            P("fsdp", None),
            P("fsdp", None),
            P("fsdp", "ctx", None),
            P("fsdp"),
            P("fsdp", None),
            P("fsdp", None),
            P("fsdp", None),
            P("fsdp", None),
            P("fsdp"),
            P("fsdp"),
            P("fsdp"),
            P("fsdp", None),
            P("ctx", "fsdp", None),
            P("ctx", "fsdp", None),
            P("ctx", "fsdp", None),
        ),
        out_specs=(
            P("fsdp", "ctx", None),
            P(),
            P("fsdp", "ctx", None),
            P("fsdp"),
            P("fsdp", None),
            P("fsdp", None),
            P("fsdp", None),
            P("fsdp", None),
            P("fsdp"),
            P("fsdp"),
            P("fsdp"),
            P("fsdp", None),
            P("ctx", "fsdp", None),
            P("ctx", "fsdp", None),
            P("ctx", "fsdp", None),
        ),
        check_vma=False,
    )
```

```python
import functools

import jax
import jax.numpy as jnp
import numpy as np
from jax import lax
from jax.experimental import pallas as pl
from jax.experimental.pallas import tpu as pltpu
from jax.sharding import PartitionSpec as P

TILE = 128
HD = 64
CAP = 40
SLOTS = 16 * CAP
EPS = 1e-05
F32 = jnp.float32
BF = jnp.bfloat16

ROW_GAIN = 192
ROW_ROUTER = 208
ROWS_IN = 240
ROW_OUT = 128
ROW_GR = 192
ROW_NF = 224
ROW_LOSS = 226
ROWS_OUT = 240

CORE = [(i, i ^ 1) for i in range(16)]
YHI = [(i, i ^ 2) for i in range(16)]
XUP = [(i, (i + 4) % 16) for i in range(16)]
XDOWN = [(i, (i - 4) % 16) for i in range(16)]
XTWO = [(i, (i + 8) % 16) for i in range(16)]
YLO = [(i, i ^ 4) for i in range(8)]
ZUP = [(i, (i // 4) * 4 + (i + 1) % 4) for i in range(8)]
ZDOWN = [(i, (i // 4) * 4 + (i - 1) % 4) for i in range(8)]
ZTWO = [(i, (i // 4) * 4 + (i + 2) % 4) for i in range(8)]
PIECES = [
    (dx, dy, dc)
    for dc in (0, 1)
    for dx, dy in ((0, 0), (0, 1), (-1, 0), (1, 0), (-1, 1), (1, 1), (2, 0), (2, 1))
]


def ctx_move(value, pairs):
    return lax.ppermute(value, "ctx", pairs)


def fsdp_move(value, pairs):
    return lax.ppermute(value, "fsdp", pairs)


def dims(left, right):
    return (((left,), (right,)), ((), ()))


def dot(a, b, left=1, right=0, precision=None):
    return lax.dot_general(
        a, b, dims(left, right), preferred_element_type=F32, precision=precision
    )


def split(value):
    high = value.astype(BF)
    return high, (value - high.astype(F32)).astype(BF)


def iota(shape, axis):
    return lax.broadcasted_iota(jnp.int32, shape, axis)


def kernel_call(
    body, outs, args, smem=(), smem_out=(), anywhere=(), scratch=(), name=None, flops=0, brief=False
):
    specs = [
        pl.BlockSpec(
            memory_space=pltpu.SMEM if i in smem else pl.ANY if i in anywhere else pltpu.VMEM
        )
        for i in range(len(args))
    ]
    size = sum(int(np.prod(o.shape)) * o.dtype.itemsize for o in outs)
    size += sum(int(np.prod(a.shape)) * a.dtype.itemsize for a in args)
    if brief:
        size = 0
    return pl.pallas_call(
        body,
        out_shape=outs,
        in_specs=specs,
        out_specs=[
            pl.BlockSpec(memory_space=pltpu.SMEM if i in smem_out else pltpu.VMEM)
            for i in range(len(outs))
        ],
        scratch_shapes=list(scratch),
        compiler_params=pltpu.CompilerParams(
            vmem_limit_bytes=58 * 2**20
        ),
        cost_estimate=pl.CostEstimate(flops=flops, bytes_accessed=size, transcendentals=0),
        name=name,
    )(*args)


def streamed_call(
    body, outs, args, smem=(), stream=(), stream_out=(), scratch=(), name=None, flops=0, limit=58
):
    count, results = len(args), len(outs)
    moved, pushed = list(stream), list(stream_out)
    auto = [i for i in range(count) if i not in smem and i not in moved]
    auto_out = [j for j in range(results) if j not in pushed]
    puts = 40

    def kernel(*refs):
        ins, targets = refs[:count], refs[count : count + results]
        rest = refs[count + results :]
        held = dict(zip(moved, rest[: len(moved)]))
        staged = list(targets)
        for j, ref in zip(pushed, rest[len(moved) : len(moved) + len(pushed)]):
            staged[j] = ref
        own = rest[len(moved) + len(pushed) : -2]
        in_sems, out_sems = rest[-2:]
        copies = {}
        for n, i in enumerate(moved):
            copies[i] = pltpu.make_async_copy(ins[i], held[i], in_sems.at[n])
            copies[i].start()
        arrived, sent, started = set(), [], set()

        def get(i):
            if i not in copies:
                return ins[i]
            if i not in arrived:
                copies[i].wait()
                arrived.add(i)
            return held[i]

        def put(j, index=None):
            source = staged[j] if index is None else staged[j].at[index]
            target = targets[j] if index is None else targets[j].at[index]
            copy = pltpu.make_async_copy(source, target, out_sems.at[len(sent)])
            copy.start()
            sent.append(copy)
            started.add(j)

        body(get, put, staged, *own)
        for i in moved:
            get(i)
        for j in pushed:
            if j not in started:
                put(j)
        for copy in sent:
            copy.wait()

    specs = [
        pl.BlockSpec(
            memory_space=pltpu.SMEM if i in smem else pltpu.VMEM if i in auto else pltpu.HBM
        )
        for i in range(count)
    ]
    size = sum(int(np.prod(o.shape)) * o.dtype.itemsize for o in outs)
    size += sum(int(np.prod(a.shape)) * a.dtype.itemsize for a in args)
    buffers = [pltpu.VMEM(args[i].shape, args[i].dtype) for i in moved]
    buffers += [pltpu.VMEM(outs[j].shape, outs[j].dtype) for j in pushed]
    return pl.pallas_call(
        kernel,
        out_shape=outs,
        in_specs=specs,
        out_specs=[
            pl.BlockSpec(memory_space=pltpu.VMEM if j in auto_out else pltpu.HBM)
            for j in range(results)
        ],
        scratch_shapes=buffers
        + list(scratch)
        + [pltpu.SemaphoreType.DMA((max(1, len(moved)),)), pltpu.SemaphoreType.DMA((puts,))],
        compiler_params=pltpu.CompilerParams(vmem_limit_bytes=limit * 2**20),
        cost_estimate=pl.CostEstimate(flops=flops, bytes_accessed=size, transcendentals=0),
        name=name,
    )(*args)


def shape(dims_, dtype):
    return jax.ShapeDtypeStruct(dims_, dtype)


def pack_kernel(
    lens, perm, wq, wk, wv, wr, na, nf, qg, kg, wo, w_gate, w_up, w_down, out, big, meta
):
    ctx = lax.axis_index("ctx")
    for tile in range(16):
        meta[0, tile] = perm[0, tile]
        meta[1, perm[0, tile]] = tile
    start = jnp.int32(0)
    total = jnp.int32(0)
    begins = []
    for seq in range(5):
        length = lens[0, seq]
        begins.append((start, length))
        start = start + (length + TILE - 1) // TILE
        total = total + length
    for tile in range(16):
        first, length = begins[0]
        for begin, own in begins[1:]:
            later = tile >= begin
            first = jnp.where(later, begin, first)
            length = jnp.where(later, own, length)
        meta[2, tile] = first
        meta[3, tile] = length
        meta[4, tile] = ctx if tile == 0 else lax.axis_index("fsdp")
    head = ctx // 2

    def rows_of(ref, pair, half):
        block = ref[:, pl.ds(pl.multiple_of(pair * 128, 128), 128)]
        pick = (iota((HD, 128), 1) == iota((HD, 128), 0) + half * HD).astype(BF)
        return dot(pick, block, 1, 1).astype(BF)

    out[0:64, :] = rows_of(wq, ctx // 2, ctx % 2)
    out[64:128, :] = rows_of(wk, head // 2, head % 2)
    out[128:192, :] = rows_of(wv, head // 2, head % 2)
    lane = iota((1, 128), 1)
    counts = jnp.where(lane == 0, total // 64, jnp.where(lane == 1, total % 64, 0))
    key_gain = jnp.concatenate([kg[...].astype(F32), jnp.zeros((1, 64), F32)], 1)
    out[192:208, :] = jnp.concatenate(
        [
            na[...].astype(F32),
            nf[...].astype(F32),
            qg[...].astype(F32),
            key_gain,
            counts.astype(F32),
            jnp.zeros((11, 128), F32),
        ],
        0,
    ).astype(BF)
    row = iota((32, 32), 0)
    expert = jnp.where(row < 16, 2 * row, 2 * row - 31)
    order = (iota((32, 32), 1) == expert).astype(BF)
    out[208:240, :] = dot(order, wr[...]).astype(BF)
    for e in (0, 1):
        at = e * 384
        big[at : at + 128, :] = w_gate[e]
        big[at + 128 : at + 256, :] = w_up[e]
        big[at + 256 : at + 320, :] = w_down[e, :, 0:512]
        big[at + 320 : at + 384, :] = w_down[e, :, 512:1024]
    for part in range(4):
        lanes = pl.ds(pl.multiple_of((ctx % 2) * 512 + part * 128, 128), 128)
        out[ROWS_IN + part * 128 : ROWS_IN + (part + 1) * 128, :] = wo[:, lanes]


def assemble_kernel(meta, near, up, down, far, packed, w_half, qg, kg, consts):
    ctx, z = meta[4, 0], meta[4, 1] % 4
    for ref, dz in ((near, 0), (up, 3), (down, 1), (far, 2)):
        for y in (0, 1):
            at = pl.ds(pl.multiple_of((y * 4 + (z + dz) % 4) * 128, 128), 128)
            packed[:, at] = ref[y, 0:ROWS_IN]
            for part in range(4):
                first = ROWS_IN + part * 128
                w_half[at, part * 128 : (part + 1) * 128] = ref[y, first : first + 128]
    lanes = pl.ds(pl.multiple_of((ctx // 2) * 128, 128), 128)
    gains = packed[192:208, lanes].astype(F32)
    at, place = iota((HD, 128), 1), iota((HD, 128), 0)
    own = at == place + (ctx % 2) * HD
    qg[...] = jnp.sum(jnp.where(own, gains[2:3, :], 0.0), 1, keepdims=True)
    kg[...] = jnp.sum(jnp.where(at == place, gains[3:4, :], 0.0), 1, keepdims=True)
    counts = packed[192:208, :].astype(F32)[4:5, :]
    lane = iota((1, 1024), 1) % 128
    count = jnp.sum(jnp.where(lane == 0, counts * 64.0, counts), 1, keepdims=True)
    elements = count * 1024.0
    row = iota((8, 128), 0)
    consts[...] = jnp.where(row == 0, 2.0 * 8388608.0 / elements, 1.0 / elements)


def place_rows(named):
    before = (iota((128, 128), 0) < iota((128, 128), 1)).astype(BF)
    rank = jnp.where(named > 0.0, dot(named.astype(BF), before), -1.0)
    place = iota((1, CAP, 1), 1).astype(F32)
    return (rank[:, None, :] == place).astype(F32).reshape(32 * CAP, 128)


def slot_of(ctx, piece):
    dx, dy, dc = piece
    return ((ctx // 4 + dx + 4) % 4) * 4 + (((ctx // 2) % 2 + dy) % 2) * 2 + (ctx + dc) % 2


def slots_kernel(routes_t, out):
    row = iota((32, 128), 0)
    expert = jnp.where(row < 16, 2 * row, 2 * row - 31).astype(F32)
    routes = routes_t[...].astype(F32)
    named = jnp.zeros((32, 128), F32)
    for k in range(8):
        named = jnp.where(routes[k : k + 1, :] == expert, 1.0, named)
    out[...] = place_rows(named).astype(BF)


def project_kernel(get, put, outs):
    qkv, squares, normed = outs
    meta, packed = get(0), get(1)
    ctx = lax.axis_index("ctx")
    weight = packed[0:192, :]
    gain = packed[192:208, :].astype(F32)[0:1, :]
    for n, where in enumerate(PIECES):
        slot = slot_of(ctx, where)
        at = pl.ds(pl.multiple_of(meta[0, slot] * TILE, TILE), TILE)
        rows = get(2 + n)[...].astype(F32)
        factor = lax.rsqrt(jnp.mean(rows * rows, -1, keepdims=True) + EPS)
        low = (rows * factor * gain).astype(BF)
        normed[at, :] = low
        lin = dot(weight, low, 1, 1)
        qkv[:, at] = lin
        squares[0:1, at] = jnp.sum(lin[0:64] * lin[0:64], 0, keepdims=True)
        squares[1:2, at] = 0.5 * jnp.sum(lin[64:128] * lin[64:128], 0, keepdims=True)


def rotate(value, cos, sin):
    a, b = value[0:32], value[32:64]
    return jnp.concatenate([a * cos - b * sin, b * cos + a * sin], 0)


def diagonal_mask(meta, tile):
    room = meta[3, tile] - (tile - meta[2, tile]) * TILE
    key = iota((TILE, TILE), 0)
    return (key <= iota((TILE, TILE), 1)) & (key < room)


def strip_scores(meta, keys, query, tile, first):
    scores = dot(keys, query)
    parts = []
    for other in range(first, tile):
        shift = jnp.where(other >= meta[2, tile], 0.0, -1000000000.0)
        parts.append(scores[(other - first) * TILE : (other - first + 1) * TILE] + shift)
    parts.append(jnp.where(diagonal_mask(meta, tile), scores[-TILE:], -1000000000.0))
    return jnp.concatenate(parts, 0) if len(parts) > 1 else parts[0]


def attend_kernel(get, put, outs, v_t):
    out_low, out_full, stats, q_t, k_t, k_rows, v_rows = outs
    meta, qg, kg = get(0), get(3)[...], get(4)[...]
    routes_t, squares, cos_t, sin_t, qkv = get(7), get(2), get(5), get(6), get(1)
    for tile in range(16):
        at = slice(tile * TILE, (tile + 1) * TILE)
        base = pl.ds(pl.multiple_of((tile - meta[2, tile]) * TILE, TILE), TILE)
        cos, sin = cos_t[:, base], sin_t[:, base]
        q_factor = lax.rsqrt(squares[0:1, at] * (1.0 / 1024) + EPS)
        k_factor = lax.rsqrt(squares[1:2, at] * (1.0 / 512) + EPS)
        query = rotate(qkv[0:64, at] * q_factor * qg, cos, sin)
        key = rotate(qkv[64:128, at] * k_factor * kg, cos, sin)
        value = qkv[128:192, at]
        q_t[:, at] = (query * 0.125).astype(BF)
        k_t[:, at] = key.astype(BF)
        v_t[:, at] = value.astype(BF)
        k_rows[at, :] = key.T.astype(BF)
        v_rows[at, :] = value.T.astype(BF)

    out_low[1024:1040, :] = jnp.concatenate(
        [routes_t[...].astype(F32), jnp.zeros((8, 128), F32)], 0
    ).astype(BF)

    for tile in range(16):
        first = max(0, tile - 7)
        mine = slice(tile * TILE, (tile + 1) * TILE)
        keys = slice(first * TILE, (tile + 1) * TILE)
        scores = strip_scores(meta, k_rows[keys, :], q_t[:, mine], tile, first)
        top = jnp.max(scores, 0, keepdims=True)
        weights = jnp.exp(scores - top)
        total = jnp.sum(weights, 0, keepdims=True)
        mixed = dot(v_t[:, keys], weights.astype(BF)) / total
        out_full[:, mine] = mixed
        half = tile // 8
        rows = slice((tile % 8) * TILE, (tile % 8 + 1) * TILE)
        out_low[rows, half * HD : (half + 1) * HD] = mixed.T.astype(BF)
        stats[0:1, mine] = top
        stats[1:2, mine] = total


def attend_back_kernel(get, put, outs, gk, gv, gain_q, gain_k):
    to_tokens, gq_weighted, keep, send, dots, gains = outs
    meta, qg, kg = get(0), get(4)[...], get(5)[...]
    qkv, squares, cos_t, sin_t, out_full, stats = [get(i) for i in (2, 3, 6, 7, 8, 9)]
    q_t, k_t, k_rows, v_rows, moved = [get(i) for i in (10, 11, 12, 13, 1)]
    gk[...] = jnp.zeros_like(gk)
    gv[...] = jnp.zeros_like(gv)
    gain_q[...] = jnp.zeros_like(gain_q)
    gain_k[...] = jnp.zeros_like(gain_k)

    def turned_back(tile, value):
        base = pl.ds(pl.multiple_of((tile - meta[2, tile]) * TILE, TILE), TILE)
        return rotate(value, cos_t[:, base], -sin_t[:, base])

    for tile in range(16):
        first = max(0, tile - 7)
        mine = slice(tile * TILE, (tile + 1) * TILE)
        keys = slice(first * TILE, (tile + 1) * TILE)
        g_out = moved[pl.ds(meta[1, tile], 1), 0:64, :][0].astype(F32)
        inverse = 1.0 / stats[1:2, mine]
        g_acc = (g_out * inverse).astype(BF)
        shift = jnp.sum(g_out * out_full[:, mine], 0, keepdims=True) * inverse
        query = q_t[:, mine]
        scores = strip_scores(meta, k_rows[keys, :], query, tile, first)
        weights = jnp.exp(scores - stats[0:1, mine])
        g_weights = dot(v_rows[keys, :], g_acc)
        g_scores = (weights * (g_weights - shift)).astype(BF)
        gk[:, keys] += dot(query, g_scores, 1, 1)
        gv[:, keys] += dot(g_acc, weights.astype(BF), 1, 1)
        g_query = turned_back(tile, dot(k_t[:, keys], g_scores) * 0.125)
        factor = lax.rsqrt(squares[0:1, mine] * (1.0 / 1024) + EPS)
        q_norm = qkv[0:64, mine] * factor
        weighted = g_query * qg
        gq_weighted[:, mine] = weighted
        dots[0:1, mine] = jnp.sum(weighted * q_norm, 0, keepdims=True)
        gain_q[...] += g_query * q_norm

    odd = meta[4, 0] % 2 == 1
    for tile in range(16):
        at = slice(tile * TILE, (tile + 1) * TILE)
        g_key = turned_back(tile, gk[:, at])
        k_norm = qkv[64:128, at] * lax.rsqrt(squares[1:2, at] * (1.0 / 512) + EPS)
        weighted = g_key * kg
        dots[1:2, at] = jnp.sum(weighted * k_norm, 0, keepdims=True)
        gain_k[...] += g_key * k_norm
        g_value = gv[:, at]
        to_tokens[pl.ds(meta[1, tile], 1), :, :] = jnp.concatenate(
            [gq_weighted[:, at], weighted, g_value], 0
        ).astype(BF)[None]
        keep[:, at] = jnp.where(odd, g_value, g_key)
        send[:, at] = jnp.where(odd, g_key, g_value)
    ones = jnp.ones((8, TILE), F32)
    gains[...] = jnp.concatenate(
        [
            dot(ones, gain_q[...], 1, 1, lax.Precision.HIGHEST),
            dot(ones, gain_k[...], 1, 1, lax.Precision.HIGHEST),
        ],
        1,
    )


def out_grad_kernel(get, put, outs):
    (result,) = outs
    meta, moved, out_rows = get(0), get(1), get(2)
    turned = jnp.concatenate(
        [moved[pl.ds(meta[1, tile], 1), 64:128, :][0] for tile in range(16)], 1
    )
    result[...] = dot(turned, out_rows[...])


def linear_grad_kernel(get, put, outs, whole):
    z = lax.axis_index("fsdp") % 4
    odd = lax.axis_index("ctx") % 2 == 1
    kg = get(6)[...]
    qkv, squares, dots, gq_weighted, keep, other = [get(i) for i in range(6)]
    lows = []
    for tile in range(16):
        at = slice(tile * TILE, (tile + 1) * TILE)
        q_factor = lax.rsqrt(squares[0:1, at] * (1.0 / 1024) + EPS)
        k_factor = lax.rsqrt(squares[1:2, at] * (1.0 / 512) + EPS)
        q_norm = qkv[0:64, at] * q_factor
        k_norm = qkv[64:128, at] * k_factor
        g_q = q_factor * (gq_weighted[:, at] - q_norm * (dots[0:1, at] * (1.0 / 1024)))
        both = keep[:, at] + other[:, at]
        g_k = k_factor * (both * kg - k_norm * (dots[1:2, at] * (1.0 / 512)))
        lows.append(jnp.concatenate([g_q, jnp.where(odd, both, g_k)], 0).astype(BF))
    whole[0:128, :] = dot(jnp.concatenate(lows, 1), get(7)[...])
    out_grad, router_grad, ffn_gain_grad, gains, loss_parts = [get(i) for i in range(8, 13)]
    lane = iota((1, 128), 1)
    tail_rows = jnp.zeros((ROWS_OUT - ROW_LOSS - 1, 128), F32)
    loss = loss_parts[0:1, :]
    whole[128:192, :] = out_grad[...]
    whole[192:224, :] = router_grad[...]
    whole[224:232, :] = jnp.where(iota((8, 1024), 0) == 0, ffn_gain_grad[...], 0.0)
    tail = jnp.concatenate([gains[0:1, :], loss, tail_rows], 0)
    for out, dz in zip(outs, (0, 1, 3, 2)):
        for y in (0, 1):
            at = pl.ds(pl.multiple_of((y * 4 + (z + dz) % 4) * 128, 128), 128)
            out[y] = jnp.concatenate([whole[0:225, at], tail], 0).astype(BF)


def loss_again(total):
    parts = jnp.sum(total[ROW_LOSS : ROW_LOSS + 1, :], 1, keepdims=True)
    first = parts.astype(BF).astype(F32)
    second = (parts - first).astype(BF).astype(F32)
    third = parts - first - second
    lane = iota(total.shape, 1)
    pieces = jnp.where(lane == 0, first, jnp.where(lane == 1, second, third))
    use = (iota(total.shape, 0) == ROW_LOSS) & (lane < 3)
    return jnp.where(use, pieces, total)


def sum_z_kernel(get, put, outs):
    keep, send = outs
    low = lax.axis_index("fsdp") < 4
    parts = [get(i)[...].astype(F32) for i in range(4)]
    total = parts[0] + parts[1] + parts[2] + parts[3]
    keep[...] = jnp.where(low, total[0], total[1])
    send[...] = loss_again(jnp.where(low, total[1], total[0])).astype(BF)


def sum_y_kernel(get, put, outs):
    total = get(0)[...] + get(1)[...].astype(F32)
    outs[0][...] = loss_again(total).astype(BF)


def own_linear_kernel(get, put, outs):
    norms, factors = outs
    hidden, packed, mine, other = [get(i) for i in range(4)]
    even = lax.axis_index("ctx") % 2 == 0
    w_q = jnp.where(even, mine[...], other[...])
    w_k = jnp.where(even, other[:, 0:512], mine[:, 0:512])
    rows = hidden[...].astype(F32)
    factor = lax.rsqrt(jnp.mean(rows * rows, -1, keepdims=True) + EPS)
    gain = packed[192:208, :].astype(F32)[0:1, :]
    low = (rows * factor * gain).astype(BF)
    q_lin = dot(low, w_q).T
    k_lin = dot(low, w_k).T
    q_factor = lax.rsqrt(jnp.mean(q_lin * q_lin, 0, keepdims=True) + EPS)
    k_factor = lax.rsqrt(jnp.mean(k_lin * k_lin, 0, keepdims=True) + EPS)
    norms[0:1024, :] = q_lin * q_factor
    norms[1024:1536, :] = k_lin * k_factor
    factors[...] = jnp.where(iota((8, 128), 0) == 0, q_factor, k_factor)


def input_grad_kernel(get, put, outs):
    (result,) = outs
    norms, factors, moved = get(0), get(1), get(2)
    q = jnp.concatenate([moved[h, 0:64, :] for h in range(16)], 0).astype(F32)

    def key_rows(at):
        pairs = [
            moved[h, at : at + 64, :].astype(F32) + moved[h + 1, at : at + 64, :].astype(F32)
            for h in range(0, 16, 2)
        ]
        return jnp.concatenate(pairs, 0)

    k, v = key_rows(64), key_rows(128)
    q_norm, k_norm = norms[0:1024, :], norms[1024:1536, :]
    g_q = factors[0:1, :] * (q - q_norm * jnp.mean(q * q_norm, 0, keepdims=True))
    g_k = factors[1:2, :] * (k - k_norm * jnp.mean(k * k_norm, 0, keepdims=True))
    g_lin = jnp.concatenate([g_q, g_k, v], 0).astype(BF)
    even = lax.axis_index("ctx") % 2 == 0
    near, far = g_lin[0:1024], g_lin[1024:2048]
    g_normed = dot(jnp.where(even, near, far), get(3)[...], 0, 1)
    g_normed += dot(jnp.where(even, far, near), get(4)[...], 0, 1)
    hidden, packed, g_resid = get(5), get(6), get(7)
    rows = hidden[...].astype(F32)
    factor = lax.rsqrt(jnp.mean(rows * rows, -1, keepdims=True) + EPS)
    n = rows * factor
    gain = packed[192:208, :].astype(F32)[0:1, :]
    weighted = g_normed * gain
    result[...] = g_resid[...] + factor * (
        weighted - n * jnp.mean(weighted * n, -1, keepdims=True)
    )


def route_kernel(get, put, outs, spread, named, w_full):
    rows, act, result, out_rows, place, gates, resid_out, post_out, probs = outs[:9]
    gate_pre, up_pre = outs[9:]
    meta, packed = get(0), get(1)
    ctx = lax.axis_index("ctx")
    odd = ctx % 2 == 1
    for n in range(2, 18):
        get(n)
    first_x, first_out, first_w, experts = 18, 2, 34, 36
    for i in range(8):
        lanes = pl.ds(pl.multiple_of((slot_of(ctx, PIECES[i]) // 2) * 128, 128), 128)
        mine = get(first_out + i)[0:1024, :]
        other = get(first_out + i + 8)[0:1024, :]
        low, high = jnp.where(odd, other, mine), jnp.where(odd, mine, other)
        out_rows[0:1024, lanes] = jnp.concatenate([low[:, 0:64], high[:, 0:64]], 1)
        out_rows[1024:2048, lanes] = jnp.concatenate([low[:, 64:128], high[:, 64:128]], 1)
    for n, piece in enumerate(PIECES):
        slot = slot_of(ctx, piece)
        routes = get(first_out + n)[1024:1040, :].astype(F32)[0:8, :]
        for e in (0, 1):
            expert = (2 * ctx + e).astype(F32)
            hit = jnp.max(jnp.where(routes == expert, 1.0, 0.0), 0, keepdims=True)
            named[pl.ds(e * 16 + slot, 1), :] = hit
    place[...] = place_rows(named[...])
    xs = [get(first_x + n) for n in range(16)]
    for core in (0, 1):
        columns = pl.ds(pl.multiple_of(((ctx + core) % 2) * 512, 512), 512)
        w_full[:, columns] = get(first_w + core)[...]
    gain = packed[192:208, :].astype(F32)[1:2, :]
    router = packed[208:240, :]
    for group in range(4):
        slots = [slot_of(ctx, PIECES[group * 4 + j]) for j in range(4)]
        tiles = [pl.ds(pl.multiple_of(meta[0, slot] * TILE, TILE), TILE) for slot in slots]
        mixed = jnp.concatenate([out_rows[at, :] for at in tiles], 0)
        x = jnp.concatenate([xs[group * 4 + j][...] for j in range(4)], 0)
        resid = x.astype(F32) + dot(mixed, w_full[...])
        factor = lax.rsqrt(jnp.mean(resid * resid, -1, keepdims=True) + EPS)
        post = (resid * factor * gain).astype(BF)
        logits = dot(router, post, 1, 1)
        shifted = jnp.exp(logits - jnp.max(logits, 0, keepdims=True))
        p = shifted / jnp.sum(shifted, 0, keepdims=True)
        if group == 0:
            resid_out[...] = resid[0:TILE]
            post_out[...] = post[0:TILE]
            probs[...] = p[:, 0:TILE]
        gate = [
            jnp.sum(jnp.where(iota(p.shape, 0) == ctx + 16 * e, p, 0.0), 0, keepdims=True)
            for e in (0, 1)
        ]
        for j, slot in enumerate(slots):
            own = slice(j * TILE, (j + 1) * TILE)
            at = pl.ds(pl.multiple_of(slot * CAP, 8), CAP)
            picks = []
            for e in (0, 1):
                gates[pl.ds(e * 16 + slot, 1), :] = gate[e][:, own]
                picks.append(place[pl.ds(pl.multiple_of(e * SLOTS + slot * CAP, 8), CAP), :])
            both = dot(jnp.concatenate(picks, 0).astype(BF), post[own])
            spread[at, 0:1024] = both[0:CAP]
            spread[at, 1024:2048] = both[CAP : 2 * CAP]
    rows[...] = spread[...].astype(BF)
    for j in (3, 4, 5, 6, 7, 8, 0):
        put(j)
    weights = get(experts)
    for e in (0, 1):
        gate_w, up_w, down_a, down_b = expert_weights(weights, e)
        x = rows[:, e * 1024 : (e + 1) * 1024]
        gp, up = dot(x, gate_w), dot(x, up_w)
        gate_pre[e] = gp.astype(BF)
        up_pre[e] = up.astype(BF)
        low = (gp * jax.nn.sigmoid(gp) * up).astype(BF)
        act[e] = low
        first = e * 1024
        result[:, first : first + 512] = dot(low, down_a).astype(BF)
        result[:, first + 512 : first + 1024] = dot(low, down_b).astype(BF)
        put(2, (slice(None), slice(first, first + 1024)))
        put(9, (e,))
        put(10, (e,))
        put(1, (e,))


def expert_weights(ref, e):
    at = e * 384
    gate = ref[:, at : at + 128, :].reshape(1024, 512)
    up = ref[:, at + 128 : at + 256, :].reshape(1024, 512)
    down_a = ref[:, at + 256 : at + 320, :].reshape(512, 512)
    down_b = ref[:, at + 320 : at + 384, :].reshape(512, 512)
    return gate, up, down_a, down_b


def expert_back_kernel(get, put, outs, spread):
    result, g_rows, g_gate, g_up = outs
    ctx = lax.axis_index("ctx")
    place, gates = get(16), get(17)
    for n in range(16):
        get(n)
    for n, piece in enumerate(PIECES):
        slot = slot_of(ctx, piece)
        at = pl.ds(pl.multiple_of(slot * CAP, 8), CAP)
        picks, scales = [], []
        for e in (0, 1):
            pick = place[pl.ds(pl.multiple_of(e * SLOTS + slot * CAP, 8), CAP), :]
            gate = gates[pl.ds(e * 16 + slot, 1), :]
            scales.append(jnp.sum(pick * gate, 1, keepdims=True))
            picks.append(pick)
        both = dot(jnp.concatenate(picks, 0).astype(BF), get(n)[...])
        spread[at, 0:1024] = both[0:CAP] * scales[0]
        spread[at, 1024:2048] = both[CAP : 2 * CAP] * scales[1]
    g_rows[...] = spread[...].astype(BF)
    put(1)
    weights, gate_pre, up_pre = get(18), get(19), get(20)
    for e in (0, 1):
        gate, up, down_a, down_b = expert_weights(weights, e)
        first = e * 1024
        g_act = dot(g_rows[:, first : first + 512], down_a, 1, 1)
        g_act += dot(g_rows[:, first + 512 : first + 1024], down_b, 1, 1)
        gp, up_value = gate_pre[e].astype(F32), up_pre[e].astype(F32)
        sg = jax.nn.sigmoid(gp)
        gg = (g_act * up_value * sg * (1.0 + gp * (1.0 - sg))).astype(BF)
        gu = (g_act * (gp * sg)).astype(BF)
        g_gate[e] = gg
        g_up[e] = gu
        result[:, first : first + 1024] = (dot(gg, gate, 1, 1) + dot(gu, up, 1, 1)).astype(BF)
        put(0, (slice(None), slice(first, first + 1024)))


def expert_weight_kernel(rows, g_rows, act, g_gate, g_up, result):
    x, g = rows[...], g_rows[...]
    result[:, 0:128, :] = dot(x, g_gate[0], 0, 0).astype(BF).reshape(8, 128, 512)
    result[:, 128:256, :] = dot(x, g_up[0], 0, 0).astype(BF).reshape(8, 128, 512)
    low = act[0]
    result[:, 256:320, :] = dot(low, g[:, 0:512], 0, 0).astype(BF).reshape(8, 64, 512)
    result[:, 320:384, :] = dot(low, g[:, 512:1024], 0, 0).astype(BF).reshape(8, 64, 512)


HALF = pl.BlockSpec((SLOTS, 1024), lambda e: (0, e))
INNER = pl.BlockSpec((1, SLOTS, 512), lambda e: (e, 0, 0))
WEIGHTS = pl.BlockSpec((8, 384, 512), lambda e: (0, e, 0))


def expert_call(body, outs, out_specs, args, in_specs, name, flops, scratch=()):
    size = sum(int(np.prod(o.shape)) * o.dtype.itemsize for o in outs)
    size += sum(int(np.prod(a.shape)) * a.dtype.itemsize for a in args)
    return pl.pallas_call(
        body,
        grid=(2,),
        out_shape=outs,
        in_specs=in_specs,
        out_specs=out_specs,
        scratch_shapes=list(scratch),
        compiler_params=pltpu.CompilerParams(vmem_limit_bytes=58 * 2**20),
        cost_estimate=pl.CostEstimate(flops=flops, bytes_accessed=size, transcendentals=0),
        name=name,
    )(*args)


def chosen_rows(place, probs):
    chosen = place[...].astype(F32).reshape(32, CAP, 128) * probs[:, None, :]
    return chosen.reshape(2 * SLOTS, 128)


def halves():
    for e in (0, 1):
        yield slice(e * SLOTS, (e + 1) * SLOTS), slice(e * 1024, (e + 1) * 1024)


def combine_kernel(get, put, outs):
    result, g_result, g_low, loss_parts = outs
    meta, consts, moved, place, probs, resid, teacher = [get(i) for i in range(7)]
    slot = meta[4, 0]
    tile = meta[0, slot]
    room = meta[3, tile] - (tile - meta[2, tile]) * TILE
    valid = (iota((TILE, 1), 0) < room).astype(F32)
    high, low = split(chosen_rows(place, probs[...]))
    total = resid[...]
    for at, lanes in halves():
        total += dot(high[at], moved[:, lanes], 0, 0) + dot(low[at], moved[:, lanes], 0, 0)
    result[...] = total.astype(BF)
    errors = (total - teacher[...].astype(F32)) * valid
    g = errors * consts[0:1, 0:1]
    g_result[...] = g
    g_low[...] = g.astype(BF)
    squared = jnp.sum(jnp.sum(errors * errors, 0, keepdims=True), 1, keepdims=True)
    first = squared.astype(BF).astype(F32)
    second = (squared - first).astype(BF).astype(F32)
    third = squared - first - second
    lane = iota((8, 128), 1)
    loss_parts[...] = jnp.where(
        lane == 0, first, jnp.where(lane == 1, second, jnp.where(lane == 2, third, 0.0))
    )


def router_grad_kernel(moved, place, probs, g_result, post, g_logits, router_grad):
    p = probs[...]
    g_high, g_low = split(g_result[...])
    g_probs = []
    for at, lanes in halves():
        match = dot(moved[:, lanes], g_high, 1, 1) + dot(moved[:, lanes], g_low, 1, 1)
        picked = place[at, :].astype(F32) * match
        g_probs.append(jnp.sum(picked.reshape(16, CAP, 128), 1))
    g_p = jnp.concatenate(g_probs, 0)
    g_z = (p * (g_p - jnp.sum(p * g_p, 0, keepdims=True))).astype(BF)
    g_logits[...] = g_z
    router_grad[...] = dot(g_z, post[...])


def resid_grad_kernel(get, put, outs):
    g_resid_out, ffn_gain_grad, to_heads = outs
    moved, place, g_logits, packed, resid_in, g_result = [get(i) for i in range(6)]
    core = lax.axis_index("ctx") % 2
    g_post = dot(g_logits[...], packed[208:240, :], 0, 0)
    for e in (0, 1):
        at, lanes = slice(e * SLOTS, (e + 1) * SLOTS), slice(e * 1024, (e + 1) * 1024)
        g_post += dot(place[at, :], moved[:, lanes], 0, 0)
    resid = resid_in[...]
    gain = packed[192:208, :].astype(F32)[1:2, :]
    factor = lax.rsqrt(jnp.mean(resid * resid, -1, keepdims=True) + EPS)
    n = resid * factor
    ffn_gain_grad[...] = jnp.broadcast_to(jnp.sum(g_post * n, 0, keepdims=True), (8, 1024))
    weighted = g_post * gain
    g_resid = g_result[...] + factor * (
        weighted - n * jnp.mean(weighted * n, -1, keepdims=True)
    )
    g_resid_out[...] = g_resid
    low = g_resid.astype(BF)
    near, far = low[:, 0:512], low[:, 512:1024]
    mine, other = jnp.where(core == 0, near, far), jnp.where(core == 0, far, near)
    g_mixed = (dot(get(6)[...], mine, 1, 1) + dot(get(7)[...], other, 1, 1)).astype(BF)
    turned = g_resid.T.astype(BF)
    for head in range(16):
        at = slice(head * 64, (head + 1) * 64)
        to_heads[head, 0:64, :] = g_mixed[at]
        to_heads[head, 64:128, :] = turned[at]


def final_kernel(get, put, outs, gain_rows):
    (
        grad_q, grad_k, grad_v, grad_o, router, q_gain, k_gain, ffn_gain, attn_gain, loss,
    ) = outs
    meta, consts, near, up, down, far, na = [get(i) for i in range(7)]
    wq, wk, wv = get(7), get(8), get(9)
    x = meta[4, 0] // 4
    shard = meta[4, 1]
    summed = jnp.zeros((ROWS_OUT - ROW_GR, 128), F32)
    for ref, dx in ((near, 0), (up, 3), (down, 1), (far, 2)):
        index = (x + dx) % 4
        blocks = ref[...].astype(F32)
        wide = pl.ds(pl.multiple_of(index * 256, 256), 256)
        slim = pl.ds(pl.multiple_of(index * 128, 128), 128)
        grad_q[:, wide] = blocks[:, 0:64, :].reshape(256, 128).T
        grad_o[:, wide] = blocks[:, 128:192, :].reshape(256, 128).T
        grad_k[:, slim] = jnp.concatenate([blocks[0, 64:128], blocks[2, 64:128]], 0).T
        grad_v[:, slim] = jnp.concatenate([blocks[1, 64:128], blocks[3, 64:128]], 0).T
        tails = blocks[:, ROW_GR:, :]
        summed += tails[0] + tails[1] + tails[2] + tails[3]
        for j in range(4):
            gain_rows[pl.ds(index * 4 + j, 1), :] = tails[j, 33:34, :]
    row = iota((32, 32), 0)
    expert = jnp.where(row < 16, 2 * row, 2 * row - 31)
    order = (iota((32, 32), 1) == expert).astype(F32)
    router[...] = dot(order, summed[0:32], 0, 0, lax.Precision.HIGHEST)
    even = gain_rows[pl.ds(2 * shard, 1), :]
    odd = gain_rows[pl.ds(2 * shard + 1, 1), :]
    q_gain[...] = jnp.concatenate([even[:, 0:64], odd[:, 0:64]], 1)
    k_gain[...] = (even + odd)[:, 64:128]
    ffn_gain[...] = summed[32:33]
    folded = (
        jnp.sum(grad_q[...] * wq[...].astype(F32), 1, keepdims=True)
        + jnp.sum(grad_k[...] * wk[...].astype(F32), 1, keepdims=True)
        + jnp.sum(grad_v[...] * wv[...].astype(F32), 1, keepdims=True)
    )
    attn_gain[...] = jnp.broadcast_to(folded, (128, 128)).T[0:1, :] / na[...].astype(F32)
    loss[...] = jnp.sum(summed[34:35, :], 1, keepdims=True) * consts[1:2, 0:1]


def unpack_kernel(get, put, outs):
    grad_gate, grad_up, grad_down = outs
    shard = get(0)
    for e in (0, 1):
        at = e * 384
        grad_gate[e] = shard[at : at + 128, :].astype(F32)
        grad_up[e] = shard[at + 128 : at + 256, :].astype(F32)
        grad_down[e, :, 0:512] = shard[at + 256 : at + 320, :].astype(F32)
        grad_down[e, :, 512:1024] = shard[at + 320 : at + 384, :].astype(F32)


def gather_rows(rows):
    across = ctx_move(rows, YHI)
    up, down = ctx_move(rows, XUP), ctx_move(rows, XDOWN)
    across_up, across_down = ctx_move(up, YHI), ctx_move(across, XDOWN)
    far, across_far = ctx_move(up, XUP), ctx_move(across_down, XDOWN)
    mine = [rows, across, up, down, across_up, across_down, far, across_far]
    return mine + [ctx_move(piece, CORE) for piece in mine]


def sum_ctx(value):
    value = value + ctx_move(value, CORE)
    value = value + ctx_move(value, YHI)
    up, down, far = ctx_move(value, XUP), ctx_move(value, XDOWN), ctx_move(value, XTWO)
    return value + up + down + far


def exchange(value, axis):
    return lax.all_to_all(value, axis, split_axis=0, concat_axis=0, tiled=True)


def on_device(
    hidden,
    teacher,
    lengths,
    tile_perm,
    routes,
    norm_attn,
    w_query,
    w_key,
    w_value,
    w_out,
    q_gain,
    k_gain,
    norm_ffn,
    w_router,
    w_gate,
    w_up,
    w_down,
):
    ctx = lax.axis_index("ctx")
    shard = lax.axis_index("fsdp")
    x_in = hidden[0]
    block, expert_block, meta = kernel_call(
        pack_kernel,
        [
            shape((ROWS_IN + 512, 128), BF),
            shape((768, 512), BF),
            shape((5, 16), jnp.int32),
        ],
        [
            lengths, tile_perm, w_query, w_key, w_value, w_router.T,
            norm_attn.reshape(1, 128), norm_ffn.reshape(1, 128),
            q_gain.reshape(1, 128), k_gain.reshape(1, 64),
            w_out, w_gate, w_up, w_down,
        ],
        smem=(0, 1),
        smem_out=(2,),
        name="pack",
    )
    x_first, block = lax.optimization_barrier((x_in, block))
    pieces = gather_rows(x_first)
    other = fsdp_move(block, YLO)
    first = shard < 4
    pair = jnp.stack([jnp.where(first, block, other), jnp.where(first, other, block)])
    pair_moves = [fsdp_move(pair, pairs) for pairs in (ZUP, ZDOWN, ZTWO)]
    *pair_moves, pieces[7] = lax.optimization_barrier((*pair_moves, pieces[7]))
    packed, w_mine, qg, kg, consts = kernel_call(
        assemble_kernel,
        [
            shape((ROWS_IN, 1024), BF),
            shape((1024, 512), BF),
            shape((HD, 1), F32),
            shape((HD, 1), F32),
            shape((8, 128), F32),
        ],
        [meta, pair] + pair_moves,
        smem=(0,),
        name="assemble",
    )
    w_other = ctx_move(w_mine, CORE)
    frequencies = 10000.0 ** (-jnp.arange(32, dtype=F32) / 32)
    angles = frequencies[:, None] * jnp.arange(1024, dtype=F32)[None, :]
    cos_t, sin_t = jnp.cos(angles), jnp.sin(angles)
    routes_t = routes[0].T.astype(BF)
    (place,) = kernel_call(
        slots_kernel, [shape((2 * SLOTS, 128), BF)], [routes_t], name="slots"
    )

    expert_block, *_ = lax.optimization_barrier((expert_block, packed, *pieces[4:8]))
    experts = lax.all_gather(expert_block, "fsdp", axis=0)
    qkv, squares, normed = streamed_call(
        project_kernel,
        [shape((192, 2048), F32), shape((2, 2048), F32), shape((2048, 1024), BF)],
        [meta, packed] + pieces,
        smem=(0,),
        name="project",
        flops=2 * 2048 * 1024 * 192,
    )
    squares = sum_ctx(squares)
    mixed_low, mixed_full, stats, q_t, k_t, k_rows, v_rows = streamed_call(
        attend_kernel,
        [
            shape((1040, 128), BF),
            shape((64, 2048), F32),
            shape((2, 2048), F32),
            shape((64, 2048), BF),
            shape((64, 2048), BF),
            shape((2048, 64), BF),
            shape((2048, 64), BF),
        ],
        [meta, qkv, squares, qg, kg, cos_t, sin_t, routes_t],
        smem=(0,),
        scratch=[pltpu.VMEM((64, 2048), BF)],
        name="attend",
        flops=54 * 4 * 128 * 128 * 64,
    )
    mixed_pieces = gather_rows(mixed_low)
    (
        rows, act, expert_out, mixed_rows, place_here, gates, resid, post, probs, gate_pre, up_pre,
    ) = streamed_call(
        route_kernel,
        [
            shape((SLOTS, 2048), BF),
            shape((2, SLOTS, 512), BF),
            shape((SLOTS, 2048), BF),
            shape((2048, 1024), BF),
            shape((2 * SLOTS, 128), F32),
            shape((32, 128), F32),
            shape((128, 1024), F32),
            shape((128, 1024), BF),
            shape((32, 128), F32),
            shape((2, SLOTS, 512), BF),
            shape((2, SLOTS, 512), BF),
        ],
        [meta, packed] + mixed_pieces + pieces + [w_mine, w_other, experts],
        smem=(0,),
        stream=range(2, 37),
        stream_out=range(11),
        scratch=[
            pltpu.VMEM((SLOTS, 2048), F32),
            pltpu.VMEM((32, 128), F32),
            pltpu.VMEM((1024, 1024), BF),
        ],
        name="route_experts",
        flops=2 * 2048 * 1024 * 1024 + 2 * 2 * SLOTS * 1024 * 1536,
    )
    even = ctx % 2 == 0
    qkv_half = jnp.where(even, w_query, jnp.concatenate([w_key, w_value], 1))
    qkv_half, _ = lax.optimization_barrier((qkv_half, rows))
    qkv_mine = lax.all_gather(qkv_half, "fsdp", axis=0, tiled=True)
    qkv_other = ctx_move(qkv_mine, CORE)
    returned = exchange(expert_out, "ctx")
    result, g_result, g_low, loss_parts = streamed_call(
        combine_kernel,
        [
            shape((128, 1024), BF),
            shape((128, 1024), F32),
            shape((128, 1024), BF),
            shape((8, 128), F32),
        ],
        [meta, consts, returned, place, probs, resid, teacher[0]],
        smem=(0,),
        name="combine",
        limit=24,
        flops=2 * SLOTS * 128 * 1024 * 4,
    )
    g_pieces = gather_rows(g_low)
    g_logits, router_grad = kernel_call(
        router_grad_kernel,
        [shape((32, 128), BF), shape((32, 1024), F32)],
        [returned, place, probs, g_result, post],
        name="router_grad",
        brief=True,
    )
    g_rows, g_slots, g_gate, g_up = streamed_call(
        expert_back_kernel,
        [
            shape((SLOTS, 2048), BF),
            shape((SLOTS, 2048), BF),
            shape((2, SLOTS, 512), BF),
            shape((2, SLOTS, 512), BF),
        ],
        g_pieces + [place_here, gates, experts, gate_pre, up_pre],
        stream=range(21),
        stream_out=range(4),
        scratch=[pltpu.VMEM((SLOTS, 2048), F32)],
        name="experts_back",
        flops=2 * 2 * SLOTS * 1024 * 1536,
    )
    g_returned = exchange(g_rows, "ctx")
    (expert_grads,) = expert_call(
        expert_weight_kernel,
        [shape((8, 768, 512), BF)],
        [WEIGHTS],
        [rows, g_slots, act, g_gate, g_up],
        [HALF, HALF, INNER, INNER, INNER],
        "experts_weights",
        2 * 2 * SLOTS * 1024 * 1536,
    )
    expert_shard = lax.psum_scatter(
        expert_grads.reshape(8 * 768, 512), "fsdp", scatter_dimension=0, tiled=True
    )

    grad_gate, grad_up, grad_down = streamed_call(
        unpack_kernel,
        [shape((2, 128, 512), F32), shape((2, 128, 512), F32), shape((2, 64, 1024), F32)],
        [expert_shard],
        name="unpack",
    )
    g_resid, ffn_gain_grad, to_heads = streamed_call(
        resid_grad_kernel,
        [shape((128, 1024), F32), shape((8, 1024), F32), shape((16, 128, 128), BF)],
        [g_returned, place, g_logits, packed, resid, g_result, w_mine, w_other],
        stream=(6, 7),
        name="resid_grad",
        limit=24,
        flops=2 * 128 * 1024 * 2400,
    )
    norms, factors = streamed_call(
        own_linear_kernel,
        [shape((1536, 128), F32), shape((8, 128), F32)],
        [x_in, packed, qkv_mine, qkv_other],
        name="own_linear",
    )
    to_heads, norms, factors = lax.optimization_barrier((to_heads, norms, factors))
    moved = exchange(to_heads.reshape(2048, 128), "ctx").reshape(16, 128, 128)
    to_tokens, gq_weighted, keep, send, dots, gains = streamed_call(
        attend_back_kernel,
        [
            shape((16, 192, 128), BF),
            shape((64, 2048), F32),
            shape((64, 2048), F32),
            shape((64, 2048), F32),
            shape((2, 2048), F32),
            shape((8, 128), F32),
        ],
        [
            meta, moved, qkv, squares, qg, kg, cos_t, sin_t,
            mixed_full, stats, q_t, k_t, k_rows, v_rows,
        ],
        smem=(0,),
        scratch=[
            pltpu.VMEM((64, 2048), F32),
            pltpu.VMEM((64, 2048), F32),
            pltpu.VMEM((64, 128), F32),
            pltpu.VMEM((64, 128), F32),
        ],
        name="attend_back",
        flops=10**11,
    )
    dots = sum_ctx(dots)
    to_tokens, dots = lax.optimization_barrier((to_tokens, dots))
    g_lin = exchange(to_tokens.reshape(16 * 192, 128), "ctx").reshape(16, 192, 128)
    (out_grad,) = streamed_call(
        out_grad_kernel,
        [shape((64, 1024), F32)],
        [meta, moved, mixed_rows],
        smem=(0,),
        name="out_grad",
        flops=2 * 2048 * 64 * 1024,
    )
    received = ctx_move(send, CORE)
    scattered = streamed_call(
        linear_grad_kernel,
        [shape((2, ROWS_OUT, 128), BF)] * 4,
        [
            qkv, squares, dots, gq_weighted, keep, received, kg, normed,
            out_grad, router_grad, ffn_gain_grad, gains, loss_parts,
        ],
        stream=(7,),
        scratch=[pltpu.VMEM((232, 1024), F32)],
        name="linear_grad",
        flops=2 * 2048 * 128 * 1024,
    )
    keep_z, send_z = streamed_call(
        sum_z_kernel,
        [shape((ROWS_OUT, 128), F32), shape((ROWS_OUT, 128), BF)],
        [scattered[0]]
        + [fsdp_move(part, pairs) for part, pairs in zip(scattered[1:], (ZUP, ZDOWN, ZTWO))],
        name="sum_z",
        limit=8,
    )
    send_z, g_lin = lax.optimization_barrier((send_z, g_lin))
    (summed,) = streamed_call(
        sum_y_kernel,
        [shape((ROWS_OUT, 128), BF)],
        [keep_z, fsdp_move(send_z, YLO)],
        name="sum_y",
        limit=8,
    )
    sibling = ctx_move(summed, CORE)
    chip = jnp.stack([jnp.where(even, summed, sibling), jnp.where(even, sibling, summed)])
    across = ctx_move(chip, YHI)
    low_y = (ctx // 2) % 2 == 0
    four = jnp.concatenate([jnp.where(low_y, chip, across), jnp.where(low_y, across, chip)])
    four, grad_gate, grad_up, grad_down = lax.optimization_barrier(
        (four, grad_gate, grad_up, grad_down)
    )
    four_up, four_down, four_far = (
        ctx_move(four, XUP),
        ctx_move(four, XDOWN),
        ctx_move(four, XTWO),
    )
    (input_grad,) = streamed_call(
        input_grad_kernel,
        [shape((128, 1024), F32)],
        [norms, factors, g_lin, qkv_mine, qkv_other, x_in, packed, g_resid],
        stream=(3, 4),
        name="input_grad",
        flops=2 * 128 * 2048 * 1024,
    )
    (
        grad_q, grad_k, grad_v, grad_o, router, q_gain_grad, k_gain_grad, ffn_gain, attn_gain,
        loss,
    ) = streamed_call(
        final_kernel,
        [
            shape((128, 1024), F32),
            shape((128, 512), F32),
            shape((128, 512), F32),
            shape((128, 1024), F32),
            shape((32, 128), F32),
            shape((1, 128), F32),
            shape((1, 64), F32),
            shape((1, 128), F32),
            shape((1, 128), F32),
            shape((1, 1), F32),
        ],
        [
            meta, consts, four, four_up, four_down, four_far, norm_attn.reshape(1, 128),
            w_query, w_key, w_value,
        ],
        smem=(0,),
        scratch=[pltpu.VMEM((16, 128), F32)],
        name="final",
        limit=16,
    )
    return (
        result[None],
        loss.reshape(()),
        input_grad[None],
        attn_gain.reshape(128),
        grad_q,
        grad_k,
        grad_v,
        grad_o,
        q_gain_grad.reshape(128),
        k_gain_grad.reshape(64),
        ffn_gain.reshape(128),
        router.T,
        grad_gate,
        grad_up,
        grad_down,
    )


def solution(mesh):
    return jax.shard_map(
        on_device,
        mesh=mesh,
        in_specs=(
            P("fsdp", "ctx", None),
            P("fsdp", "ctx", None),
            P("fsdp", None),
            P("fsdp", None),
            P("fsdp", "ctx", None),
            P("fsdp"),
            P("fsdp", None),
            P("fsdp", None),
            P("fsdp", None),
            P("fsdp", None),
            P("fsdp"),
            P("fsdp"),
            P("fsdp"),
            P("fsdp", None),
            P("ctx", "fsdp", None),
            P("ctx", "fsdp", None),
            P("ctx", "fsdp", None),
        ),
        out_specs=(
            P("fsdp", "ctx", None),
            P(),
            P("fsdp", "ctx", None),
            P("fsdp"),
            P("fsdp", None),
            P("fsdp", None),
            P("fsdp", None),
            P("fsdp", None),
            P("fsdp"),
            P("fsdp"),
            P("fsdp"),
            P("fsdp", None),
            P("ctx", "fsdp", None),
            P("ctx", "fsdp", None),
            P("ctx", "fsdp", None),
        ),
        check_vma=False,
    )
```

```python
import functools

import jax
import jax.numpy as jnp
import numpy as np
from jax import lax
from jax.experimental import pallas as pl
from jax.experimental.pallas import tpu as pltpu
from jax.sharding import PartitionSpec as P

TILE = 128
HD = 64
FULL = 36
CAP = 40
SLOTS = 16 * CAP
SENT = 32 * FULL
EPS = 1e-05
F32 = jnp.float32
BF = jnp.bfloat16

ROW_GAIN = 192
ROW_ROUTER = 208
ROWS_IN = 240
ROW_OUT = 128
ROW_GR = 192
ROW_NF = 224
ROW_LOSS = 226
ROWS_OUT = 240

CORE = [(i, i ^ 1) for i in range(16)]
YHI = [(i, i ^ 2) for i in range(16)]
XUP = [(i, (i + 4) % 16) for i in range(16)]
XDOWN = [(i, (i - 4) % 16) for i in range(16)]
XTWO = [(i, (i + 8) % 16) for i in range(16)]
YLO = [(i, i ^ 4) for i in range(8)]
ZUP = [(i, (i // 4) * 4 + (i + 1) % 4) for i in range(8)]
ZDOWN = [(i, (i // 4) * 4 + (i - 1) % 4) for i in range(8)]
ZTWO = [(i, (i // 4) * 4 + (i + 2) % 4) for i in range(8)]
PIECES = [
    (dx, dy, dc)
    for dc in (0, 1)
    for dx, dy in ((0, 0), (0, 1), (-1, 0), (1, 0), (-1, 1), (1, 1), (2, 0), (2, 1))
]


def ctx_move(value, pairs):
    return lax.ppermute(value, "ctx", pairs)


def fsdp_move(value, pairs):
    return lax.ppermute(value, "fsdp", pairs)


def dims(left, right):
    return (((left,), (right,)), ((), ()))


def dot(a, b, left=1, right=0, precision=None):
    return lax.dot_general(
        a, b, dims(left, right), preferred_element_type=F32, precision=precision
    )


def split(value):
    high = value.astype(BF)
    return high, (value - high.astype(F32)).astype(BF)


def iota(shape, axis):
    return lax.broadcasted_iota(jnp.int32, shape, axis)


def kernel_call(
    body, outs, args, smem=(), smem_out=(), anywhere=(), scratch=(), name=None, flops=0, brief=False
):
    specs = [
        pl.BlockSpec(
            memory_space=pltpu.SMEM if i in smem else pl.ANY if i in anywhere else pltpu.VMEM
        )
        for i in range(len(args))
    ]
    size = sum(int(np.prod(o.shape)) * o.dtype.itemsize for o in outs)
    size += sum(int(np.prod(a.shape)) * a.dtype.itemsize for a in args)
    if brief:
        size = 0
    return pl.pallas_call(
        body,
        out_shape=outs,
        in_specs=specs,
        out_specs=[
            pl.BlockSpec(memory_space=pltpu.SMEM if i in smem_out else pltpu.VMEM)
            for i in range(len(outs))
        ],
        scratch_shapes=list(scratch),
        compiler_params=pltpu.CompilerParams(
            vmem_limit_bytes=58 * 2**20
        ),
        cost_estimate=pl.CostEstimate(flops=flops, bytes_accessed=size, transcendentals=0),
        name=name,
    )(*args)


def streamed_call(
    body, outs, args, smem=(), stream=(), stream_out=(), scratch=(), name=None, flops=0, limit=58
):
    count, results = len(args), len(outs)
    moved, pushed = list(stream), list(stream_out)
    auto = [i for i in range(count) if i not in smem and i not in moved]
    auto_out = [j for j in range(results) if j not in pushed]
    puts = 40

    def kernel(*refs):
        ins, targets = refs[:count], refs[count : count + results]
        rest = refs[count + results :]
        held = dict(zip(moved, rest[: len(moved)]))
        staged = list(targets)
        for j, ref in zip(pushed, rest[len(moved) : len(moved) + len(pushed)]):
            staged[j] = ref
        own = rest[len(moved) + len(pushed) : -2]
        in_sems, out_sems = rest[-2:]
        copies = {}
        for n, i in enumerate(moved):
            copies[i] = pltpu.make_async_copy(ins[i], held[i], in_sems.at[n])
            copies[i].start()
        arrived, sent, started = set(), [], set()

        def get(i):
            if i not in copies:
                return ins[i]
            if i not in arrived:
                copies[i].wait()
                arrived.add(i)
            return held[i]

        def put(j, index=None):
            source = staged[j] if index is None else staged[j].at[index]
            target = targets[j] if index is None else targets[j].at[index]
            copy = pltpu.make_async_copy(source, target, out_sems.at[len(sent)])
            copy.start()
            sent.append(copy)
            started.add(j)

        body(get, put, staged, *own)
        for i in moved:
            get(i)
        for j in pushed:
            if j not in started:
                put(j)
        for copy in sent:
            copy.wait()

    specs = [
        pl.BlockSpec(
            memory_space=pltpu.SMEM if i in smem else pltpu.VMEM if i in auto else pltpu.HBM
        )
        for i in range(count)
    ]
    size = sum(int(np.prod(o.shape)) * o.dtype.itemsize for o in outs)
    size += sum(int(np.prod(a.shape)) * a.dtype.itemsize for a in args)
    buffers = [pltpu.VMEM(args[i].shape, args[i].dtype) for i in moved]
    buffers += [pltpu.VMEM(outs[j].shape, outs[j].dtype) for j in pushed]
    return pl.pallas_call(
        kernel,
        out_shape=outs,
        in_specs=specs,
        out_specs=[
            pl.BlockSpec(memory_space=pltpu.VMEM if j in auto_out else pltpu.HBM)
            for j in range(results)
        ],
        scratch_shapes=buffers
        + list(scratch)
        + [pltpu.SemaphoreType.DMA((max(1, len(moved)),)), pltpu.SemaphoreType.DMA((puts,))],
        compiler_params=pltpu.CompilerParams(vmem_limit_bytes=limit * 2**20),
        cost_estimate=pl.CostEstimate(flops=flops, bytes_accessed=size, transcendentals=0),
        name=name,
    )(*args)


def shape(dims_, dtype):
    return jax.ShapeDtypeStruct(dims_, dtype)


def pack_kernel(
    lens, perm, wq, wk, wv, wr, na, nf, qg, kg, wo, w_gate, w_up, w_down, out, big, meta
):
    ctx = lax.axis_index("ctx")
    for tile in range(16):
        meta[0, tile] = perm[0, tile]
        meta[1, perm[0, tile]] = tile
    start = jnp.int32(0)
    total = jnp.int32(0)
    begins = []
    for seq in range(5):
        length = lens[0, seq]
        begins.append((start, length))
        start = start + (length + TILE - 1) // TILE
        total = total + length
    for tile in range(16):
        first, length = begins[0]
        for begin, own in begins[1:]:
            later = tile >= begin
            first = jnp.where(later, begin, first)
            length = jnp.where(later, own, length)
        meta[2, tile] = first
        meta[3, tile] = length
        meta[4, tile] = ctx if tile == 0 else lax.axis_index("fsdp")
    head = ctx // 2

    def rows_of(ref, pair, half):
        block = ref[:, pl.ds(pl.multiple_of(pair * 128, 128), 128)]
        pick = (iota((HD, 128), 1) == iota((HD, 128), 0) + half * HD).astype(BF)
        return dot(pick, block, 1, 1).astype(BF)

    out[0:64, :] = rows_of(wq, ctx // 2, ctx % 2)
    out[64:128, :] = rows_of(wk, head // 2, head % 2)
    out[128:192, :] = rows_of(wv, head // 2, head % 2)
    lane = iota((1, 128), 1)
    counts = jnp.where(lane == 0, total // 64, jnp.where(lane == 1, total % 64, 0))
    key_gain = jnp.concatenate([kg[...].astype(F32), jnp.zeros((1, 64), F32)], 1)
    out[192:208, :] = jnp.concatenate(
        [
            na[...].astype(F32),
            nf[...].astype(F32),
            qg[...].astype(F32),
            key_gain,
            counts.astype(F32),
            jnp.zeros((11, 128), F32),
        ],
        0,
    ).astype(BF)
    out[208:240, :] = wr[...]
    for e in (0, 1):
        at = e * 384
        big[at : at + 128, :] = w_gate[e]
        big[at + 128 : at + 256, :] = w_up[e]
        big[at + 256 : at + 320, :] = w_down[e, :, 0:512]
        big[at + 320 : at + 384, :] = w_down[e, :, 512:1024]
    for part in range(4):
        lanes = pl.ds(pl.multiple_of((ctx % 2) * 512 + part * 128, 128), 128)
        out[ROWS_IN + part * 128 : ROWS_IN + (part + 1) * 128, :] = wo[:, lanes]


def assemble_kernel(meta, near, up, down, far, packed, w_half, qg, kg, consts):
    ctx, z = meta[4, 0], meta[4, 1] % 4
    for ref, dz in ((near, 0), (up, 3), (down, 1), (far, 2)):
        for y in (0, 1):
            at = pl.ds(pl.multiple_of((y * 4 + (z + dz) % 4) * 128, 128), 128)
            packed[:, at] = ref[y, 0:ROWS_IN]
            for part in range(4):
                first = ROWS_IN + part * 128
                w_half[at, part * 128 : (part + 1) * 128] = ref[y, first : first + 128]
    lanes = pl.ds(pl.multiple_of((ctx // 2) * 128, 128), 128)
    gains = packed[192:208, lanes].astype(F32)
    at, place = iota((HD, 128), 1), iota((HD, 128), 0)
    own = at == place + (ctx % 2) * HD
    qg[...] = jnp.sum(jnp.where(own, gains[2:3, :], 0.0), 1, keepdims=True)
    kg[...] = jnp.sum(jnp.where(at == place, gains[3:4, :], 0.0), 1, keepdims=True)
    counts = packed[192:208, :].astype(F32)[4:5, :]
    lane = iota((1, 1024), 1) % 128
    count = jnp.sum(jnp.where(lane == 0, counts * 64.0, counts), 1, keepdims=True)
    elements = count * 1024.0
    row = iota((8, 128), 0)
    consts[...] = jnp.where(row == 0, 2.0 * 8388608.0 / elements, 1.0 / elements)


def place_rows(named):
    before = (iota((128, 128), 0) < iota((128, 128), 1)).astype(BF)
    rank = jnp.where(named > 0.0, dot(named.astype(BF), before), -1.0)
    place = iota((1, CAP, 1), 1).astype(F32)
    return (rank[:, None, :] == place).astype(F32).reshape(32 * CAP, 128)


def slot_of(ctx, piece):
    dx, dy, dc = piece
    return ((ctx // 4 + dx + 4) % 4) * 4 + (((ctx // 2) % 2 + dy) % 2) * 2 + (ctx + dc) % 2


def slot_experts():
    row, first = iota((SENT, 32), 0), iota((SENT, 32), 1) * FULL
    return (row >= first) & (row < first + FULL)


def slots_kernel(routes_t, probs, out, high_out, low_out):
    expert = iota((32, 128), 0).astype(F32)
    routes = routes_t[...].astype(F32)
    named = jnp.zeros((32, 128), F32)
    for k in range(8):
        named = jnp.where(routes[k : k + 1, :] == expert, 1.0, named)
    before = (iota((128, 128), 0) < iota((128, 128), 1)).astype(BF)
    rank = jnp.where(named > 0.0, dot(named.astype(BF), before), -1.0)
    of_expert = slot_experts()
    spread = of_expert.astype(F32).astype(BF)
    first = jnp.sum(jnp.where(of_expert, iota((SENT, 32), 1) * FULL, 0), 1, keepdims=True)
    place = (iota((SENT, 1), 0) - first).astype(F32)
    match = dot(spread, rank.astype(BF)) == place
    out[...] = match.astype(F32).astype(BF)
    p = probs[...]
    p_high = p.astype(BF)
    p_rest = p - p_high.astype(F32)
    p_low = p_rest.astype(BF)
    p_last = (p_rest - p_low.astype(F32)).astype(BF)
    gate = dot(spread, p_high) + dot(spread, p_low) + dot(spread, p_last)
    high, low = split(jnp.where(match, gate, 0.0))
    high_out[...] = high
    low_out[...] = low


def project_kernel(get, put, outs):
    qkv, squares, normed = outs
    meta, packed = get(0), get(1)
    ctx = lax.axis_index("ctx")
    weight = packed[0:192, :]
    gain = packed[192:208, :].astype(F32)[0:1, :]
    for n, where in enumerate(PIECES):
        slot = slot_of(ctx, where)
        at = pl.ds(pl.multiple_of(meta[0, slot] * TILE, TILE), TILE)
        rows = get(2 + n)[...].astype(F32)
        factor = lax.rsqrt(jnp.mean(rows * rows, -1, keepdims=True) + EPS)
        low = (rows * factor * gain).astype(BF)
        normed[at, :] = low
        lin = dot(weight, low, 1, 1)
        qkv[:, at] = lin
        squares[0:1, at] = jnp.sum(lin[0:64] * lin[0:64], 0, keepdims=True)
        squares[1:2, at] = 0.5 * jnp.sum(lin[64:128] * lin[64:128], 0, keepdims=True)


def rotate(value, cos, sin):
    a, b = value[0:32], value[32:64]
    return jnp.concatenate([a * cos - b * sin, b * cos + a * sin], 0)


def diagonal_mask(meta, tile):
    room = meta[3, tile] - (tile - meta[2, tile]) * TILE
    key = iota((TILE, TILE), 0)
    return (key <= iota((TILE, TILE), 1)) & (key < room)


def strip_scores(meta, keys, query, tile, first):
    scores = dot(keys, query)
    parts = []
    for other in range(first, tile):
        shift = jnp.where(other >= meta[2, tile], 0.0, -1000000000.0)
        parts.append(scores[(other - first) * TILE : (other - first + 1) * TILE] + shift)
    parts.append(jnp.where(diagonal_mask(meta, tile), scores[-TILE:], -1000000000.0))
    return jnp.concatenate(parts, 0) if len(parts) > 1 else parts[0]


def attend_kernel(get, put, outs, v_t):
    out_low, out_full, stats, q_t, k_t, k_rows, v_rows = outs
    meta, qg, kg = get(0), get(3)[...], get(4)[...]
    routes_t, squares, cos_t, sin_t, qkv = get(7), get(2), get(5), get(6), get(1)
    for tile in range(16):
        at = slice(tile * TILE, (tile + 1) * TILE)
        base = pl.ds(pl.multiple_of((tile - meta[2, tile]) * TILE, TILE), TILE)
        cos, sin = cos_t[:, base], sin_t[:, base]
        q_factor = lax.rsqrt(squares[0:1, at] * (1.0 / 1024) + EPS)
        k_factor = lax.rsqrt(squares[1:2, at] * (1.0 / 512) + EPS)
        query = rotate(qkv[0:64, at] * q_factor * qg, cos, sin)
        key = rotate(qkv[64:128, at] * k_factor * kg, cos, sin)
        value = qkv[128:192, at]
        q_t[:, at] = (query * 0.125).astype(BF)
        k_t[:, at] = key.astype(BF)
        v_t[:, at] = value.astype(BF)
        k_rows[at, :] = key.T.astype(BF)
        v_rows[at, :] = value.T.astype(BF)

    out_low[1024:1040, :] = jnp.concatenate(
        [routes_t[...].astype(F32), jnp.zeros((8, 128), F32)], 0
    ).astype(BF)

    for tile in range(16):
        first = max(0, tile - 7)
        mine = slice(tile * TILE, (tile + 1) * TILE)
        keys = slice(first * TILE, (tile + 1) * TILE)
        scores = strip_scores(meta, k_rows[keys, :], q_t[:, mine], tile, first)
        top = jnp.max(scores, 0, keepdims=True)
        weights = jnp.exp(scores - top)
        total = jnp.sum(weights, 0, keepdims=True)
        mixed = dot(v_t[:, keys], weights.astype(BF)) / total
        out_full[:, mine] = mixed
        half = tile // 8
        rows = slice((tile % 8) * TILE, (tile % 8 + 1) * TILE)
        out_low[rows, half * HD : (half + 1) * HD] = mixed.T.astype(BF)
        stats[0:1, mine] = top
        stats[1:2, mine] = total


def attend_back_kernel(get, put, outs, gk, gv, gain_q, gain_k):
    to_tokens, gq_weighted, keep, send, dots, gains = outs
    meta, qg, kg = get(0), get(4)[...], get(5)[...]
    qkv, squares, cos_t, sin_t, out_full, stats = [get(i) for i in (2, 3, 6, 7, 8, 9)]
    q_t, k_t, k_rows, v_rows, moved = [get(i) for i in (10, 11, 12, 13, 1)]
    gk[...] = jnp.zeros_like(gk)
    gv[...] = jnp.zeros_like(gv)
    gain_q[...] = jnp.zeros_like(gain_q)
    gain_k[...] = jnp.zeros_like(gain_k)

    def turned_back(tile, value):
        base = pl.ds(pl.multiple_of((tile - meta[2, tile]) * TILE, TILE), TILE)
        return rotate(value, cos_t[:, base], -sin_t[:, base])

    for tile in range(16):
        first = max(0, tile - 7)
        mine = slice(tile * TILE, (tile + 1) * TILE)
        keys = slice(first * TILE, (tile + 1) * TILE)
        g_out = moved[pl.ds(meta[1, tile], 1), 0:64, :][0].astype(F32)
        inverse = 1.0 / stats[1:2, mine]
        g_acc = (g_out * inverse).astype(BF)
        shift = jnp.sum(g_out * out_full[:, mine], 0, keepdims=True) * inverse
        query = q_t[:, mine]
        scores = strip_scores(meta, k_rows[keys, :], query, tile, first)
        weights = jnp.exp(scores - stats[0:1, mine])
        g_weights = dot(v_rows[keys, :], g_acc)
        g_scores = (weights * (g_weights - shift)).astype(BF)
        gk[:, keys] += dot(query, g_scores, 1, 1)
        gv[:, keys] += dot(g_acc, weights.astype(BF), 1, 1)
        g_query = turned_back(tile, dot(k_t[:, keys], g_scores) * 0.125)
        factor = lax.rsqrt(squares[0:1, mine] * (1.0 / 1024) + EPS)
        q_norm = qkv[0:64, mine] * factor
        weighted = g_query * qg
        gq_weighted[:, mine] = weighted
        dots[0:1, mine] = jnp.sum(weighted * q_norm, 0, keepdims=True)
        gain_q[...] += g_query * q_norm

    odd = meta[4, 0] % 2 == 1
    for tile in range(16):
        at = slice(tile * TILE, (tile + 1) * TILE)
        g_key = turned_back(tile, gk[:, at])
        k_norm = qkv[64:128, at] * lax.rsqrt(squares[1:2, at] * (1.0 / 512) + EPS)
        weighted = g_key * kg
        dots[1:2, at] = jnp.sum(weighted * k_norm, 0, keepdims=True)
        gain_k[...] += g_key * k_norm
        g_value = gv[:, at]
        to_tokens[pl.ds(meta[1, tile], 1), :, :] = jnp.concatenate(
            [gq_weighted[:, at], weighted, g_value], 0
        ).astype(BF)[None]
        keep[:, at] = jnp.where(odd, g_value, g_key)
        send[:, at] = jnp.where(odd, g_key, g_value)
    ones = jnp.ones((8, TILE), F32)
    gains[...] = jnp.concatenate(
        [
            dot(ones, gain_q[...], 1, 1, lax.Precision.HIGHEST),
            dot(ones, gain_k[...], 1, 1, lax.Precision.HIGHEST),
        ],
        1,
    )


def out_grad_kernel(get, put, outs):
    (result,) = outs
    meta, moved = get(0), get(1)
    ctx = lax.axis_index("ctx")
    turned = jnp.concatenate(
        [
            jnp.concatenate(
                [moved[pl.ds(meta[1, tile + 8 * half], 1), 64:128, :][0] for tile in range(8)], 1
            )
            for half in (0, 1)
        ],
        0,
    )
    for i in range(8):
        lanes = pl.ds(pl.multiple_of((slot_of(ctx, PIECES[i]) // 2) * 128, 128), 128)
        parts = []
        for piece in (i, i + 8):
            both = dot(turned, get(2 + piece)[0:1024, :])
            parts.append(both[0:64, 0:64] + both[64:128, 64:128])
        mine, other = parts
        odd = ctx % 2 == 1
        result[:, lanes] = jnp.concatenate(
            [jnp.where(odd, other, mine), jnp.where(odd, mine, other)], 1
        )


def linear_grad_kernel(get, put, outs, whole):
    z = lax.axis_index("fsdp") % 4
    odd = lax.axis_index("ctx") % 2 == 1
    kg = get(6)[...]
    qkv, squares, dots, gq_weighted, keep, other = [get(i) for i in range(6)]
    lows = []
    for tile in range(16):
        at = slice(tile * TILE, (tile + 1) * TILE)
        q_factor = lax.rsqrt(squares[0:1, at] * (1.0 / 1024) + EPS)
        k_factor = lax.rsqrt(squares[1:2, at] * (1.0 / 512) + EPS)
        q_norm = qkv[0:64, at] * q_factor
        k_norm = qkv[64:128, at] * k_factor
        g_q = q_factor * (gq_weighted[:, at] - q_norm * (dots[0:1, at] * (1.0 / 1024)))
        both = keep[:, at] + other[:, at]
        g_k = k_factor * (both * kg - k_norm * (dots[1:2, at] * (1.0 / 512)))
        lows.append(jnp.concatenate([g_q, jnp.where(odd, both, g_k)], 0).astype(BF))
    whole[0:128, :] = dot(jnp.concatenate(lows, 1), get(7)[...])
    out_grad, router_grad, ffn_gain_grad, gains, loss_parts = [get(i) for i in range(8, 13)]
    lane = iota((1, 128), 1)
    tail_rows = jnp.zeros((ROWS_OUT - ROW_LOSS - 1, 128), F32)
    loss = loss_parts[0:1, :]
    whole[128:192, :] = out_grad[...]
    whole[192:224, :] = router_grad[...]
    whole[224:232, :] = jnp.where(iota((8, 1024), 0) == 0, ffn_gain_grad[...], 0.0)
    tail = jnp.concatenate([gains[0:1, :], loss, tail_rows], 0)
    for out, dz in zip(outs, (0, 1, 3, 2)):
        for y in (0, 1):
            at = pl.ds(pl.multiple_of((y * 4 + (z + dz) % 4) * 128, 128), 128)
            out[y] = jnp.concatenate([whole[0:225, at], tail], 0).astype(BF)


def loss_again(total):
    parts = jnp.sum(total[ROW_LOSS : ROW_LOSS + 1, :], 1, keepdims=True)
    first = parts.astype(BF).astype(F32)
    second = (parts - first).astype(BF).astype(F32)
    third = parts - first - second
    lane = iota(total.shape, 1)
    pieces = jnp.where(lane == 0, first, jnp.where(lane == 1, second, third))
    use = (iota(total.shape, 0) == ROW_LOSS) & (lane < 3)
    return jnp.where(use, pieces, total)


def sum_z_kernel(get, put, outs):
    keep, send = outs
    low = lax.axis_index("fsdp") < 4
    parts = [get(i)[...].astype(F32) for i in range(4)]
    total = parts[0] + parts[1] + parts[2] + parts[3]
    keep[...] = jnp.where(low, total[0], total[1])
    send[...] = loss_again(jnp.where(low, total[1], total[0])).astype(BF)


def sum_y_kernel(get, put, outs):
    total = get(0)[...] + get(1)[...].astype(F32)
    outs[0][...] = loss_again(total).astype(BF)


def own_linear_kernel(get, put, outs):
    norms, factors = outs
    hidden, packed, mine, other = [get(i) for i in range(4)]
    even = lax.axis_index("ctx") % 2 == 0
    w_q = jnp.where(even, mine[...], other[...])
    w_k = jnp.where(even, other[:, 0:512], mine[:, 0:512])
    rows = hidden[...].astype(F32)
    factor = lax.rsqrt(jnp.mean(rows * rows, -1, keepdims=True) + EPS)
    gain = packed[192:208, :].astype(F32)[0:1, :]
    low = (rows * factor * gain).astype(BF)
    q_lin = dot(low, w_q).T
    k_lin = dot(low, w_k).T
    q_factor = lax.rsqrt(jnp.mean(q_lin * q_lin, 0, keepdims=True) + EPS)
    k_factor = lax.rsqrt(jnp.mean(k_lin * k_lin, 0, keepdims=True) + EPS)
    norms[0:1024, :] = q_lin * q_factor
    norms[1024:1536, :] = k_lin * k_factor
    factors[...] = jnp.where(iota((8, 128), 0) == 0, q_factor, k_factor)


def input_grad_kernel(get, put, outs):
    (result,) = outs
    norms, factors, moved = get(0), get(1), get(2)
    q = jnp.concatenate([moved[h, 0:64, :] for h in range(16)], 0).astype(F32)

    def key_rows(at):
        pairs = [
            moved[h, at : at + 64, :].astype(F32) + moved[h + 1, at : at + 64, :].astype(F32)
            for h in range(0, 16, 2)
        ]
        return jnp.concatenate(pairs, 0)

    k, v = key_rows(64), key_rows(128)
    q_norm, k_norm = norms[0:1024, :], norms[1024:1536, :]
    g_q = factors[0:1, :] * (q - q_norm * jnp.mean(q * q_norm, 0, keepdims=True))
    g_k = factors[1:2, :] * (k - k_norm * jnp.mean(k * k_norm, 0, keepdims=True))
    g_lin = jnp.concatenate([g_q, g_k, v], 0).astype(BF)
    even = lax.axis_index("ctx") % 2 == 0
    near, far = g_lin[0:1024], g_lin[1024:2048]
    g_normed = dot(jnp.where(even, near, far), get(3)[...], 0, 1)
    g_normed += dot(jnp.where(even, far, near), get(4)[...], 0, 1)
    hidden, packed, g_resid = get(5), get(6), get(7)
    rows = hidden[...].astype(F32)
    factor = lax.rsqrt(jnp.mean(rows * rows, -1, keepdims=True) + EPS)
    n = rows * factor
    gain = packed[192:208, :].astype(F32)[0:1, :]
    weighted = g_normed * gain
    result[...] = g_resid[...] + factor * (
        weighted - n * jnp.mean(weighted * n, -1, keepdims=True)
    )


def stage(target, e, lane, values):
    for slot in range(16):
        at = (2 * slot + e) * FULL
        target[at : at + FULL, lane : lane + 512] = values[slot * CAP : slot * CAP + FULL]


def route_kernel(get, put, outs, spread, named, w_full, out_rows):
    rows, act, result, place, gates, resid_out, post_out, probs = outs[:8]
    gate_pre, up_pre = outs[8:]
    meta, packed = get(0), get(1)
    ctx = lax.axis_index("ctx")
    odd = ctx % 2 == 1
    for n in range(2, 18):
        get(n)
    first_x, first_out, first_w, experts = 18, 2, 34, 36
    for i in range(8):
        lanes = pl.ds(pl.multiple_of((slot_of(ctx, PIECES[i]) // 2) * 128, 128), 128)
        mine = get(first_out + i)[0:1024, :]
        other = get(first_out + i + 8)[0:1024, :]
        low, high = jnp.where(odd, other, mine), jnp.where(odd, mine, other)
        out_rows[0:1024, lanes] = jnp.concatenate([low[:, 0:64], high[:, 0:64]], 1)
        out_rows[1024:2048, lanes] = jnp.concatenate([low[:, 64:128], high[:, 64:128]], 1)
    for n, piece in enumerate(PIECES):
        slot = slot_of(ctx, piece)
        routes = get(first_out + n)[1024:1040, :].astype(F32)[0:8, :]
        for e in (0, 1):
            expert = (2 * ctx + e).astype(F32)
            hit = jnp.max(jnp.where(routes == expert, 1.0, 0.0), 0, keepdims=True)
            named[pl.ds(e * 16 + slot, 1), :] = hit
    place[...] = place_rows(named[...])
    xs = [get(first_x + n) for n in range(16)]
    for core in (0, 1):
        columns = pl.ds(pl.multiple_of(((ctx + core) % 2) * 512, 512), 512)
        w_full[:, columns] = get(first_w + core)[...]
    gain = packed[192:208, :].astype(F32)[1:2, :]
    router = packed[208:240, :]
    for group in range(4):
        slots = [slot_of(ctx, PIECES[group * 4 + j]) for j in range(4)]
        tiles = [pl.ds(pl.multiple_of(meta[0, slot] * TILE, TILE), TILE) for slot in slots]
        mixed = jnp.concatenate([out_rows[at, :] for at in tiles], 0)
        x = jnp.concatenate([xs[group * 4 + j][...] for j in range(4)], 0)
        resid = x.astype(F32) + dot(mixed, w_full[...])
        factor = lax.rsqrt(jnp.mean(resid * resid, -1, keepdims=True) + EPS)
        post = (resid * factor * gain).astype(BF)
        logits = dot(router, post, 1, 1)
        shifted = jnp.exp(logits - jnp.max(logits, 0, keepdims=True))
        p = shifted / jnp.sum(shifted, 0, keepdims=True)
        if group == 0:
            resid_out[...] = resid[0:TILE]
            post_out[...] = post[0:TILE]
            probs[...] = p[:, 0:TILE]
        gate = [
            jnp.sum(jnp.where(iota(p.shape, 0) == 2 * ctx + e, p, 0.0), 0, keepdims=True)
            for e in (0, 1)
        ]
        for j, slot in enumerate(slots):
            own = slice(j * TILE, (j + 1) * TILE)
            at = pl.ds(pl.multiple_of(slot * CAP, 8), CAP)
            picks = []
            for e in (0, 1):
                gates[pl.ds(e * 16 + slot, 1), :] = gate[e][:, own]
                picks.append(place[pl.ds(pl.multiple_of(e * SLOTS + slot * CAP, 8), CAP), :])
            both = dot(jnp.concatenate(picks, 0).astype(BF), post[own])
            spread[at, :] = both[0:CAP]
            spread[pl.ds(pl.multiple_of(SLOTS + slot * CAP, 8), CAP), :] = both[CAP : 2 * CAP]
    rows[...] = spread[...].astype(BF)
    for j in (3, 4, 5, 6, 7, 0):
        put(j)
    weights = get(experts)
    for e in (0, 1):
        gate_w, up_w, down_a, down_b = expert_weights(weights, e)
        x = rows[e * SLOTS : (e + 1) * SLOTS, :]
        gp, up = dot(x, gate_w), dot(x, up_w)
        gate_pre[e] = gp.astype(BF)
        up_pre[e] = up.astype(BF)
        low = (gp * jax.nn.sigmoid(gp) * up).astype(BF)
        act[e] = low
        stage(spread, e, 0, dot(low, down_a))
        stage(spread, e, 512, dot(low, down_b))
        put(8, (e,))
        put(9, (e,))
        put(1, (e,))
    result[...] = spread[0:SENT, :].astype(BF)
    put(2)


def expert_weights(ref, e):
    at = e * 384
    gate = ref[:, at : at + 128, :].reshape(1024, 512)
    up = ref[:, at + 128 : at + 256, :].reshape(1024, 512)
    down_a = ref[:, at + 256 : at + 320, :].reshape(512, 512)
    down_b = ref[:, at + 320 : at + 384, :].reshape(512, 512)
    return gate, up, down_a, down_b


def expert_back_kernel(get, put, outs, spread):
    result, g_rows, g_gate, g_up = outs
    ctx = lax.axis_index("ctx")
    place, gates = get(16), get(17)
    for n in range(16):
        get(n)
    for n, piece in enumerate(PIECES):
        slot = slot_of(ctx, piece)
        at = pl.ds(pl.multiple_of(slot * CAP, 8), CAP)
        picks, scales = [], []
        for e in (0, 1):
            pick = place[pl.ds(pl.multiple_of(e * SLOTS + slot * CAP, 8), CAP), :]
            gate = gates[pl.ds(e * 16 + slot, 1), :]
            scales.append(jnp.sum(pick * gate, 1, keepdims=True))
            picks.append(pick)
        both = dot(jnp.concatenate(picks, 0).astype(BF), get(n)[...])
        spread[at, :] = both[0:CAP] * scales[0]
        second = pl.ds(pl.multiple_of(SLOTS + slot * CAP, 8), CAP)
        spread[second, :] = both[CAP : 2 * CAP] * scales[1]
    g_rows[...] = spread[...].astype(BF)
    put(1)
    weights, gate_pre, up_pre = get(18), get(19), get(20)
    for e in (0, 1):
        gate, up, down_a, down_b = expert_weights(weights, e)
        own = slice(e * SLOTS, (e + 1) * SLOTS)
        g_act = dot(g_rows[own, 0:512], down_a, 1, 1)
        g_act += dot(g_rows[own, 512:1024], down_b, 1, 1)
        gp, up_value = gate_pre[e].astype(F32), up_pre[e].astype(F32)
        sg = jax.nn.sigmoid(gp)
        gg = (g_act * up_value * sg * (1.0 + gp * (1.0 - sg))).astype(BF)
        gu = (g_act * (gp * sg)).astype(BF)
        g_gate[e] = gg
        g_up[e] = gu
        for lane in (0, 512):
            part = dot(gg, gate[lane : lane + 512], 1, 1) + dot(gu, up[lane : lane + 512], 1, 1)
            stage(spread, e, lane, part)
    result[...] = spread[0:SENT, :].astype(BF)


def expert_weight_kernel(rows, g_rows, act, g_gate, g_up, result):
    x, g = rows[...], g_rows[...]
    result[:, 0:128, :] = dot(x, g_gate[0], 0, 0).astype(BF).reshape(8, 128, 512)
    result[:, 128:256, :] = dot(x, g_up[0], 0, 0).astype(BF).reshape(8, 128, 512)
    low = act[0]
    result[:, 256:320, :] = dot(low, g[:, 0:512], 0, 0).astype(BF).reshape(8, 64, 512)
    result[:, 320:384, :] = dot(low, g[:, 512:1024], 0, 0).astype(BF).reshape(8, 64, 512)


HALF = pl.BlockSpec((SLOTS, 1024), lambda e: (e, 0))
INNER = pl.BlockSpec((1, SLOTS, 512), lambda e: (e, 0, 0))
WEIGHTS = pl.BlockSpec((8, 384, 512), lambda e: (0, e, 0))


def expert_call(body, outs, out_specs, args, in_specs, name, flops, scratch=()):
    size = sum(int(np.prod(o.shape)) * o.dtype.itemsize for o in outs)
    size += sum(int(np.prod(a.shape)) * a.dtype.itemsize for a in args)
    return pl.pallas_call(
        body,
        grid=(2,),
        out_shape=outs,
        in_specs=in_specs,
        out_specs=out_specs,
        scratch_shapes=list(scratch),
        compiler_params=pltpu.CompilerParams(vmem_limit_bytes=58 * 2**20),
        cost_estimate=pl.CostEstimate(flops=flops, bytes_accessed=size, transcendentals=0),
        name=name,
    )(*args)


def combine_kernel(get, put, outs):
    result, g_result, g_low, loss_parts = outs
    meta, consts = get(0), get(1)
    moved, high, low, resid, teacher = [get(i) for i in range(2, 7)]
    slot = meta[4, 0]
    tile = meta[0, slot]
    room = meta[3, tile] - (tile - meta[2, tile]) * TILE
    valid = (iota((TILE, 1), 0) < room).astype(F32)
    total = resid[...] + dot(high[...], moved[...], 0, 0) + dot(low[...], moved[...], 0, 0)
    result[...] = total.astype(BF)
    errors = (total - teacher[...].astype(F32)) * valid
    g = errors * consts[0:1, 0:1]
    g_result[...] = g
    g_low[...] = g.astype(BF)
    squared = jnp.sum(jnp.sum(errors * errors, 0, keepdims=True), 1, keepdims=True)
    first = squared.astype(BF).astype(F32)
    second = (squared - first).astype(BF).astype(F32)
    third = squared - first - second
    lane = iota((8, 128), 1)
    loss_parts[...] = jnp.where(
        lane == 0, first, jnp.where(lane == 1, second, jnp.where(lane == 2, third, 0.0))
    )


def router_grad_kernel(moved, place, probs, g_result, post, g_logits, router_grad):
    p = probs[...]
    g_high, g_low = split(g_result[...])
    match = dot(moved[...], g_high, 1, 1) + dot(moved[...], g_low, 1, 1)
    picked = place[...].astype(F32) * match
    g_p = dot(slot_experts().astype(F32), picked, 0, 0, lax.Precision.HIGHEST)
    g_z = (p * (g_p - jnp.sum(p * g_p, 0, keepdims=True))).astype(BF)
    g_logits[...] = g_z
    router_grad[...] = dot(g_z, post[...])


def resid_grad_kernel(get, put, outs):
    g_resid_out, ffn_gain_grad, to_heads = outs
    moved, place, g_logits, packed, resid_in, g_result = [get(i) for i in range(6)]
    core = lax.axis_index("ctx") % 2
    g_post = dot(g_logits[...], packed[208:240, :], 0, 0)
    g_post += dot(place[...], moved[...], 0, 0)
    resid = resid_in[...]
    gain = packed[192:208, :].astype(F32)[1:2, :]
    factor = lax.rsqrt(jnp.mean(resid * resid, -1, keepdims=True) + EPS)
    n = resid * factor
    ffn_gain_grad[...] = jnp.broadcast_to(jnp.sum(g_post * n, 0, keepdims=True), (8, 1024))
    weighted = g_post * gain
    g_resid = g_result[...] + factor * (
        weighted - n * jnp.mean(weighted * n, -1, keepdims=True)
    )
    g_resid_out[...] = g_resid
    low = g_resid.astype(BF)
    near, far = low[:, 0:512], low[:, 512:1024]
    mine, other = jnp.where(core == 0, near, far), jnp.where(core == 0, far, near)
    g_mixed = (dot(get(6)[...], mine, 1, 1) + dot(get(7)[...], other, 1, 1)).astype(BF)
    turned = g_resid.T.astype(BF)
    for head in range(16):
        at = slice(head * 64, (head + 1) * 64)
        to_heads[head, 0:64, :] = g_mixed[at]
        to_heads[head, 64:128, :] = turned[at]


def final_kernel(get, put, outs, gain_rows):
    (
        grad_q, grad_k, grad_v, grad_o, router, q_gain, k_gain, ffn_gain, attn_gain, loss,
    ) = outs
    meta, consts, near, up, down, far, na = [get(i) for i in range(7)]
    wq, wk, wv = get(7), get(8), get(9)
    x = meta[4, 0] // 4
    shard = meta[4, 1]
    summed = jnp.zeros((ROWS_OUT - ROW_GR, 128), F32)
    for ref, dx in ((near, 0), (up, 3), (down, 1), (far, 2)):
        index = (x + dx) % 4
        blocks = ref[...].astype(F32)
        wide = pl.ds(pl.multiple_of(index * 256, 256), 256)
        slim = pl.ds(pl.multiple_of(index * 128, 128), 128)
        grad_q[:, wide] = blocks[:, 0:64, :].reshape(256, 128).T
        grad_o[:, wide] = blocks[:, 128:192, :].reshape(256, 128).T
        grad_k[:, slim] = jnp.concatenate([blocks[0, 64:128], blocks[2, 64:128]], 0).T
        grad_v[:, slim] = jnp.concatenate([blocks[1, 64:128], blocks[3, 64:128]], 0).T
        tails = blocks[:, ROW_GR:, :]
        summed += tails[0] + tails[1] + tails[2] + tails[3]
        for j in range(4):
            gain_rows[pl.ds(index * 4 + j, 1), :] = tails[j, 33:34, :]
    router[...] = summed[0:32]
    even = gain_rows[pl.ds(2 * shard, 1), :]
    odd = gain_rows[pl.ds(2 * shard + 1, 1), :]
    q_gain[...] = jnp.concatenate([even[:, 0:64], odd[:, 0:64]], 1)
    k_gain[...] = (even + odd)[:, 64:128]
    ffn_gain[...] = summed[32:33]
    folded = (
        jnp.sum(grad_q[...] * wq[...].astype(F32), 1, keepdims=True)
        + jnp.sum(grad_k[...] * wk[...].astype(F32), 1, keepdims=True)
        + jnp.sum(grad_v[...] * wv[...].astype(F32), 1, keepdims=True)
    )
    attn_gain[...] = jnp.broadcast_to(folded, (128, 128)).T[0:1, :] / na[...].astype(F32)
    loss[...] = jnp.sum(summed[34:35, :], 1, keepdims=True) * consts[1:2, 0:1]


def unpack_kernel(get, put, outs):
    grad_gate, grad_up, grad_down = outs
    shard = get(0)
    for e in (0, 1):
        at = e * 384
        grad_gate[e] = shard[at : at + 128, :].astype(F32)
        grad_up[e] = shard[at + 128 : at + 256, :].astype(F32)
        grad_down[e, :, 0:512] = shard[at + 256 : at + 320, :].astype(F32)
        grad_down[e, :, 512:1024] = shard[at + 320 : at + 384, :].astype(F32)


def gather_rows(rows, y_again=True):
    across = ctx_move(rows, YHI)
    up, down = ctx_move(rows, XUP), ctx_move(rows, XDOWN)
    across_up = ctx_move(up, YHI) if y_again else ctx_move(across, XUP)
    across_down = ctx_move(across, XDOWN)
    far, across_far = ctx_move(up, XUP), ctx_move(across_down, XDOWN)
    mine = [rows, across, up, down, across_up, across_down, far, across_far]
    return mine + [ctx_move(piece, CORE) for piece in mine]


def sum_ctx(value, beside=()):
    value = value + ctx_move(value, CORE)
    moved, *beside = lax.optimization_barrier((ctx_move(value, YHI), *beside))
    value = value + moved
    up, down, far = ctx_move(value, XUP), ctx_move(value, XDOWN), ctx_move(value, XTWO)
    return value + up + down + far, *beside


def exchange(value, axis):
    return lax.all_to_all(value, axis, split_axis=0, concat_axis=0, tiled=True)


def on_device(
    hidden,
    teacher,
    lengths,
    tile_perm,
    routes,
    norm_attn,
    w_query,
    w_key,
    w_value,
    w_out,
    q_gain,
    k_gain,
    norm_ffn,
    w_router,
    w_gate,
    w_up,
    w_down,
):
    ctx = lax.axis_index("ctx")
    shard = lax.axis_index("fsdp")
    x_in = hidden[0]
    block, expert_block, meta = kernel_call(
        pack_kernel,
        [
            shape((ROWS_IN + 512, 128), BF),
            shape((768, 512), BF),
            shape((5, 16), jnp.int32),
        ],
        [
            lengths, tile_perm, w_query, w_key, w_value, w_router.T,
            norm_attn.reshape(1, 128), norm_ffn.reshape(1, 128),
            q_gain.reshape(1, 128), k_gain.reshape(1, 64),
            w_out, w_gate, w_up, w_down,
        ],
        smem=(0, 1),
        smem_out=(2,),
        name="pack",
    )
    x_first, block = lax.optimization_barrier((x_in, block))
    pieces = gather_rows(x_first)
    other = fsdp_move(block, YLO)
    first = shard < 4
    pair = jnp.stack([jnp.where(first, block, other), jnp.where(first, other, block)])
    pair_moves = [fsdp_move(pair, ZUP), fsdp_move(pair, ZDOWN)]
    pair_moves.append(fsdp_move(pair_moves[0], ZUP))
    *pair_moves, pieces[3], pieces[7] = lax.optimization_barrier(
        (*pair_moves, pieces[3], pieces[7])
    )
    packed, w_mine, qg, kg, consts = kernel_call(
        assemble_kernel,
        [
            shape((ROWS_IN, 1024), BF),
            shape((1024, 512), BF),
            shape((HD, 1), F32),
            shape((HD, 1), F32),
            shape((8, 128), F32),
        ],
        [meta, pair] + pair_moves,
        smem=(0,),
        name="assemble",
    )
    w_other = ctx_move(w_mine, CORE)
    frequencies = 10000.0 ** (-jnp.arange(32, dtype=F32) / 32)
    angles = frequencies[:, None] * jnp.arange(1024, dtype=F32)[None, :]
    cos_t, sin_t = jnp.cos(angles), jnp.sin(angles)
    routes_t = routes[0].T.astype(BF)

    expert_block, *_ = lax.optimization_barrier((expert_block, packed, *pieces[4:8]))
    experts = lax.all_gather(expert_block, "fsdp", axis=0)
    qkv, squares, normed = streamed_call(
        project_kernel,
        [shape((192, 2048), F32), shape((2, 2048), F32), shape((2048, 1024), BF)],
        [meta, packed] + pieces,
        smem=(0,),
        name="project",
        flops=2 * 2048 * 1024 * 192,
    )
    (squares,) = sum_ctx(squares)
    mixed_low, mixed_full, stats, q_t, k_t, k_rows, v_rows = streamed_call(
        attend_kernel,
        [
            shape((1040, 128), BF),
            shape((64, 2048), F32),
            shape((2, 2048), F32),
            shape((64, 2048), BF),
            shape((64, 2048), BF),
            shape((2048, 64), BF),
            shape((2048, 64), BF),
        ],
        [meta, qkv, squares, qg, kg, cos_t, sin_t, routes_t],
        smem=(0,),
        scratch=[pltpu.VMEM((64, 2048), BF)],
        name="attend",
        flops=54 * 4 * 128 * 128 * 64,
    )
    even = ctx % 2 == 0
    qkv_half = jnp.where(even, w_query, jnp.concatenate([w_key, w_value], 1))
    qkv_half, mixed_low = lax.optimization_barrier((qkv_half, mixed_low))
    qkv_mine = lax.all_gather(qkv_half, "fsdp", axis=0, tiled=True)
    qkv_other = ctx_move(qkv_mine, CORE)
    mixed_pieces = gather_rows(mixed_low, False)
    (
        rows, act, expert_out, place_here, gates, resid, post, probs, gate_pre, up_pre,
    ) = streamed_call(
        route_kernel,
        [
            shape((2 * SLOTS, 1024), BF),
            shape((2, SLOTS, 512), BF),
            shape((SENT, 1024), BF),
            shape((2 * SLOTS, 128), F32),
            shape((32, 128), F32),
            shape((128, 1024), F32),
            shape((128, 1024), BF),
            shape((32, 128), F32),
            shape((2, SLOTS, 512), BF),
            shape((2, SLOTS, 512), BF),
        ],
        [meta, packed] + mixed_pieces + pieces + [w_mine, w_other, experts],
        smem=(0,),
        stream=range(2, 37),
        stream_out=range(10),
        scratch=[
            pltpu.VMEM((2 * SLOTS, 1024), F32),
            pltpu.VMEM((32, 128), F32),
            pltpu.VMEM((1024, 1024), BF),
            pltpu.VMEM((2048, 1024), BF),
        ],
        name="route_experts",
        flops=2 * 2048 * 1024 * 1024 + 2 * 2 * SLOTS * 1024 * 1536,
    )
    returned = exchange(expert_out, "ctx")
    place, gate_high, gate_low = kernel_call(
        slots_kernel, [shape((SENT, 128), BF)] * 3, [routes_t, probs], name="slots"
    )
    result, g_result, g_low, loss_parts = streamed_call(
        combine_kernel,
        [
            shape((128, 1024), BF),
            shape((128, 1024), F32),
            shape((128, 1024), BF),
            shape((8, 128), F32),
        ],
        [meta, consts, returned, gate_high, gate_low, resid, teacher[0]],
        smem=(0,),
        stream=range(2, 7),
        name="combine",
        flops=2 * SLOTS * 128 * 1024 * 4,
    )
    g_pieces = gather_rows(g_low)
    g_logits, router_grad = kernel_call(
        router_grad_kernel,
        [shape((32, 128), BF), shape((32, 1024), F32)],
        [returned, place, probs, g_result, post],
        name="router_grad",
        brief=True,
    )
    g_rows, g_slots, g_gate, g_up = streamed_call(
        expert_back_kernel,
        [
            shape((SENT, 1024), BF),
            shape((2 * SLOTS, 1024), BF),
            shape((2, SLOTS, 512), BF),
            shape((2, SLOTS, 512), BF),
        ],
        g_pieces + [place_here, gates, experts, gate_pre, up_pre],
        stream=range(21),
        stream_out=range(4),
        scratch=[pltpu.VMEM((2 * SLOTS, 1024), F32)],
        name="experts_back",
        flops=2 * 2 * SLOTS * 1024 * 1536,
    )
    g_returned = exchange(g_rows, "ctx")
    (expert_grads,) = expert_call(
        expert_weight_kernel,
        [shape((8, 768, 512), BF)],
        [WEIGHTS],
        [rows, g_slots, act, g_gate, g_up],
        [HALF, HALF, INNER, INNER, INNER],
        "experts_weights",
        2 * 2 * SLOTS * 1024 * 1536,
    )
    expert_shard = lax.psum_scatter(
        expert_grads.reshape(8 * 768, 512), "fsdp", scatter_dimension=0, tiled=True
    )

    grad_gate, grad_up, grad_down = streamed_call(
        unpack_kernel,
        [shape((2, 128, 512), F32), shape((2, 128, 512), F32), shape((2, 64, 1024), F32)],
        [expert_shard],
        name="unpack",
    )
    g_resid, ffn_gain_grad, to_heads = streamed_call(
        resid_grad_kernel,
        [shape((128, 1024), F32), shape((8, 1024), F32), shape((16, 128, 128), BF)],
        [g_returned, place, g_logits, packed, resid, g_result, w_mine, w_other],
        stream=(0, 1, 4, 5, 6, 7),
        name="resid_grad",
        flops=2 * 128 * 1024 * 2400,
    )
    norms, factors = streamed_call(
        own_linear_kernel,
        [shape((1536, 128), F32), shape((8, 128), F32)],
        [x_in, packed, qkv_mine, qkv_other],
        name="own_linear",
    )
    to_heads, norms, factors = lax.optimization_barrier((to_heads, norms, factors))
    moved = exchange(to_heads.reshape(2048, 128), "ctx").reshape(16, 128, 128)
    to_tokens, gq_weighted, keep, send, dots, gains = streamed_call(
        attend_back_kernel,
        [
            shape((16, 192, 128), BF),
            shape((64, 2048), F32),
            shape((64, 2048), F32),
            shape((64, 2048), F32),
            shape((2, 2048), F32),
            shape((8, 128), F32),
        ],
        [
            meta, moved, qkv, squares, qg, kg, cos_t, sin_t,
            mixed_full, stats, q_t, k_t, k_rows, v_rows,
        ],
        smem=(0,),
        scratch=[
            pltpu.VMEM((64, 2048), F32),
            pltpu.VMEM((64, 2048), F32),
            pltpu.VMEM((64, 128), F32),
            pltpu.VMEM((64, 128), F32),
        ],
        name="attend_back",
        flops=10**11,
    )
    (out_grad,) = streamed_call(
        out_grad_kernel,
        [shape((64, 1024), F32)],
        [meta, moved] + mixed_pieces,
        smem=(0,),
        name="out_grad",
        flops=2 * 2048 * 64 * 1024,
    )
    dots, out_grad = sum_ctx(dots, (out_grad,))
    to_tokens, dots = lax.optimization_barrier((to_tokens, dots))
    g_lin = exchange(to_tokens.reshape(16 * 192, 128), "ctx").reshape(16, 192, 128)
    received = ctx_move(send, CORE)
    scattered = streamed_call(
        linear_grad_kernel,
        [shape((2, ROWS_OUT, 128), BF)] * 4,
        [
            qkv, squares, dots, gq_weighted, keep, received, kg, normed,
            out_grad, router_grad, ffn_gain_grad, gains, loss_parts,
        ],
        stream=(7,),
        scratch=[pltpu.VMEM((232, 1024), F32)],
        name="linear_grad",
        flops=2 * 2048 * 128 * 1024,
    )
    came = [fsdp_move(part, pairs) for part, pairs in zip(scattered[1:], (ZUP, ZDOWN, ZTWO))]
    *came, grad_gate, grad_up, grad_down = lax.optimization_barrier(
        (*came, grad_gate, grad_up, grad_down)
    )
    keep_z, send_z = streamed_call(
        sum_z_kernel,
        [shape((ROWS_OUT, 128), F32), shape((ROWS_OUT, 128), BF)],
        [scattered[0]] + came,
        name="sum_z",
        limit=8,
    )
    send_z, g_lin = lax.optimization_barrier((send_z, g_lin))
    (summed,) = streamed_call(
        sum_y_kernel,
        [shape((ROWS_OUT, 128), BF)],
        [keep_z, fsdp_move(send_z, YLO)],
        name="sum_y",
        limit=8,
    )
    sibling = ctx_move(summed, CORE)
    chip = jnp.stack([jnp.where(even, summed, sibling), jnp.where(even, sibling, summed)])
    across = ctx_move(chip, YHI)
    low_y = (ctx // 2) % 2 == 0
    four = jnp.concatenate([jnp.where(low_y, chip, across), jnp.where(low_y, across, chip)])
    four_up, four_down, four_far = (
        ctx_move(four, XUP),
        ctx_move(four, XDOWN),
        ctx_move(four, XTWO),
    )
    (input_grad,) = streamed_call(
        input_grad_kernel,
        [shape((128, 1024), F32)],
        [norms, factors, g_lin, qkv_mine, qkv_other, x_in, packed, g_resid],
        stream=(3, 4),
        name="input_grad",
        flops=2 * 128 * 2048 * 1024,
    )
    (
        grad_q, grad_k, grad_v, grad_o, router, q_gain_grad, k_gain_grad, ffn_gain, attn_gain,
        loss,
    ) = streamed_call(
        final_kernel,
        [
            shape((128, 1024), F32),
            shape((128, 512), F32),
            shape((128, 512), F32),
            shape((128, 1024), F32),
            shape((32, 128), F32),
            shape((1, 128), F32),
            shape((1, 64), F32),
            shape((1, 128), F32),
            shape((1, 128), F32),
            shape((1, 1), F32),
        ],
        [
            meta, consts, four, four_up, four_down, four_far, norm_attn.reshape(1, 128),
            w_query, w_key, w_value,
        ],
        smem=(0,),
        scratch=[pltpu.VMEM((16, 128), F32)],
        name="final",
        limit=16,
    )
    return (
        result[None],
        loss.reshape(()),
        input_grad[None],
        attn_gain.reshape(128),
        grad_q,
        grad_k,
        grad_v,
        grad_o,
        q_gain_grad.reshape(128),
        k_gain_grad.reshape(64),
        ffn_gain.reshape(128),
        router.T,
        grad_gate,
        grad_up,
        grad_down,
    )


def solution(mesh):
    return jax.shard_map(
        on_device,
        mesh=mesh,
        in_specs=(
            P("fsdp", "ctx", None),
            P("fsdp", "ctx", None),
            P("fsdp", None),
            P("fsdp", None),
            P("fsdp", "ctx", None),
            P("fsdp"),
            P("fsdp", None),
            P("fsdp", None),
            P("fsdp", None),
            P("fsdp", None),
            P("fsdp"),
            P("fsdp"),
            P("fsdp"),
            P("fsdp", None),
            P("ctx", "fsdp", None),
            P("ctx", "fsdp", None),
            P("ctx", "fsdp", None),
        ),
        out_specs=(
            P("fsdp", "ctx", None),
            P(),
            P("fsdp", "ctx", None),
            P("fsdp"),
            P("fsdp", None),
            P("fsdp", None),
            P("fsdp", None),
            P("fsdp", None),
            P("fsdp"),
            P("fsdp"),
            P("fsdp"),
            P("fsdp", None),
            P("ctx", "fsdp", None),
            P("ctx", "fsdp", None),
            P("ctx", "fsdp", None),
        ),
        check_vma=False,
    )
```

```python
import functools

import jax
import jax.numpy as jnp
import numpy as np
from jax import lax
from jax.experimental import pallas as pl
from jax.experimental.pallas import tpu as pltpu
from jax.sharding import PartitionSpec as P

TILE = 128
HD = 64
FULL = 36
CAP = 40
SLOTS = 16 * CAP
SENT = 32 * FULL
EPS = 1e-05
F32 = jnp.float32
BF = jnp.bfloat16

ROW_GAIN = 192
ROW_ROUTER = 208
ROWS_IN = 240
ROW_OUT = 128
ROW_GR = 192
ROW_NF = 224
ROW_LOSS = 226
ROWS_OUT = 240

CORE = [(i, i ^ 1) for i in range(16)]
YHI = [(i, i ^ 2) for i in range(16)]
XUP = [(i, (i + 4) % 16) for i in range(16)]
XDOWN = [(i, (i - 4) % 16) for i in range(16)]
XTWO = [(i, (i + 8) % 16) for i in range(16)]
YLO = [(i, i ^ 4) for i in range(8)]
ZUP = [(i, (i // 4) * 4 + (i + 1) % 4) for i in range(8)]
ZDOWN = [(i, (i // 4) * 4 + (i - 1) % 4) for i in range(8)]
ZTWO = [(i, (i // 4) * 4 + (i + 2) % 4) for i in range(8)]
PIECES = [
    (dx, dy, dc)
    for dc in (0, 1)
    for dx, dy in ((0, 0), (0, 1), (-1, 0), (1, 0), (-1, 1), (1, 1), (2, 0), (2, 1))
]


def ctx_move(value, pairs):
    return lax.ppermute(value, "ctx", pairs)


def fsdp_move(value, pairs):
    return lax.ppermute(value, "fsdp", pairs)


def dims(left, right):
    return (((left,), (right,)), ((), ()))


def dot(a, b, left=1, right=0, precision=None):
    return lax.dot_general(
        a, b, dims(left, right), preferred_element_type=F32, precision=precision
    )


def split(value):
    high = value.astype(BF)
    return high, (value - high.astype(F32)).astype(BF)


def iota(shape, axis):
    return lax.broadcasted_iota(jnp.int32, shape, axis)


def kernel_call(
    body, outs, args, smem=(), smem_out=(), anywhere=(), scratch=(), name=None, flops=0, brief=False
):
    specs = [
        pl.BlockSpec(
            memory_space=pltpu.SMEM if i in smem else pl.ANY if i in anywhere else pltpu.VMEM
        )
        for i in range(len(args))
    ]
    size = sum(int(np.prod(o.shape)) * o.dtype.itemsize for o in outs)
    size += sum(int(np.prod(a.shape)) * a.dtype.itemsize for a in args)
    if brief:
        size = 0
    return pl.pallas_call(
        body,
        out_shape=outs,
        in_specs=specs,
        out_specs=[
            pl.BlockSpec(memory_space=pltpu.SMEM if i in smem_out else pltpu.VMEM)
            for i in range(len(outs))
        ],
        scratch_shapes=list(scratch),
        compiler_params=pltpu.CompilerParams(
            vmem_limit_bytes=58 * 2**20
        ),
        cost_estimate=pl.CostEstimate(flops=flops, bytes_accessed=size, transcendentals=0),
        name=name,
    )(*args)


def streamed_call(
    body, outs, args, smem=(), stream=(), stream_out=(), scratch=(), name=None, flops=0, limit=58
):
    count, results = len(args), len(outs)
    moved, pushed = list(stream), list(stream_out)
    auto = [i for i in range(count) if i not in smem and i not in moved]
    auto_out = [j for j in range(results) if j not in pushed]
    puts = 40

    def kernel(*refs):
        ins, targets = refs[:count], refs[count : count + results]
        rest = refs[count + results :]
        held = dict(zip(moved, rest[: len(moved)]))
        staged = list(targets)
        for j, ref in zip(pushed, rest[len(moved) : len(moved) + len(pushed)]):
            staged[j] = ref
        own = rest[len(moved) + len(pushed) : -2]
        in_sems, out_sems = rest[-2:]
        copies = {}
        for n, i in enumerate(moved):
            copies[i] = pltpu.make_async_copy(ins[i], held[i], in_sems.at[n])
            copies[i].start()
        arrived, sent, started = set(), [], set()

        def get(i):
            if i not in copies:
                return ins[i]
            if i not in arrived:
                copies[i].wait()
                arrived.add(i)
            return held[i]

        def put(j, index=None):
            source = staged[j] if index is None else staged[j].at[index]
            target = targets[j] if index is None else targets[j].at[index]
            copy = pltpu.make_async_copy(source, target, out_sems.at[len(sent)])
            copy.start()
            sent.append(copy)
            started.add(j)

        body(get, put, staged, *own)
        for i in moved:
            get(i)
        for j in pushed:
            if j not in started:
                put(j)
        for copy in sent:
            copy.wait()

    specs = [
        pl.BlockSpec(
            memory_space=pltpu.SMEM if i in smem else pltpu.VMEM if i in auto else pltpu.HBM
        )
        for i in range(count)
    ]
    size = sum(int(np.prod(o.shape)) * o.dtype.itemsize for o in outs)
    size += sum(int(np.prod(a.shape)) * a.dtype.itemsize for a in args)
    buffers = [pltpu.VMEM(args[i].shape, args[i].dtype) for i in moved]
    buffers += [pltpu.VMEM(outs[j].shape, outs[j].dtype) for j in pushed]
    return pl.pallas_call(
        kernel,
        out_shape=outs,
        in_specs=specs,
        out_specs=[
            pl.BlockSpec(memory_space=pltpu.VMEM if j in auto_out else pltpu.HBM)
            for j in range(results)
        ],
        scratch_shapes=buffers
        + list(scratch)
        + [pltpu.SemaphoreType.DMA((max(1, len(moved)),)), pltpu.SemaphoreType.DMA((puts,))],
        compiler_params=pltpu.CompilerParams(vmem_limit_bytes=limit * 2**20),
        cost_estimate=pl.CostEstimate(flops=flops, bytes_accessed=size, transcendentals=0),
        name=name,
    )(*args)


def shape(dims_, dtype):
    return jax.ShapeDtypeStruct(dims_, dtype)


def pack_kernel(
    lens, perm, wq, wk, wv, wr, na, nf, qg, kg, wo, w_gate, w_up, w_down, out, big, meta
):
    ctx = lax.axis_index("ctx")
    for tile in range(16):
        meta[0, tile] = perm[0, tile]
        meta[1, perm[0, tile]] = tile
    start = jnp.int32(0)
    total = jnp.int32(0)
    begins = []
    for seq in range(5):
        length = lens[0, seq]
        begins.append((start, length))
        start = start + (length + TILE - 1) // TILE
        total = total + length
    for tile in range(16):
        first, length = begins[0]
        for begin, own in begins[1:]:
            later = tile >= begin
            first = jnp.where(later, begin, first)
            length = jnp.where(later, own, length)
        meta[2, tile] = first
        meta[3, tile] = length
        meta[4, tile] = ctx if tile == 0 else lax.axis_index("fsdp")
    head = ctx // 2

    def rows_of(ref, pair, half):
        block = ref[:, pl.ds(pl.multiple_of(pair * 128, 128), 128)]
        pick = (iota((HD, 128), 1) == iota((HD, 128), 0) + half * HD).astype(BF)
        return dot(pick, block, 1, 1).astype(BF)

    out[0:64, :] = rows_of(wq, ctx // 2, ctx % 2)
    out[64:128, :] = rows_of(wk, head // 2, head % 2)
    out[128:192, :] = rows_of(wv, head // 2, head % 2)
    lane = iota((1, 128), 1)
    counts = jnp.where(lane == 0, total // 64, jnp.where(lane == 1, total % 64, 0))
    key_gain = jnp.concatenate([kg[...].astype(F32), jnp.zeros((1, 64), F32)], 1)
    out[192:208, :] = jnp.concatenate(
        [
            na[...].astype(F32),
            nf[...].astype(F32),
            qg[...].astype(F32),
            key_gain,
            counts.astype(F32),
            jnp.zeros((11, 128), F32),
        ],
        0,
    ).astype(BF)
    out[208:240, :] = wr[...]
    for e in (0, 1):
        at = e * 384
        big[at : at + 128, :] = w_gate[e]
        big[at + 128 : at + 256, :] = w_up[e]
        big[at + 256 : at + 320, :] = w_down[e, :, 0:512]
        big[at + 320 : at + 384, :] = w_down[e, :, 512:1024]
    for part in range(4):
        lanes = pl.ds(pl.multiple_of((ctx % 2) * 512 + part * 128, 128), 128)
        out[ROWS_IN + part * 128 : ROWS_IN + (part + 1) * 128, :] = wo[:, lanes]


def assemble_kernel(meta, near, up, down, far, packed, w_half, qg, kg, consts):
    ctx, z = meta[4, 0], meta[4, 1] % 4
    for ref, dz in ((near, 0), (up, 3), (down, 1), (far, 2)):
        for y in (0, 1):
            at = pl.ds(pl.multiple_of((y * 4 + (z + dz) % 4) * 128, 128), 128)
            packed[:, at] = ref[y, 0:ROWS_IN]
            for part in range(4):
                first = ROWS_IN + part * 128
                w_half[at, part * 128 : (part + 1) * 128] = ref[y, first : first + 128]
    lanes = pl.ds(pl.multiple_of((ctx // 2) * 128, 128), 128)
    gains = packed[192:208, lanes].astype(F32)
    at, place = iota((HD, 128), 1), iota((HD, 128), 0)
    own = at == place + (ctx % 2) * HD
    qg[...] = jnp.sum(jnp.where(own, gains[2:3, :], 0.0), 1, keepdims=True)
    kg[...] = jnp.sum(jnp.where(at == place, gains[3:4, :], 0.0), 1, keepdims=True)
    counts = packed[192:208, :].astype(F32)[4:5, :]
    lane = iota((1, 1024), 1) % 128
    count = jnp.sum(jnp.where(lane == 0, counts * 64.0, counts), 1, keepdims=True)
    elements = count * 1024.0
    row = iota((8, 128), 0)
    consts[...] = jnp.where(row == 0, 2.0 * 8388608.0 / elements, 1.0 / elements)


def place_rows(named):
    before = (iota((128, 128), 0) < iota((128, 128), 1)).astype(BF)
    rank = jnp.where(named > 0.0, dot(named.astype(BF), before), -1.0)
    place = iota((1, CAP, 1), 1).astype(F32)
    return (rank[:, None, :] == place).astype(F32).reshape(32 * CAP, 128)


def slot_of(ctx, piece):
    dx, dy, dc = piece
    return ((ctx // 4 + dx + 4) % 4) * 4 + (((ctx // 2) % 2 + dy) % 2) * 2 + (ctx + dc) % 2


def slot_experts():
    row, first = iota((SENT, 32), 0), iota((SENT, 32), 1) * FULL
    return (row >= first) & (row < first + FULL)


def slots_kernel(routes_t, probs, out, high_out, low_out):
    expert = iota((32, 128), 0).astype(F32)
    routes = routes_t[...].astype(F32)
    named = jnp.zeros((32, 128), F32)
    for k in range(8):
        named = jnp.where(routes[k : k + 1, :] == expert, 1.0, named)
    before = (iota((128, 128), 0) < iota((128, 128), 1)).astype(BF)
    rank = jnp.where(named > 0.0, dot(named.astype(BF), before), -1.0)
    of_expert = slot_experts()
    spread = of_expert.astype(F32).astype(BF)
    first = jnp.sum(jnp.where(of_expert, iota((SENT, 32), 1) * FULL, 0), 1, keepdims=True)
    place = (iota((SENT, 1), 0) - first).astype(F32)
    match = dot(spread, rank.astype(BF)) == place
    out[...] = match.astype(F32).astype(BF)
    p = probs[...]
    p_high = p.astype(BF)
    p_rest = p - p_high.astype(F32)
    p_low = p_rest.astype(BF)
    p_last = (p_rest - p_low.astype(F32)).astype(BF)
    gate = dot(spread, p_high) + dot(spread, p_low) + dot(spread, p_last)
    high, low = split(jnp.where(match, gate, 0.0))
    high_out[...] = high
    low_out[...] = low


def project_kernel(get, put, outs):
    qkv, squares, normed = outs
    meta, packed = get(0), get(1)
    ctx = lax.axis_index("ctx")
    weight = packed[0:192, :]
    gain = packed[192:208, :].astype(F32)[0:1, :]
    for n, where in enumerate(PIECES):
        slot = slot_of(ctx, where)
        at = pl.ds(pl.multiple_of(meta[0, slot] * TILE, TILE), TILE)
        rows = get(2 + n)[...].astype(F32)
        factor = lax.rsqrt(jnp.mean(rows * rows, -1, keepdims=True) + EPS)
        low = (rows * factor * gain).astype(BF)
        normed[at, :] = low
        lin = dot(weight, low, 1, 1)
        qkv[:, at] = lin
        squares[0:1, at] = jnp.sum(lin[0:64] * lin[0:64], 0, keepdims=True)
        squares[1:2, at] = 0.5 * jnp.sum(lin[64:128] * lin[64:128], 0, keepdims=True)


def rotate(value, cos, sin):
    a, b = value[0:32], value[32:64]
    return jnp.concatenate([a * cos - b * sin, b * cos + a * sin], 0)


def diagonal_mask(meta, tile):
    room = meta[3, tile] - (tile - meta[2, tile]) * TILE
    key = iota((TILE, TILE), 0)
    return (key <= iota((TILE, TILE), 1)) & (key < room)


def strip_scores(meta, keys, query, tile, first):
    scores = dot(keys, query)
    parts = []
    for other in range(first, tile):
        shift = jnp.where(other >= meta[2, tile], 0.0, -1000000000.0)
        parts.append(scores[(other - first) * TILE : (other - first + 1) * TILE] + shift)
    parts.append(jnp.where(diagonal_mask(meta, tile), scores[-TILE:], -1000000000.0))
    return jnp.concatenate(parts, 0) if len(parts) > 1 else parts[0]


def attend_kernel(get, put, outs, v_t):
    out_low, out_full, stats, q_t, k_t, k_rows, v_rows = outs
    meta, qg, kg = get(0), get(3)[...], get(4)[...]
    routes_t, squares, cos_t, sin_t, qkv = get(7), get(2), get(5), get(6), get(1)
    for tile in range(16):
        at = slice(tile * TILE, (tile + 1) * TILE)
        base = pl.ds(pl.multiple_of((tile - meta[2, tile]) * TILE, TILE), TILE)
        cos, sin = cos_t[:, base], sin_t[:, base]
        q_factor = lax.rsqrt(squares[0:1, at] * (1.0 / 1024) + EPS)
        k_factor = lax.rsqrt(squares[1:2, at] * (1.0 / 512) + EPS)
        query = rotate(qkv[0:64, at] * q_factor * qg, cos, sin)
        key = rotate(qkv[64:128, at] * k_factor * kg, cos, sin)
        value = qkv[128:192, at]
        q_t[:, at] = (query * 0.125).astype(BF)
        k_t[:, at] = key.astype(BF)
        v_t[:, at] = value.astype(BF)
        k_rows[at, :] = key.T.astype(BF)
        v_rows[at, :] = value.T.astype(BF)

    out_low[1024:1040, :] = jnp.concatenate(
        [routes_t[...].astype(F32), jnp.zeros((8, 128), F32)], 0
    ).astype(BF)

    for tile in range(16):
        first = max(0, tile - 7)
        mine = slice(tile * TILE, (tile + 1) * TILE)
        keys = slice(first * TILE, (tile + 1) * TILE)
        scores = strip_scores(meta, k_rows[keys, :], q_t[:, mine], tile, first)
        top = jnp.max(scores, 0, keepdims=True)
        weights = jnp.exp(scores - top)
        total = jnp.sum(weights, 0, keepdims=True)
        mixed = dot(v_t[:, keys], weights.astype(BF)) / total
        out_full[:, mine] = mixed
        half = tile // 8
        rows = slice((tile % 8) * TILE, (tile % 8 + 1) * TILE)
        out_low[rows, half * HD : (half + 1) * HD] = mixed.T.astype(BF)
        stats[0:1, mine] = top
        stats[1:2, mine] = total


def attend_back_kernel(get, put, outs, gk, gv, gain_q, gain_k):
    to_tokens, gq_weighted, keep, send, dots, gains = outs
    meta, qg, kg = get(0), get(4)[...], get(5)[...]
    qkv, squares, cos_t, sin_t, out_full, stats = [get(i) for i in (2, 3, 6, 7, 8, 9)]
    q_t, k_t, k_rows, v_rows, moved = [get(i) for i in (10, 11, 12, 13, 1)]
    gk[...] = jnp.zeros_like(gk)
    gv[...] = jnp.zeros_like(gv)
    gain_q[...] = jnp.zeros_like(gain_q)
    gain_k[...] = jnp.zeros_like(gain_k)

    def turned_back(tile, value):
        base = pl.ds(pl.multiple_of((tile - meta[2, tile]) * TILE, TILE), TILE)
        return rotate(value, cos_t[:, base], -sin_t[:, base])

    for tile in range(16):
        first = max(0, tile - 7)
        mine = slice(tile * TILE, (tile + 1) * TILE)
        keys = slice(first * TILE, (tile + 1) * TILE)
        g_out = moved[pl.ds(meta[1, tile], 1), 0:64, :][0].astype(F32)
        inverse = 1.0 / stats[1:2, mine]
        g_acc = (g_out * inverse).astype(BF)
        shift = jnp.sum(g_out * out_full[:, mine], 0, keepdims=True) * inverse
        query = q_t[:, mine]
        scores = strip_scores(meta, k_rows[keys, :], query, tile, first)
        weights = jnp.exp(scores - stats[0:1, mine])
        g_weights = dot(v_rows[keys, :], g_acc)
        g_scores = (weights * (g_weights - shift)).astype(BF)
        gk[:, keys] += dot(query, g_scores, 1, 1)
        gv[:, keys] += dot(g_acc, weights.astype(BF), 1, 1)
        g_query = turned_back(tile, dot(k_t[:, keys], g_scores) * 0.125)
        factor = lax.rsqrt(squares[0:1, mine] * (1.0 / 1024) + EPS)
        q_norm = qkv[0:64, mine] * factor
        weighted = g_query * qg
        gq_weighted[:, mine] = weighted
        dots[0:1, mine] = jnp.sum(weighted * q_norm, 0, keepdims=True)
        gain_q[...] += g_query * q_norm

    odd = meta[4, 0] % 2 == 1
    for tile in range(16):
        at = slice(tile * TILE, (tile + 1) * TILE)
        g_key = turned_back(tile, gk[:, at])
        k_norm = qkv[64:128, at] * lax.rsqrt(squares[1:2, at] * (1.0 / 512) + EPS)
        weighted = g_key * kg
        dots[1:2, at] = jnp.sum(weighted * k_norm, 0, keepdims=True)
        gain_k[...] += g_key * k_norm
        g_value = gv[:, at]
        to_tokens[pl.ds(meta[1, tile], 1), :, :] = jnp.concatenate(
            [gq_weighted[:, at], weighted, g_value], 0
        ).astype(BF)[None]
        keep[:, at] = jnp.where(odd, g_value, g_key)
        send[:, at] = jnp.where(odd, g_key, g_value)
    ones = jnp.ones((8, TILE), F32)
    gains[...] = jnp.concatenate(
        [
            dot(ones, gain_q[...], 1, 1, lax.Precision.HIGHEST),
            dot(ones, gain_k[...], 1, 1, lax.Precision.HIGHEST),
        ],
        1,
    )


def out_grad_kernel(get, put, outs):
    (result,) = outs
    meta, moved = get(0), get(1)
    ctx = lax.axis_index("ctx")
    turned = jnp.concatenate(
        [
            jnp.concatenate(
                [moved[pl.ds(meta[1, tile + 8 * half], 1), 64:128, :][0] for tile in range(8)], 1
            )
            for half in (0, 1)
        ],
        0,
    )
    for i in range(8):
        lanes = pl.ds(pl.multiple_of((slot_of(ctx, PIECES[i]) // 2) * 128, 128), 128)
        parts = []
        for piece in (i, i + 8):
            both = dot(turned, get(2 + piece)[0:1024, :])
            parts.append(both[0:64, 0:64] + both[64:128, 64:128])
        mine, other = parts
        odd = ctx % 2 == 1
        result[:, lanes] = jnp.concatenate(
            [jnp.where(odd, other, mine), jnp.where(odd, mine, other)], 1
        )


def linear_grad_kernel(get, put, outs, whole):
    z = lax.axis_index("fsdp") % 4
    odd = lax.axis_index("ctx") % 2 == 1
    kg = get(6)[...]
    qkv, squares, dots, gq_weighted, keep, other = [get(i) for i in range(6)]
    lows = []
    for tile in range(16):
        at = slice(tile * TILE, (tile + 1) * TILE)
        q_factor = lax.rsqrt(squares[0:1, at] * (1.0 / 1024) + EPS)
        k_factor = lax.rsqrt(squares[1:2, at] * (1.0 / 512) + EPS)
        q_norm = qkv[0:64, at] * q_factor
        k_norm = qkv[64:128, at] * k_factor
        g_q = q_factor * (gq_weighted[:, at] - q_norm * (dots[0:1, at] * (1.0 / 1024)))
        both = keep[:, at] + other[:, at]
        g_k = k_factor * (both * kg - k_norm * (dots[1:2, at] * (1.0 / 512)))
        lows.append(jnp.concatenate([g_q, jnp.where(odd, both, g_k)], 0).astype(BF))
    whole[0:128, :] = dot(jnp.concatenate(lows, 1), get(7)[...])
    out_grad, router_grad, ffn_gain_grad, gains, loss_parts = [get(i) for i in range(8, 13)]
    lane = iota((1, 128), 1)
    tail_rows = jnp.zeros((ROWS_OUT - ROW_LOSS - 1, 128), F32)
    loss = loss_parts[0:1, :]
    whole[128:192, :] = out_grad[...]
    whole[192:224, :] = router_grad[...]
    whole[224:232, :] = jnp.where(iota((8, 1024), 0) == 0, ffn_gain_grad[...], 0.0)
    tail = jnp.concatenate([gains[0:1, :], loss, tail_rows], 0)
    for out, dz in zip(outs, (0, 1, 3, 2)):
        for y in (0, 1):
            at = pl.ds(pl.multiple_of((y * 4 + (z + dz) % 4) * 128, 128), 128)
            out[y] = jnp.concatenate([whole[0:225, at], tail], 0).astype(BF)


def loss_again(total):
    parts = jnp.sum(total[ROW_LOSS : ROW_LOSS + 1, :], 1, keepdims=True)
    first = parts.astype(BF).astype(F32)
    second = (parts - first).astype(BF).astype(F32)
    third = parts - first - second
    lane = iota(total.shape, 1)
    pieces = jnp.where(lane == 0, first, jnp.where(lane == 1, second, third))
    use = (iota(total.shape, 0) == ROW_LOSS) & (lane < 3)
    return jnp.where(use, pieces, total)


def sum_z_kernel(get, put, outs):
    keep, send = outs
    low = lax.axis_index("fsdp") < 4
    parts = [get(i)[...].astype(F32) for i in range(4)]
    total = parts[0] + parts[1] + parts[2] + parts[3]
    keep[...] = jnp.where(low, total[0], total[1])
    send[...] = loss_again(jnp.where(low, total[1], total[0])).astype(BF)


def sum_y_kernel(get, put, outs):
    total = get(0)[...] + get(1)[...].astype(F32)
    outs[0][...] = loss_again(total).astype(BF)


def own_linear_kernel(get, put, outs):
    norms, factors = outs
    hidden, packed, mine, other = [get(i) for i in range(4)]
    even = lax.axis_index("ctx") % 2 == 0
    w_q = jnp.where(even, mine[...], other[...])
    w_k = jnp.where(even, other[:, 0:512], mine[:, 0:512])
    rows = hidden[...].astype(F32)
    factor = lax.rsqrt(jnp.mean(rows * rows, -1, keepdims=True) + EPS)
    gain = packed[192:208, :].astype(F32)[0:1, :]
    low = (rows * factor * gain).astype(BF)
    q_lin = dot(low, w_q).T
    k_lin = dot(low, w_k).T
    q_factor = lax.rsqrt(jnp.mean(q_lin * q_lin, 0, keepdims=True) + EPS)
    k_factor = lax.rsqrt(jnp.mean(k_lin * k_lin, 0, keepdims=True) + EPS)
    norms[0:1024, :] = q_lin * q_factor
    norms[1024:1536, :] = k_lin * k_factor
    factors[...] = jnp.where(iota((8, 128), 0) == 0, q_factor, k_factor)


def input_grad_kernel(get, put, outs):
    (result,) = outs
    norms, factors, moved = get(0), get(1), get(2)
    q = jnp.concatenate([moved[h, 0:64, :] for h in range(16)], 0).astype(F32)

    def key_rows(at):
        pairs = [
            moved[h, at : at + 64, :].astype(F32) + moved[h + 1, at : at + 64, :].astype(F32)
            for h in range(0, 16, 2)
        ]
        return jnp.concatenate(pairs, 0)

    k, v = key_rows(64), key_rows(128)
    q_norm, k_norm = norms[0:1024, :], norms[1024:1536, :]
    g_q = factors[0:1, :] * (q - q_norm * jnp.mean(q * q_norm, 0, keepdims=True))
    g_k = factors[1:2, :] * (k - k_norm * jnp.mean(k * k_norm, 0, keepdims=True))
    g_lin = jnp.concatenate([g_q, g_k, v], 0).astype(BF)
    even = lax.axis_index("ctx") % 2 == 0
    near, far = g_lin[0:1024], g_lin[1024:2048]
    g_normed = dot(jnp.where(even, near, far), get(3)[...], 0, 1)
    g_normed += dot(jnp.where(even, far, near), get(4)[...], 0, 1)
    hidden, packed, g_resid = get(5), get(6), get(7)
    rows = hidden[...].astype(F32)
    factor = lax.rsqrt(jnp.mean(rows * rows, -1, keepdims=True) + EPS)
    n = rows * factor
    gain = packed[192:208, :].astype(F32)[0:1, :]
    weighted = g_normed * gain
    result[...] = g_resid[...] + factor * (
        weighted - n * jnp.mean(weighted * n, -1, keepdims=True)
    )


def stage(target, e, lane, values):
    for slot in range(16):
        at = (2 * slot + e) * FULL
        target[at : at + FULL, lane : lane + 512] = values[slot * CAP : slot * CAP + FULL]


def route_kernel(get, put, outs, spread, named, w_full, out_rows):
    rows, act, result, place, gates, resid_out, post_out, probs = outs[:8]
    gate_pre, up_pre = outs[8:]
    meta, packed = get(0), get(1)
    ctx = lax.axis_index("ctx")
    odd = ctx % 2 == 1
    for n in range(2, 18):
        get(n)
    first_x, first_out, first_w, experts = 18, 2, 34, 36
    for i in range(8):
        lanes = pl.ds(pl.multiple_of((slot_of(ctx, PIECES[i]) // 2) * 128, 128), 128)
        mine = get(first_out + i)[0:1024, :]
        other = get(first_out + i + 8)[0:1024, :]
        low, high = jnp.where(odd, other, mine), jnp.where(odd, mine, other)
        out_rows[0:1024, lanes] = jnp.concatenate([low[:, 0:64], high[:, 0:64]], 1)
        out_rows[1024:2048, lanes] = jnp.concatenate([low[:, 64:128], high[:, 64:128]], 1)
    for n, piece in enumerate(PIECES):
        slot = slot_of(ctx, piece)
        routes = get(first_out + n)[1024:1040, :].astype(F32)[0:8, :]
        for e in (0, 1):
            expert = (2 * ctx + e).astype(F32)
            hit = jnp.max(jnp.where(routes == expert, 1.0, 0.0), 0, keepdims=True)
            named[pl.ds(e * 16 + slot, 1), :] = hit
    place[...] = place_rows(named[...])
    xs = [get(first_x + n) for n in range(16)]
    for core in (0, 1):
        columns = pl.ds(pl.multiple_of(((ctx + core) % 2) * 512, 512), 512)
        w_full[:, columns] = get(first_w + core)[...]
    gain = packed[192:208, :].astype(F32)[1:2, :]
    router = packed[208:240, :]
    for group in range(4):
        slots = [slot_of(ctx, PIECES[group * 4 + j]) for j in range(4)]
        tiles = [pl.ds(pl.multiple_of(meta[0, slot] * TILE, TILE), TILE) for slot in slots]
        mixed = jnp.concatenate([out_rows[at, :] for at in tiles], 0)
        x = jnp.concatenate([xs[group * 4 + j][...] for j in range(4)], 0)
        resid = x.astype(F32) + dot(mixed, w_full[...])
        factor = lax.rsqrt(jnp.mean(resid * resid, -1, keepdims=True) + EPS)
        post = (resid * factor * gain).astype(BF)
        logits = dot(router, post, 1, 1)
        shifted = jnp.exp(logits - jnp.max(logits, 0, keepdims=True))
        p = shifted / jnp.sum(shifted, 0, keepdims=True)
        if group == 0:
            resid_out[...] = resid[0:TILE]
            post_out[...] = post[0:TILE]
            probs[...] = p[:, 0:TILE]
        gate = [
            jnp.sum(jnp.where(iota(p.shape, 0) == 2 * ctx + e, p, 0.0), 0, keepdims=True)
            for e in (0, 1)
        ]
        for j, slot in enumerate(slots):
            own = slice(j * TILE, (j + 1) * TILE)
            at = pl.ds(pl.multiple_of(slot * CAP, 8), CAP)
            picks = []
            for e in (0, 1):
                gates[pl.ds(e * 16 + slot, 1), :] = gate[e][:, own]
                picks.append(place[pl.ds(pl.multiple_of(e * SLOTS + slot * CAP, 8), CAP), :])
            both = dot(jnp.concatenate(picks, 0).astype(BF), post[own])
            spread[at, :] = both[0:CAP]
            spread[pl.ds(pl.multiple_of(SLOTS + slot * CAP, 8), CAP), :] = both[CAP : 2 * CAP]
    rows[...] = spread[...].astype(BF)
    for j in (3, 4, 5, 6, 7, 0):
        put(j)
    weights = get(experts)
    for e in (0, 1):
        gate_w, up_w, down_a, down_b = expert_weights(weights, e)
        x = rows[e * SLOTS : (e + 1) * SLOTS, :]
        gp, up = dot(x, gate_w), dot(x, up_w)
        gate_pre[e] = gp.astype(BF)
        up_pre[e] = up.astype(BF)
        low = (gp * jax.nn.sigmoid(gp) * up).astype(BF)
        act[e] = low
        stage(spread, e, 0, dot(low, down_a))
        stage(spread, e, 512, dot(low, down_b))
        put(8, (e,))
        put(9, (e,))
        put(1, (e,))
    result[...] = spread[0:SENT, :].astype(BF)
    put(2)


def expert_weights(ref, e):
    at = e * 384
    gate = ref[:, at : at + 128, :].reshape(1024, 512)
    up = ref[:, at + 128 : at + 256, :].reshape(1024, 512)
    down_a = ref[:, at + 256 : at + 320, :].reshape(512, 512)
    down_b = ref[:, at + 320 : at + 384, :].reshape(512, 512)
    return gate, up, down_a, down_b


def expert_back_kernel(get, put, outs, spread):
    result, g_rows, g_gate, g_up = outs
    ctx = lax.axis_index("ctx")
    place, gates = get(16), get(17)
    for n in range(16):
        get(n)
    for n, piece in enumerate(PIECES):
        slot = slot_of(ctx, piece)
        at = pl.ds(pl.multiple_of(slot * CAP, 8), CAP)
        picks, scales = [], []
        for e in (0, 1):
            pick = place[pl.ds(pl.multiple_of(e * SLOTS + slot * CAP, 8), CAP), :]
            gate = gates[pl.ds(e * 16 + slot, 1), :]
            scales.append(jnp.sum(pick * gate, 1, keepdims=True))
            picks.append(pick)
        both = dot(jnp.concatenate(picks, 0).astype(BF), get(n)[...])
        spread[at, :] = both[0:CAP] * scales[0]
        second = pl.ds(pl.multiple_of(SLOTS + slot * CAP, 8), CAP)
        spread[second, :] = both[CAP : 2 * CAP] * scales[1]
    g_rows[...] = spread[...].astype(BF)
    put(1)
    weights, gate_pre, up_pre = get(18), get(19), get(20)
    for e in (0, 1):
        gate, up, down_a, down_b = expert_weights(weights, e)
        own = slice(e * SLOTS, (e + 1) * SLOTS)
        g_act = dot(g_rows[own, 0:512], down_a, 1, 1)
        g_act += dot(g_rows[own, 512:1024], down_b, 1, 1)
        gp, up_value = gate_pre[e].astype(F32), up_pre[e].astype(F32)
        sg = jax.nn.sigmoid(gp)
        gg = (g_act * up_value * sg * (1.0 + gp * (1.0 - sg))).astype(BF)
        gu = (g_act * (gp * sg)).astype(BF)
        g_gate[e] = gg
        g_up[e] = gu
        for lane in (0, 512):
            part = dot(gg, gate[lane : lane + 512], 1, 1) + dot(gu, up[lane : lane + 512], 1, 1)
            stage(spread, e, lane, part)
    result[...] = spread[0:SENT, :].astype(BF)


def expert_weight_kernel(rows, g_rows, act, g_gate, g_up, result):
    x, g = rows[...], g_rows[...]
    result[:, 0:128, :] = dot(x, g_gate[0], 0, 0).astype(BF).reshape(8, 128, 512)
    result[:, 128:256, :] = dot(x, g_up[0], 0, 0).astype(BF).reshape(8, 128, 512)
    low = act[0]
    result[:, 256:320, :] = dot(low, g[:, 0:512], 0, 0).astype(BF).reshape(8, 64, 512)
    result[:, 320:384, :] = dot(low, g[:, 512:1024], 0, 0).astype(BF).reshape(8, 64, 512)


HALF = pl.BlockSpec((SLOTS, 1024), lambda e: (e, 0))
INNER = pl.BlockSpec((1, SLOTS, 512), lambda e: (e, 0, 0))
WEIGHTS = pl.BlockSpec((8, 384, 512), lambda e: (0, e, 0))


def expert_call(body, outs, out_specs, args, in_specs, name, flops, scratch=()):
    size = sum(int(np.prod(o.shape)) * o.dtype.itemsize for o in outs)
    size += sum(int(np.prod(a.shape)) * a.dtype.itemsize for a in args)
    return pl.pallas_call(
        body,
        grid=(2,),
        out_shape=outs,
        in_specs=in_specs,
        out_specs=out_specs,
        scratch_shapes=list(scratch),
        compiler_params=pltpu.CompilerParams(vmem_limit_bytes=58 * 2**20),
        cost_estimate=pl.CostEstimate(flops=flops, bytes_accessed=size, transcendentals=0),
        name=name,
    )(*args)


def combine_kernel(get, put, outs):
    result, g_result, g_low, loss_parts = outs
    meta, consts = get(0), get(1)
    moved, high, low, resid, teacher = [get(i) for i in range(2, 7)]
    slot = meta[4, 0]
    tile = meta[0, slot]
    room = meta[3, tile] - (tile - meta[2, tile]) * TILE
    valid = (iota((TILE, 1), 0) < room).astype(F32)
    total = resid[...] + dot(high[...], moved[...], 0, 0) + dot(low[...], moved[...], 0, 0)
    result[...] = total.astype(BF)
    errors = (total - teacher[...].astype(F32)) * valid
    g = errors * consts[0:1, 0:1]
    g_result[...] = g
    g_low[...] = g.astype(BF)
    squared = jnp.sum(jnp.sum(errors * errors, 0, keepdims=True), 1, keepdims=True)
    first = squared.astype(BF).astype(F32)
    second = (squared - first).astype(BF).astype(F32)
    third = squared - first - second
    lane = iota((8, 128), 1)
    loss_parts[...] = jnp.where(
        lane == 0, first, jnp.where(lane == 1, second, jnp.where(lane == 2, third, 0.0))
    )


def router_grad_kernel(moved, place, probs, g_result, post, g_logits, router_grad):
    p = probs[...]
    g_high, g_low = split(g_result[...])
    match = dot(moved[...], g_high, 1, 1) + dot(moved[...], g_low, 1, 1)
    picked = place[...].astype(F32) * match
    g_p = dot(slot_experts().astype(F32), picked, 0, 0, lax.Precision.HIGHEST)
    g_z = (p * (g_p - jnp.sum(p * g_p, 0, keepdims=True))).astype(BF)
    g_logits[...] = g_z
    router_grad[...] = dot(g_z, post[...])


def resid_grad_kernel(get, put, outs):
    g_resid_out, ffn_gain_grad, to_heads = outs
    moved, place, g_logits, packed, resid_in, g_result = [get(i) for i in range(6)]
    core = lax.axis_index("ctx") % 2
    g_post = dot(g_logits[...], packed[208:240, :], 0, 0)
    g_post += dot(place[...], moved[...], 0, 0)
    resid = resid_in[...]
    gain = packed[192:208, :].astype(F32)[1:2, :]
    factor = lax.rsqrt(jnp.mean(resid * resid, -1, keepdims=True) + EPS)
    n = resid * factor
    ffn_gain_grad[...] = jnp.broadcast_to(jnp.sum(g_post * n, 0, keepdims=True), (8, 1024))
    weighted = g_post * gain
    g_resid = g_result[...] + factor * (
        weighted - n * jnp.mean(weighted * n, -1, keepdims=True)
    )
    g_resid_out[...] = g_resid
    low = g_resid.astype(BF)
    near, far = low[:, 0:512], low[:, 512:1024]
    mine, other = jnp.where(core == 0, near, far), jnp.where(core == 0, far, near)
    g_mixed = (dot(get(6)[...], mine, 1, 1) + dot(get(7)[...], other, 1, 1)).astype(BF)
    turned = g_resid.T.astype(BF)
    for head in range(16):
        at = slice(head * 64, (head + 1) * 64)
        to_heads[head, 0:64, :] = g_mixed[at]
        to_heads[head, 64:128, :] = turned[at]


def final_kernel(get, put, outs, gain_rows):
    (
        grad_q, grad_k, grad_v, grad_o, router, q_gain, k_gain, ffn_gain, attn_gain, loss,
    ) = outs
    meta, consts, na = [get(i) for i in range(3)]
    odd_core = meta[4, 0] % 2 == 1
    wq, wk, wv = get(3), get(4), get(5)
    x = meta[4, 0] // 4
    shard = meta[4, 1]
    summed = jnp.zeros((ROWS_OUT - ROW_GR, 128), F32)
    for n, dx in enumerate((0, 3, 1, 2)):
        index = (x + dx) % 4
        mine, other = get(6 + n)[...].astype(F32), get(10 + n)[...].astype(F32)
        low, high = jnp.where(odd_core, other, mine), jnp.where(odd_core, mine, other)
        blocks = jnp.stack([low[0], high[0], low[1], high[1]])
        wide = pl.ds(pl.multiple_of(index * 256, 256), 256)
        slim = pl.ds(pl.multiple_of(index * 128, 128), 128)
        grad_q[:, wide] = blocks[:, 0:64, :].reshape(256, 128).T
        grad_o[:, wide] = blocks[:, 128:192, :].reshape(256, 128).T
        grad_k[:, slim] = jnp.concatenate([blocks[0, 64:128], blocks[2, 64:128]], 0).T
        grad_v[:, slim] = jnp.concatenate([blocks[1, 64:128], blocks[3, 64:128]], 0).T
        tails = blocks[:, ROW_GR:, :]
        summed += tails[0] + tails[1] + tails[2] + tails[3]
        for j in range(4):
            gain_rows[pl.ds(index * 4 + j, 1), :] = tails[j, 33:34, :]
    router[...] = summed[0:32]
    even = gain_rows[pl.ds(2 * shard, 1), :]
    odd = gain_rows[pl.ds(2 * shard + 1, 1), :]
    q_gain[...] = jnp.concatenate([even[:, 0:64], odd[:, 0:64]], 1)
    k_gain[...] = (even + odd)[:, 64:128]
    ffn_gain[...] = summed[32:33]
    folded = (
        jnp.sum(grad_q[...] * wq[...].astype(F32), 1, keepdims=True)
        + jnp.sum(grad_k[...] * wk[...].astype(F32), 1, keepdims=True)
        + jnp.sum(grad_v[...] * wv[...].astype(F32), 1, keepdims=True)
    )
    attn_gain[...] = jnp.broadcast_to(folded, (128, 128)).T[0:1, :] / na[...].astype(F32)
    loss[...] = jnp.sum(summed[34:35, :], 1, keepdims=True) * consts[1:2, 0:1]


def unpack_kernel(get, put, outs):
    grad_gate, grad_up, grad_down = outs
    shard = get(0)
    for e in (0, 1):
        at = e * 384
        grad_gate[e] = shard[at : at + 128, :].astype(F32)
        grad_up[e] = shard[at + 128 : at + 256, :].astype(F32)
        grad_down[e, :, 0:512] = shard[at + 256 : at + 320, :].astype(F32)
        grad_down[e, :, 512:1024] = shard[at + 320 : at + 384, :].astype(F32)


def gather_rows(rows, y_again=True):
    across = ctx_move(rows, YHI)
    up, down = ctx_move(rows, XUP), ctx_move(rows, XDOWN)
    across_up = ctx_move(up, YHI) if y_again else ctx_move(across, XUP)
    across_down = ctx_move(across, XDOWN)
    far, across_far = ctx_move(up, XUP), ctx_move(across_down, XDOWN)
    mine = [rows, across, up, down, across_up, across_down, far, across_far]
    return mine + [ctx_move(piece, CORE) for piece in mine]


def sum_ctx(value, beside=()):
    value = value + ctx_move(value, CORE)
    moved, *beside = lax.optimization_barrier((ctx_move(value, YHI), *beside))
    value = value + moved
    up, down, far = ctx_move(value, XUP), ctx_move(value, XDOWN), ctx_move(value, XTWO)
    return value + up + down + far, *beside


def exchange(value, axis):
    return lax.all_to_all(value, axis, split_axis=0, concat_axis=0, tiled=True)


def on_device(
    hidden,
    teacher,
    lengths,
    tile_perm,
    routes,
    norm_attn,
    w_query,
    w_key,
    w_value,
    w_out,
    q_gain,
    k_gain,
    norm_ffn,
    w_router,
    w_gate,
    w_up,
    w_down,
):
    ctx = lax.axis_index("ctx")
    shard = lax.axis_index("fsdp")
    x_in = hidden[0]
    block, expert_block, meta = kernel_call(
        pack_kernel,
        [
            shape((ROWS_IN + 512, 128), BF),
            shape((768, 512), BF),
            shape((5, 16), jnp.int32),
        ],
        [
            lengths, tile_perm, w_query, w_key, w_value, w_router.T,
            norm_attn.reshape(1, 128), norm_ffn.reshape(1, 128),
            q_gain.reshape(1, 128), k_gain.reshape(1, 64),
            w_out, w_gate, w_up, w_down,
        ],
        smem=(0, 1),
        smem_out=(2,),
        name="pack",
    )
    x_first, block = lax.optimization_barrier((x_in, block))
    pieces = gather_rows(x_first)
    other = fsdp_move(block, YLO)
    first = shard < 4
    pair = jnp.stack([jnp.where(first, block, other), jnp.where(first, other, block)])
    pair_moves = [fsdp_move(pair, ZUP), fsdp_move(pair, ZDOWN)]
    pair_moves.append(fsdp_move(pair_moves[0], ZUP))
    *pair_moves, pieces[3], pieces[7] = lax.optimization_barrier(
        (*pair_moves, pieces[3], pieces[7])
    )
    packed, w_mine, qg, kg, consts = kernel_call(
        assemble_kernel,
        [
            shape((ROWS_IN, 1024), BF),
            shape((1024, 512), BF),
            shape((HD, 1), F32),
            shape((HD, 1), F32),
            shape((8, 128), F32),
        ],
        [meta, pair] + pair_moves,
        smem=(0,),
        name="assemble",
    )
    w_other = ctx_move(w_mine, CORE)
    frequencies = 10000.0 ** (-jnp.arange(32, dtype=F32) / 32)
    angles = frequencies[:, None] * jnp.arange(1024, dtype=F32)[None, :]
    cos_t, sin_t = jnp.cos(angles), jnp.sin(angles)
    routes_t = routes[0].T.astype(BF)

    expert_block, *_ = lax.optimization_barrier((expert_block, packed, *pieces[4:8]))
    experts = lax.all_gather(expert_block, "fsdp", axis=0)
    qkv, squares, normed = streamed_call(
        project_kernel,
        [shape((192, 2048), F32), shape((2, 2048), F32), shape((2048, 1024), BF)],
        [meta, packed] + pieces,
        smem=(0,),
        name="project",
        flops=2 * 2048 * 1024 * 192,
    )
    (squares,) = sum_ctx(squares)
    mixed_low, mixed_full, stats, q_t, k_t, k_rows, v_rows = streamed_call(
        attend_kernel,
        [
            shape((1040, 128), BF),
            shape((64, 2048), F32),
            shape((2, 2048), F32),
            shape((64, 2048), BF),
            shape((64, 2048), BF),
            shape((2048, 64), BF),
            shape((2048, 64), BF),
        ],
        [meta, qkv, squares, qg, kg, cos_t, sin_t, routes_t],
        smem=(0,),
        scratch=[pltpu.VMEM((64, 2048), BF)],
        name="attend",
        flops=54 * 4 * 128 * 128 * 64,
    )
    even = ctx % 2 == 0
    qkv_half = jnp.where(even, w_query, jnp.concatenate([w_key, w_value], 1))
    qkv_half, mixed_low = lax.optimization_barrier((qkv_half, mixed_low))
    qkv_mine = lax.all_gather(qkv_half, "fsdp", axis=0, tiled=True)
    mixed_pieces = gather_rows(mixed_low, False)
    (
        rows, act, expert_out, place_here, gates, resid, post, probs, gate_pre, up_pre,
    ) = streamed_call(
        route_kernel,
        [
            shape((2 * SLOTS, 1024), BF),
            shape((2, SLOTS, 512), BF),
            shape((SENT, 1024), BF),
            shape((2 * SLOTS, 128), F32),
            shape((32, 128), F32),
            shape((128, 1024), F32),
            shape((128, 1024), BF),
            shape((32, 128), F32),
            shape((2, SLOTS, 512), BF),
            shape((2, SLOTS, 512), BF),
        ],
        [meta, packed] + mixed_pieces + pieces + [w_mine, w_other, experts],
        smem=(0,),
        stream=range(2, 37),
        stream_out=range(10),
        scratch=[
            pltpu.VMEM((2 * SLOTS, 1024), F32),
            pltpu.VMEM((32, 128), F32),
            pltpu.VMEM((1024, 1024), BF),
            pltpu.VMEM((2048, 1024), BF),
        ],
        name="route_experts",
        flops=2 * 2048 * 1024 * 1024 + 2 * 2 * SLOTS * 1024 * 1536,
    )
    returned = exchange(expert_out, "ctx")
    returned, qkv_mine = lax.optimization_barrier((returned, qkv_mine))
    qkv_other = ctx_move(qkv_mine, CORE)
    place, gate_high, gate_low = kernel_call(
        slots_kernel, [shape((SENT, 128), BF)] * 3, [routes_t, probs], name="slots"
    )
    result, g_result, g_low, loss_parts = streamed_call(
        combine_kernel,
        [
            shape((128, 1024), BF),
            shape((128, 1024), F32),
            shape((128, 1024), BF),
            shape((8, 128), F32),
        ],
        [meta, consts, returned, gate_high, gate_low, resid, teacher[0]],
        smem=(0,),
        stream=range(2, 7),
        name="combine",
        flops=2 * SLOTS * 128 * 1024 * 4,
    )
    g_pieces = gather_rows(g_low)
    g_logits, router_grad = kernel_call(
        router_grad_kernel,
        [shape((32, 128), BF), shape((32, 1024), F32)],
        [returned, place, probs, g_result, post],
        name="router_grad",
        brief=True,
    )
    g_rows, g_slots, g_gate, g_up = streamed_call(
        expert_back_kernel,
        [
            shape((SENT, 1024), BF),
            shape((2 * SLOTS, 1024), BF),
            shape((2, SLOTS, 512), BF),
            shape((2, SLOTS, 512), BF),
        ],
        g_pieces + [place_here, gates, experts, gate_pre, up_pre],
        stream=range(21),
        stream_out=range(4),
        scratch=[pltpu.VMEM((2 * SLOTS, 1024), F32)],
        name="experts_back",
        flops=2 * 2 * SLOTS * 1024 * 1536,
    )
    g_returned = exchange(g_rows, "ctx")
    (expert_grads,) = expert_call(
        expert_weight_kernel,
        [shape((8, 768, 512), BF)],
        [WEIGHTS],
        [rows, g_slots, act, g_gate, g_up],
        [HALF, HALF, INNER, INNER, INNER],
        "experts_weights",
        2 * 2 * SLOTS * 1024 * 1536,
    )
    expert_shard = lax.psum_scatter(
        expert_grads.reshape(8 * 768, 512), "fsdp", scatter_dimension=0, tiled=True
    )

    grad_gate, grad_up, grad_down = streamed_call(
        unpack_kernel,
        [shape((2, 128, 512), F32), shape((2, 128, 512), F32), shape((2, 64, 1024), F32)],
        [expert_shard],
        name="unpack",
    )
    g_resid, ffn_gain_grad, to_heads = streamed_call(
        resid_grad_kernel,
        [shape((128, 1024), F32), shape((8, 1024), F32), shape((16, 128, 128), BF)],
        [g_returned, place, g_logits, packed, resid, g_result, w_mine, w_other],
        stream=(0, 1, 4, 5, 6, 7),
        name="resid_grad",
        flops=2 * 128 * 1024 * 2400,
    )
    norms, factors = streamed_call(
        own_linear_kernel,
        [shape((1536, 128), F32), shape((8, 128), F32)],
        [x_in, packed, qkv_mine, qkv_other],
        name="own_linear",
    )
    to_heads, norms, factors = lax.optimization_barrier((to_heads, norms, factors))
    moved = exchange(to_heads.reshape(2048, 128), "ctx").reshape(16, 128, 128)
    to_tokens, gq_weighted, keep, send, dots, gains = streamed_call(
        attend_back_kernel,
        [
            shape((16, 192, 128), BF),
            shape((64, 2048), F32),
            shape((64, 2048), F32),
            shape((64, 2048), F32),
            shape((2, 2048), F32),
            shape((8, 128), F32),
        ],
        [
            meta, moved, qkv, squares, qg, kg, cos_t, sin_t,
            mixed_full, stats, q_t, k_t, k_rows, v_rows,
        ],
        smem=(0,),
        scratch=[
            pltpu.VMEM((64, 2048), F32),
            pltpu.VMEM((64, 2048), F32),
            pltpu.VMEM((64, 128), F32),
            pltpu.VMEM((64, 128), F32),
        ],
        name="attend_back",
        limit=20,
        flops=10**11,
    )
    (out_grad,) = streamed_call(
        out_grad_kernel,
        [shape((64, 1024), F32)],
        [meta, moved] + mixed_pieces,
        smem=(0,),
        name="out_grad",
        limit=20,
        flops=2 * 2048 * 64 * 1024,
    )
    dots, out_grad, received = sum_ctx(dots, (out_grad, ctx_move(send, CORE)))
    to_tokens, dots = lax.optimization_barrier((to_tokens, dots))
    g_lin = exchange(to_tokens.reshape(16 * 192, 128), "ctx").reshape(16, 192, 128)
    scattered = streamed_call(
        linear_grad_kernel,
        [shape((2, ROWS_OUT, 128), BF)] * 4,
        [
            qkv, squares, dots, gq_weighted, keep, received, kg, normed,
            out_grad, router_grad, ffn_gain_grad, gains, loss_parts,
        ],
        stream=(7,),
        scratch=[pltpu.VMEM((232, 1024), F32)],
        name="linear_grad",
        limit=24,
        flops=2 * 2048 * 128 * 1024,
    )
    came = [fsdp_move(part, pairs) for part, pairs in zip(scattered[1:], (ZUP, ZDOWN, ZTWO))]
    keep_z, send_z = streamed_call(
        sum_z_kernel,
        [shape((ROWS_OUT, 128), F32), shape((ROWS_OUT, 128), BF)],
        [scattered[0]] + came,
        name="sum_z",
        limit=8,
    )
    send_z, g_lin = lax.optimization_barrier((send_z, g_lin))
    came_y = fsdp_move(send_z, YLO)
    (summed,) = streamed_call(
        sum_y_kernel,
        [shape((ROWS_OUT, 128), BF)],
        [keep_z, came_y],
        name="sum_y",
        limit=8,
    )
    across = ctx_move(summed, YHI)
    low_y = (ctx // 2) % 2 == 0
    both = jnp.stack([jnp.where(low_y, summed, across), jnp.where(low_y, across, summed)])
    shares = [both] + [ctx_move(both, pairs) for pairs in (XUP, XDOWN, XTWO)]
    (input_grad,) = streamed_call(
        input_grad_kernel,
        [shape((128, 1024), F32)],
        [norms, factors, g_lin, qkv_mine, qkv_other, x_in, packed, g_resid],
        stream=(3, 4),
        name="input_grad",
        flops=2 * 128 * 2048 * 1024,
    )
    *shares, input_grad, grad_gate, grad_up, grad_down = lax.optimization_barrier(
        (*shares, input_grad, grad_gate, grad_up, grad_down)
    )
    shares += [ctx_move(share, CORE) for share in shares]
    (
        grad_q, grad_k, grad_v, grad_o, router, q_gain_grad, k_gain_grad, ffn_gain, attn_gain,
        loss,
    ) = streamed_call(
        final_kernel,
        [
            shape((128, 1024), F32),
            shape((128, 512), F32),
            shape((128, 512), F32),
            shape((128, 1024), F32),
            shape((32, 128), F32),
            shape((1, 128), F32),
            shape((1, 64), F32),
            shape((1, 128), F32),
            shape((1, 128), F32),
            shape((1, 1), F32),
        ],
        [
            meta, consts, norm_attn.reshape(1, 128), w_query, w_key, w_value,
        ]
        + shares,
        smem=(0,),
        scratch=[pltpu.VMEM((16, 128), F32)],
        name="final",
        limit=16,
    )
    return (
        result[None],
        loss.reshape(()),
        input_grad[None],
        attn_gain.reshape(128),
        grad_q,
        grad_k,
        grad_v,
        grad_o,
        q_gain_grad.reshape(128),
        k_gain_grad.reshape(64),
        ffn_gain.reshape(128),
        router.T,
        grad_gate,
        grad_up,
        grad_down,
    )


def solution(mesh):
    return jax.shard_map(
        on_device,
        mesh=mesh,
        in_specs=(
            P("fsdp", "ctx", None),
            P("fsdp", "ctx", None),
            P("fsdp", None),
            P("fsdp", None),
            P("fsdp", "ctx", None),
            P("fsdp"),
            P("fsdp", None),
            P("fsdp", None),
            P("fsdp", None),
            P("fsdp", None),
            P("fsdp"),
            P("fsdp"),
            P("fsdp"),
            P("fsdp", None),
            P("ctx", "fsdp", None),
            P("ctx", "fsdp", None),
            P("ctx", "fsdp", None),
        ),
        out_specs=(
            P("fsdp", "ctx", None),
            P(),
            P("fsdp", "ctx", None),
            P("fsdp"),
            P("fsdp", None),
            P("fsdp", None),
            P("fsdp", None),
            P("fsdp", None),
            P("fsdp"),
            P("fsdp"),
            P("fsdp"),
            P("fsdp", None),
            P("ctx", "fsdp", None),
            P("ctx", "fsdp", None),
            P("ctx", "fsdp", None),
        ),
        check_vma=False,
    )
```

```python
import functools

import jax
import jax.numpy as jnp
import numpy as np
from jax import lax
from jax.experimental import pallas as pl
from jax.experimental.pallas import tpu as pltpu
from jax.sharding import PartitionSpec as P

TILE = 128
HD = 64
FULL = 36
CAP = 40
SLOTS = 16 * CAP
SENT = 32 * FULL
EPS = 1e-05
F32 = jnp.float32
BF = jnp.bfloat16

ROW_GAIN = 192
ROW_ROUTER = 208
ROWS_IN = 240
ROW_OUT = 128
ROW_GR = 192
ROW_NF = 224
ROW_LOSS = 226
ROWS_OUT = 240

CORE = [(i, i ^ 1) for i in range(16)]
YHI = [(i, i ^ 2) for i in range(16)]
XUP = [(i, (i + 4) % 16) for i in range(16)]
XDOWN = [(i, (i - 4) % 16) for i in range(16)]
XTWO = [(i, (i + 8) % 16) for i in range(16)]
YLO = [(i, i ^ 4) for i in range(8)]
ZUP = [(i, (i // 4) * 4 + (i + 1) % 4) for i in range(8)]
ZDOWN = [(i, (i // 4) * 4 + (i - 1) % 4) for i in range(8)]
ZTWO = [(i, (i // 4) * 4 + (i + 2) % 4) for i in range(8)]
PIECES = [
    (dx, dy, dc)
    for dc in (0, 1)
    for dx, dy in ((0, 0), (0, 1), (-1, 0), (1, 0), (-1, 1), (1, 1), (2, 0), (2, 1))
]


def ctx_move(value, pairs):
    return lax.ppermute(value, "ctx", pairs)


def fsdp_move(value, pairs):
    return lax.ppermute(value, "fsdp", pairs)


def dims(left, right):
    return (((left,), (right,)), ((), ()))


def dot(a, b, left=1, right=0, precision=None):
    return lax.dot_general(
        a, b, dims(left, right), preferred_element_type=F32, precision=precision
    )


def split(value):
    high = value.astype(BF)
    return high, (value - high.astype(F32)).astype(BF)


def iota(shape, axis):
    return lax.broadcasted_iota(jnp.int32, shape, axis)


def kernel_call(
    body, outs, args, smem=(), smem_out=(), anywhere=(), scratch=(), name=None, flops=0, brief=False
):
    specs = [
        pl.BlockSpec(
            memory_space=pltpu.SMEM if i in smem else pl.ANY if i in anywhere else pltpu.VMEM
        )
        for i in range(len(args))
    ]
    size = sum(int(np.prod(o.shape)) * o.dtype.itemsize for o in outs)
    size += sum(int(np.prod(a.shape)) * a.dtype.itemsize for a in args)
    if brief:
        size = 0
    return pl.pallas_call(
        body,
        out_shape=outs,
        in_specs=specs,
        out_specs=[
            pl.BlockSpec(memory_space=pltpu.SMEM if i in smem_out else pltpu.VMEM)
            for i in range(len(outs))
        ],
        scratch_shapes=list(scratch),
        compiler_params=pltpu.CompilerParams(
            vmem_limit_bytes=58 * 2**20
        ),
        cost_estimate=pl.CostEstimate(flops=flops, bytes_accessed=size, transcendentals=0),
        name=name,
    )(*args)


def streamed_call(
    body, outs, args, smem=(), stream=(), stream_out=(), scratch=(), name=None, flops=0, limit=58
):
    count, results = len(args), len(outs)
    moved, pushed = list(stream), list(stream_out)
    auto = [i for i in range(count) if i not in smem and i not in moved]
    auto_out = [j for j in range(results) if j not in pushed]
    puts = 40

    def kernel(*refs):
        ins, targets = refs[:count], refs[count : count + results]
        rest = refs[count + results :]
        held = dict(zip(moved, rest[: len(moved)]))
        staged = list(targets)
        for j, ref in zip(pushed, rest[len(moved) : len(moved) + len(pushed)]):
            staged[j] = ref
        own = rest[len(moved) + len(pushed) : -2]
        in_sems, out_sems = rest[-2:]
        copies = {}
        for n, i in enumerate(moved):
            copies[i] = pltpu.make_async_copy(ins[i], held[i], in_sems.at[n])
            copies[i].start()
        arrived, sent, started = set(), [], set()

        def get(i):
            if i not in copies:
                return ins[i]
            if i not in arrived:
                copies[i].wait()
                arrived.add(i)
            return held[i]

        def put(j, index=None):
            source = staged[j] if index is None else staged[j].at[index]
            target = targets[j] if index is None else targets[j].at[index]
            copy = pltpu.make_async_copy(source, target, out_sems.at[len(sent)])
            copy.start()
            sent.append(copy)
            started.add(j)

        body(get, put, staged, *own)
        for i in moved:
            get(i)
        for j in pushed:
            if j not in started:
                put(j)
        for copy in sent:
            copy.wait()

    specs = [
        pl.BlockSpec(
            memory_space=pltpu.SMEM if i in smem else pltpu.VMEM if i in auto else pltpu.HBM
        )
        for i in range(count)
    ]
    size = sum(int(np.prod(o.shape)) * o.dtype.itemsize for o in outs)
    size += sum(int(np.prod(a.shape)) * a.dtype.itemsize for a in args)
    buffers = [pltpu.VMEM(args[i].shape, args[i].dtype) for i in moved]
    buffers += [pltpu.VMEM(outs[j].shape, outs[j].dtype) for j in pushed]
    return pl.pallas_call(
        kernel,
        out_shape=outs,
        in_specs=specs,
        out_specs=[
            pl.BlockSpec(memory_space=pltpu.VMEM if j in auto_out else pltpu.HBM)
            for j in range(results)
        ],
        scratch_shapes=buffers
        + list(scratch)
        + [pltpu.SemaphoreType.DMA((max(1, len(moved)),)), pltpu.SemaphoreType.DMA((puts,))],
        compiler_params=pltpu.CompilerParams(vmem_limit_bytes=limit * 2**20),
        cost_estimate=pl.CostEstimate(flops=flops, bytes_accessed=size, transcendentals=0),
        name=name,
    )(*args)


def shape(dims_, dtype):
    return jax.ShapeDtypeStruct(dims_, dtype)


def pack_kernel(
    lens, perm, wq, wk, wv, wr, na, nf, qg, kg, wo, w_gate, w_up, w_down, out, big, meta
):
    ctx = lax.axis_index("ctx")
    for tile in range(16):
        meta[0, tile] = perm[0, tile]
        meta[1, perm[0, tile]] = tile
    start = jnp.int32(0)
    total = jnp.int32(0)
    begins = []
    for seq in range(5):
        length = lens[0, seq]
        begins.append((start, length))
        start = start + (length + TILE - 1) // TILE
        total = total + length
    for tile in range(16):
        first, length = begins[0]
        for begin, own in begins[1:]:
            later = tile >= begin
            first = jnp.where(later, begin, first)
            length = jnp.where(later, own, length)
        meta[2, tile] = first
        meta[3, tile] = length
        meta[4, tile] = ctx if tile == 0 else lax.axis_index("fsdp")
    head = ctx // 2

    def rows_of(ref, pair, half):
        block = ref[:, pl.ds(pl.multiple_of(pair * 128, 128), 128)]
        pick = (iota((HD, 128), 1) == iota((HD, 128), 0) + half * HD).astype(BF)
        return dot(pick, block, 1, 1).astype(BF)

    out[0:64, :] = rows_of(wq, ctx // 2, ctx % 2)
    out[64:128, :] = rows_of(wk, head // 2, head % 2)
    out[128:192, :] = rows_of(wv, head // 2, head % 2)
    lane = iota((1, 128), 1)
    counts = jnp.where(lane == 0, total // 64, jnp.where(lane == 1, total % 64, 0))
    key_gain = jnp.concatenate([kg[...].astype(F32), jnp.zeros((1, 64), F32)], 1)
    out[192:208, :] = jnp.concatenate(
        [
            na[...].astype(F32),
            nf[...].astype(F32),
            qg[...].astype(F32),
            key_gain,
            counts.astype(F32),
            jnp.zeros((11, 128), F32),
        ],
        0,
    ).astype(BF)
    out[208:240, :] = wr[...]
    for e in (0, 1):
        at = e * 384
        big[at : at + 128, :] = w_gate[e]
        big[at + 128 : at + 256, :] = w_up[e]
        big[at + 256 : at + 320, :] = w_down[e, :, 0:512]
        big[at + 320 : at + 384, :] = w_down[e, :, 512:1024]
    for part in range(4):
        lanes = pl.ds(pl.multiple_of((ctx % 2) * 512 + part * 128, 128), 128)
        out[ROWS_IN + part * 128 : ROWS_IN + (part + 1) * 128, :] = wo[:, lanes]


def assemble_kernel(meta, near, up, down, far, packed, w_half, qg, kg, consts):
    ctx, z = meta[4, 0], meta[4, 1] % 4
    for ref, dz in ((near, 0), (up, 3), (down, 1), (far, 2)):
        for y in (0, 1):
            at = pl.ds(pl.multiple_of((y * 4 + (z + dz) % 4) * 128, 128), 128)
            packed[:, at] = ref[y, 0:ROWS_IN]
            for part in range(4):
                first = ROWS_IN + part * 128
                w_half[at, part * 128 : (part + 1) * 128] = ref[y, first : first + 128]
    lanes = pl.ds(pl.multiple_of((ctx // 2) * 128, 128), 128)
    gains = packed[192:208, lanes].astype(F32)
    at, place = iota((HD, 128), 1), iota((HD, 128), 0)
    own = at == place + (ctx % 2) * HD
    qg[...] = jnp.sum(jnp.where(own, gains[2:3, :], 0.0), 1, keepdims=True)
    kg[...] = jnp.sum(jnp.where(at == place, gains[3:4, :], 0.0), 1, keepdims=True)
    counts = packed[192:208, :].astype(F32)[4:5, :]
    lane = iota((1, 1024), 1) % 128
    count = jnp.sum(jnp.where(lane == 0, counts * 64.0, counts), 1, keepdims=True)
    elements = count * 1024.0
    row = iota((8, 128), 0)
    consts[...] = jnp.where(row == 0, 2.0 * 8388608.0 / elements, 1.0 / elements)


def place_rows(named):
    before = (iota((128, 128), 0) < iota((128, 128), 1)).astype(BF)
    rank = jnp.where(named > 0.0, dot(named.astype(BF), before), -1.0)
    place = iota((1, CAP, 1), 1).astype(F32)
    return (rank[:, None, :] == place).astype(F32).reshape(32 * CAP, 128)


def slot_of(ctx, piece):
    dx, dy, dc = piece
    return ((ctx // 4 + dx + 4) % 4) * 4 + (((ctx // 2) % 2 + dy) % 2) * 2 + (ctx + dc) % 2


def slot_experts():
    row, first = iota((SENT, 32), 0), iota((SENT, 32), 1) * FULL
    return (row >= first) & (row < first + FULL)


def slots_kernel(routes_t, probs, out, high_out, low_out):
    expert = iota((32, 128), 0).astype(F32)
    routes = routes_t[...].astype(F32)
    named = jnp.zeros((32, 128), F32)
    for k in range(8):
        named = jnp.where(routes[k : k + 1, :] == expert, 1.0, named)
    before = (iota((128, 128), 0) < iota((128, 128), 1)).astype(BF)
    rank = jnp.where(named > 0.0, dot(named.astype(BF), before), -1.0)
    of_expert = slot_experts()
    spread = of_expert.astype(F32).astype(BF)
    first = jnp.sum(jnp.where(of_expert, iota((SENT, 32), 1) * FULL, 0), 1, keepdims=True)
    place = (iota((SENT, 1), 0) - first).astype(F32)
    match = dot(spread, rank.astype(BF)) == place
    out[...] = match.astype(F32).astype(BF)
    p = probs[...]
    p_high = p.astype(BF)
    p_rest = p - p_high.astype(F32)
    p_low = p_rest.astype(BF)
    p_last = (p_rest - p_low.astype(F32)).astype(BF)
    gate = dot(spread, p_high) + dot(spread, p_low) + dot(spread, p_last)
    high, low = split(jnp.where(match, gate, 0.0))
    high_out[...] = high
    low_out[...] = low


def project_kernel(get, put, outs):
    qkv, squares, normed = outs
    meta, packed = get(0), get(1)
    ctx = lax.axis_index("ctx")
    weight = packed[0:192, :]
    gain = packed[192:208, :].astype(F32)[0:1, :]
    for n, where in enumerate(PIECES):
        slot = slot_of(ctx, where)
        at = pl.ds(pl.multiple_of(meta[0, slot] * TILE, TILE), TILE)
        rows = get(2 + n)[...].astype(F32)
        factor = lax.rsqrt(jnp.mean(rows * rows, -1, keepdims=True) + EPS)
        low = (rows * factor * gain).astype(BF)
        normed[at, :] = low
        lin = dot(weight, low, 1, 1)
        qkv[:, at] = lin
        squares[0:1, at] = jnp.sum(lin[0:64] * lin[0:64], 0, keepdims=True)
        squares[1:2, at] = 0.5 * jnp.sum(lin[64:128] * lin[64:128], 0, keepdims=True)


def rotate(value, cos, sin):
    a, b = value[0:32], value[32:64]
    return jnp.concatenate([a * cos - b * sin, b * cos + a * sin], 0)


def diagonal_mask(meta, tile):
    room = meta[3, tile] - (tile - meta[2, tile]) * TILE
    key = iota((TILE, TILE), 0)
    return (key <= iota((TILE, TILE), 1)) & (key < room)


def strip_scores(meta, keys, query, tile, first):
    scores = dot(keys, query)
    parts = []
    for other in range(first, tile):
        shift = jnp.where(other >= meta[2, tile], 0.0, -1000000000.0)
        parts.append(scores[(other - first) * TILE : (other - first + 1) * TILE] + shift)
    parts.append(jnp.where(diagonal_mask(meta, tile), scores[-TILE:], -1000000000.0))
    return jnp.concatenate(parts, 0) if len(parts) > 1 else parts[0]


def attend_kernel(get, put, outs, v_t):
    out_low, out_full, stats, q_t, k_t, k_rows, v_rows = outs
    meta, qg, kg = get(0), get(3)[...], get(4)[...]
    routes_t, squares, cos_t, sin_t, qkv = get(7), get(2), get(5), get(6), get(1)
    for tile in range(16):
        at = slice(tile * TILE, (tile + 1) * TILE)
        base = pl.ds(pl.multiple_of((tile - meta[2, tile]) * TILE, TILE), TILE)
        cos, sin = cos_t[:, base], sin_t[:, base]
        q_factor = lax.rsqrt(squares[0:1, at] * (1.0 / 1024) + EPS)
        k_factor = lax.rsqrt(squares[1:2, at] * (1.0 / 512) + EPS)
        query = rotate(qkv[0:64, at] * q_factor * qg, cos, sin)
        key = rotate(qkv[64:128, at] * k_factor * kg, cos, sin)
        value = qkv[128:192, at]
        q_t[:, at] = (query * 0.125).astype(BF)
        k_t[:, at] = key.astype(BF)
        v_t[:, at] = value.astype(BF)
        k_rows[at, :] = key.T.astype(BF)
        v_rows[at, :] = value.T.astype(BF)

    out_low[1024:1040, :] = jnp.concatenate(
        [routes_t[...].astype(F32), jnp.zeros((8, 128), F32)], 0
    ).astype(BF)

    for tile in range(16):
        first = max(0, tile - 7)
        mine = slice(tile * TILE, (tile + 1) * TILE)
        keys = slice(first * TILE, (tile + 1) * TILE)
        scores = strip_scores(meta, k_rows[keys, :], q_t[:, mine], tile, first)
        top = jnp.max(scores, 0, keepdims=True)
        weights = jnp.exp(scores - top)
        total = jnp.sum(weights, 0, keepdims=True)
        mixed = dot(v_t[:, keys], weights.astype(BF)) / total
        out_full[:, mine] = mixed
        half = tile // 8
        rows = slice((tile % 8) * TILE, (tile % 8 + 1) * TILE)
        out_low[rows, half * HD : (half + 1) * HD] = mixed.T.astype(BF)
        stats[0:1, mine] = top
        stats[1:2, mine] = total


def attend_back_kernel(get, put, outs, gk, gv, gain_q, gain_k):
    to_tokens, gq_weighted, keep, send, dots, gains = outs
    meta, qg, kg = get(0), get(4)[...], get(5)[...]
    qkv, squares, cos_t, sin_t, out_full, stats = [get(i) for i in (2, 3, 6, 7, 8, 9)]
    q_t, k_t, k_rows, v_rows, moved = [get(i) for i in (10, 11, 12, 13, 1)]
    gk[...] = jnp.zeros_like(gk)
    gv[...] = jnp.zeros_like(gv)
    gain_q[...] = jnp.zeros_like(gain_q)
    gain_k[...] = jnp.zeros_like(gain_k)

    def turned_back(tile, value):
        base = pl.ds(pl.multiple_of((tile - meta[2, tile]) * TILE, TILE), TILE)
        return rotate(value, cos_t[:, base], -sin_t[:, base])

    for tile in range(16):
        first = max(0, tile - 7)
        mine = slice(tile * TILE, (tile + 1) * TILE)
        keys = slice(first * TILE, (tile + 1) * TILE)
        g_out = moved[pl.ds(meta[1, tile], 1), 0:64, :][0].astype(F32)
        inverse = 1.0 / stats[1:2, mine]
        g_acc = (g_out * inverse).astype(BF)
        shift = jnp.sum(g_out * out_full[:, mine], 0, keepdims=True) * inverse
        query = q_t[:, mine]
        scores = strip_scores(meta, k_rows[keys, :], query, tile, first)
        weights = jnp.exp(scores - stats[0:1, mine])
        g_weights = dot(v_rows[keys, :], g_acc)
        g_scores = (weights * (g_weights - shift)).astype(BF)
        gk[:, keys] += dot(query, g_scores, 1, 1)
        gv[:, keys] += dot(g_acc, weights.astype(BF), 1, 1)
        g_query = turned_back(tile, dot(k_t[:, keys], g_scores) * 0.125)
        factor = lax.rsqrt(squares[0:1, mine] * (1.0 / 1024) + EPS)
        q_norm = qkv[0:64, mine] * factor
        weighted = g_query * qg
        gq_weighted[:, mine] = weighted
        dots[0:1, mine] = jnp.sum(weighted * q_norm, 0, keepdims=True)
        gain_q[...] += g_query * q_norm

    odd = meta[4, 0] % 2 == 1
    for tile in range(16):
        at = slice(tile * TILE, (tile + 1) * TILE)
        g_key = turned_back(tile, gk[:, at])
        k_norm = qkv[64:128, at] * lax.rsqrt(squares[1:2, at] * (1.0 / 512) + EPS)
        weighted = g_key * kg
        dots[1:2, at] = jnp.sum(weighted * k_norm, 0, keepdims=True)
        gain_k[...] += g_key * k_norm
        g_value = gv[:, at]
        to_tokens[pl.ds(meta[1, tile], 1), :, :] = jnp.concatenate(
            [gq_weighted[:, at], weighted, g_value], 0
        ).astype(BF)[None]
        keep[:, at] = jnp.where(odd, g_value, g_key)
        send[:, at] = jnp.where(odd, g_key, g_value)
    ones = jnp.ones((8, TILE), F32)
    gains[...] = jnp.concatenate(
        [
            dot(ones, gain_q[...], 1, 1, lax.Precision.HIGHEST),
            dot(ones, gain_k[...], 1, 1, lax.Precision.HIGHEST),
        ],
        1,
    )


def out_grad_kernel(get, put, outs):
    (result,) = outs
    meta, moved = get(0), get(1)
    ctx = lax.axis_index("ctx")
    turned = jnp.concatenate(
        [
            jnp.concatenate(
                [moved[pl.ds(meta[1, tile + 8 * half], 1), 64:128, :][0] for tile in range(8)], 1
            )
            for half in (0, 1)
        ],
        0,
    )
    for i in range(8):
        lanes = pl.ds(pl.multiple_of((slot_of(ctx, PIECES[i]) // 2) * 128, 128), 128)
        parts = []
        for piece in (i, i + 8):
            both = dot(turned, get(2 + piece)[0:1024, :])
            parts.append(both[0:64, 0:64] + both[64:128, 64:128])
        mine, other = parts
        odd = ctx % 2 == 1
        result[:, lanes] = jnp.concatenate(
            [jnp.where(odd, other, mine), jnp.where(odd, mine, other)], 1
        )


def linear_grad_kernel(get, put, outs, whole):
    z = lax.axis_index("fsdp") % 4
    odd = lax.axis_index("ctx") % 2 == 1
    kg = get(6)[...]
    qkv, squares, dots, gq_weighted, keep, other = [get(i) for i in range(6)]
    lows = []
    for tile in range(16):
        at = slice(tile * TILE, (tile + 1) * TILE)
        q_factor = lax.rsqrt(squares[0:1, at] * (1.0 / 1024) + EPS)
        k_factor = lax.rsqrt(squares[1:2, at] * (1.0 / 512) + EPS)
        q_norm = qkv[0:64, at] * q_factor
        k_norm = qkv[64:128, at] * k_factor
        g_q = q_factor * (gq_weighted[:, at] - q_norm * (dots[0:1, at] * (1.0 / 1024)))
        both = keep[:, at] + other[:, at]
        g_k = k_factor * (both * kg - k_norm * (dots[1:2, at] * (1.0 / 512)))
        lows.append(jnp.concatenate([g_q, jnp.where(odd, both, g_k)], 0).astype(BF))
    whole[0:128, :] = dot(jnp.concatenate(lows, 1), get(7)[...])
    out_grad, router_grad, ffn_gain_grad, gains, loss_parts = [get(i) for i in range(8, 13)]
    lane = iota((1, 128), 1)
    tail_rows = jnp.zeros((ROWS_OUT - ROW_LOSS - 1, 128), F32)
    loss = loss_parts[0:1, :]
    whole[128:192, :] = out_grad[...]
    whole[192:224, :] = router_grad[...]
    whole[224:232, :] = jnp.where(iota((8, 1024), 0) == 0, ffn_gain_grad[...], 0.0)
    tail = jnp.concatenate([gains[0:1, :], loss, tail_rows], 0)
    for out, dz in zip(outs, (0, 1, 3, 2)):
        for y in (0, 1):
            at = pl.ds(pl.multiple_of((y * 4 + (z + dz) % 4) * 128, 128), 128)
            out[y] = jnp.concatenate([whole[0:225, at], tail], 0).astype(BF)


def loss_again(total):
    parts = jnp.sum(total[ROW_LOSS : ROW_LOSS + 1, :], 1, keepdims=True)
    first = parts.astype(BF).astype(F32)
    second = (parts - first).astype(BF).astype(F32)
    third = parts - first - second
    lane = iota(total.shape, 1)
    pieces = jnp.where(lane == 0, first, jnp.where(lane == 1, second, third))
    use = (iota(total.shape, 0) == ROW_LOSS) & (lane < 3)
    return jnp.where(use, pieces, total)


def sum_z_kernel(get, put, outs):
    keep, send = outs
    low = lax.axis_index("fsdp") < 4
    parts = [get(i)[...].astype(F32) for i in range(4)]
    total = parts[0] + parts[1] + parts[2] + parts[3]
    keep[...] = jnp.where(low, total[0], total[1])
    send[...] = loss_again(jnp.where(low, total[1], total[0])).astype(BF)


def sum_y_kernel(get, put, outs):
    total = get(0)[...] + get(1)[...].astype(F32)
    outs[0][...] = loss_again(total).astype(BF)


def own_linear_kernel(get, put, outs):
    norms, factors = outs
    hidden, packed, mine, other = [get(i) for i in range(4)]
    even = lax.axis_index("ctx") % 2 == 0
    w_q = jnp.where(even, mine[...], other[...])
    w_k = jnp.where(even, other[:, 0:512], mine[:, 0:512])
    rows = hidden[...].astype(F32)
    factor = lax.rsqrt(jnp.mean(rows * rows, -1, keepdims=True) + EPS)
    gain = packed[192:208, :].astype(F32)[0:1, :]
    low = (rows * factor * gain).astype(BF)
    q_lin = dot(low, w_q).T
    k_lin = dot(low, w_k).T
    q_factor = lax.rsqrt(jnp.mean(q_lin * q_lin, 0, keepdims=True) + EPS)
    k_factor = lax.rsqrt(jnp.mean(k_lin * k_lin, 0, keepdims=True) + EPS)
    norms[0:1024, :] = q_lin * q_factor
    norms[1024:1536, :] = k_lin * k_factor
    factors[...] = jnp.where(iota((8, 128), 0) == 0, q_factor, k_factor)


def input_grad_kernel(get, put, outs):
    (result,) = outs
    norms, factors, moved = get(0), get(1), get(2)
    q = jnp.concatenate([moved[h, 0:64, :] for h in range(16)], 0).astype(F32)

    def key_rows(at):
        pairs = [
            moved[h, at : at + 64, :].astype(F32) + moved[h + 1, at : at + 64, :].astype(F32)
            for h in range(0, 16, 2)
        ]
        return jnp.concatenate(pairs, 0)

    k, v = key_rows(64), key_rows(128)
    q_norm, k_norm = norms[0:1024, :], norms[1024:1536, :]
    g_q = factors[0:1, :] * (q - q_norm * jnp.mean(q * q_norm, 0, keepdims=True))
    g_k = factors[1:2, :] * (k - k_norm * jnp.mean(k * k_norm, 0, keepdims=True))
    g_lin = jnp.concatenate([g_q, g_k, v], 0).astype(BF)
    even = lax.axis_index("ctx") % 2 == 0
    near, far = g_lin[0:1024], g_lin[1024:2048]
    g_normed = dot(jnp.where(even, near, far), get(3)[...], 0, 1)
    g_normed += dot(jnp.where(even, far, near), get(4)[...], 0, 1)
    hidden, packed, g_resid = get(5), get(6), get(7)
    rows = hidden[...].astype(F32)
    factor = lax.rsqrt(jnp.mean(rows * rows, -1, keepdims=True) + EPS)
    n = rows * factor
    gain = packed[192:208, :].astype(F32)[0:1, :]
    weighted = g_normed * gain
    result[...] = g_resid[...] + factor * (
        weighted - n * jnp.mean(weighted * n, -1, keepdims=True)
    )


def stage(target, e, lane, values):
    for slot in range(16):
        at = (2 * slot + e) * FULL
        target[at : at + FULL, lane : lane + 512] = values[slot * CAP : slot * CAP + FULL]


def route_kernel(get, put, outs, spread, named, w_full, out_rows):
    rows, act, result, place, gates, resid_out, post_out, probs = outs[:8]
    gate_pre, up_pre = outs[8:]
    meta, packed = get(0), get(1)
    ctx = lax.axis_index("ctx")
    odd = ctx % 2 == 1
    for n in range(2, 18):
        get(n)
    first_x, first_out, first_w, experts = 18, 2, 34, 36
    for i in range(8):
        lanes = pl.ds(pl.multiple_of((slot_of(ctx, PIECES[i]) // 2) * 128, 128), 128)
        mine = get(first_out + i)[0:1024, :]
        other = get(first_out + i + 8)[0:1024, :]
        low, high = jnp.where(odd, other, mine), jnp.where(odd, mine, other)
        out_rows[0:1024, lanes] = jnp.concatenate([low[:, 0:64], high[:, 0:64]], 1)
        out_rows[1024:2048, lanes] = jnp.concatenate([low[:, 64:128], high[:, 64:128]], 1)
    for n, piece in enumerate(PIECES):
        slot = slot_of(ctx, piece)
        routes = get(first_out + n)[1024:1040, :].astype(F32)[0:8, :]
        for e in (0, 1):
            expert = (2 * ctx + e).astype(F32)
            hit = jnp.max(jnp.where(routes == expert, 1.0, 0.0), 0, keepdims=True)
            named[pl.ds(e * 16 + slot, 1), :] = hit
    place[...] = place_rows(named[...])
    xs = [get(first_x + n) for n in range(16)]
    for core in (0, 1):
        columns = pl.ds(pl.multiple_of(((ctx + core) % 2) * 512, 512), 512)
        w_full[:, columns] = get(first_w + core)[...]
    gain = packed[192:208, :].astype(F32)[1:2, :]
    router = packed[208:240, :]
    for group in range(4):
        slots = [slot_of(ctx, PIECES[group * 4 + j]) for j in range(4)]
        tiles = [pl.ds(pl.multiple_of(meta[0, slot] * TILE, TILE), TILE) for slot in slots]
        mixed = jnp.concatenate([out_rows[at, :] for at in tiles], 0)
        x = jnp.concatenate([xs[group * 4 + j][...] for j in range(4)], 0)
        resid = x.astype(F32) + dot(mixed, w_full[...])
        factor = lax.rsqrt(jnp.mean(resid * resid, -1, keepdims=True) + EPS)
        post = (resid * factor * gain).astype(BF)
        logits = dot(router, post, 1, 1)
        shifted = jnp.exp(logits - jnp.max(logits, 0, keepdims=True))
        p = shifted / jnp.sum(shifted, 0, keepdims=True)
        if group == 0:
            resid_out[...] = resid[0:TILE]
            post_out[...] = post[0:TILE]
            probs[...] = p[:, 0:TILE]
        gate = [
            jnp.sum(jnp.where(iota(p.shape, 0) == 2 * ctx + e, p, 0.0), 0, keepdims=True)
            for e in (0, 1)
        ]
        for j, slot in enumerate(slots):
            own = slice(j * TILE, (j + 1) * TILE)
            at = pl.ds(pl.multiple_of(slot * CAP, 8), CAP)
            picks = []
            for e in (0, 1):
                gates[pl.ds(e * 16 + slot, 1), :] = gate[e][:, own]
                picks.append(place[pl.ds(pl.multiple_of(e * SLOTS + slot * CAP, 8), CAP), :])
            both = dot(jnp.concatenate(picks, 0).astype(BF), post[own])
            spread[at, :] = both[0:CAP]
            spread[pl.ds(pl.multiple_of(SLOTS + slot * CAP, 8), CAP), :] = both[CAP : 2 * CAP]
    rows[...] = spread[...].astype(BF)
    for j in (3, 4, 5, 6, 7, 0):
        put(j)
    weights = get(experts)
    for e in (0, 1):
        gate_w, up_w, down_a, down_b = expert_weights(weights, e)
        x = rows[e * SLOTS : (e + 1) * SLOTS, :]
        gp, up = dot(x, gate_w), dot(x, up_w)
        gate_pre[e] = gp.astype(BF)
        up_pre[e] = up.astype(BF)
        low = (gp * jax.nn.sigmoid(gp) * up).astype(BF)
        act[e] = low
        for j in (8, 9, 1):
            put(j, (e,))
        for lane, down in ((0, down_a), (512, down_b)):
            stage(spread, e, lane, dot(low, down))
            if e == 1:
                lanes = slice(lane, lane + 512)
                result[:, lanes] = spread[0:SENT, lanes].astype(BF)
                put(2, (slice(None), lanes))


def expert_weights(ref, e):
    at = e * 384
    gate = ref[:, at : at + 128, :].reshape(1024, 512)
    up = ref[:, at + 128 : at + 256, :].reshape(1024, 512)
    down_a = ref[:, at + 256 : at + 320, :].reshape(512, 512)
    down_b = ref[:, at + 320 : at + 384, :].reshape(512, 512)
    return gate, up, down_a, down_b


def expert_back_kernel(get, put, outs, spread):
    result, g_rows, g_gate, g_up = outs
    ctx = lax.axis_index("ctx")
    place, gates = get(16), get(17)
    for n in range(16):
        get(n)
    for n, piece in enumerate(PIECES):
        slot = slot_of(ctx, piece)
        at = pl.ds(pl.multiple_of(slot * CAP, 8), CAP)
        picks, scales = [], []
        for e in (0, 1):
            pick = place[pl.ds(pl.multiple_of(e * SLOTS + slot * CAP, 8), CAP), :]
            gate = gates[pl.ds(e * 16 + slot, 1), :]
            scales.append(jnp.sum(pick * gate, 1, keepdims=True))
            picks.append(pick)
        both = dot(jnp.concatenate(picks, 0).astype(BF), get(n)[...])
        spread[at, :] = both[0:CAP] * scales[0]
        second = pl.ds(pl.multiple_of(SLOTS + slot * CAP, 8), CAP)
        spread[second, :] = both[CAP : 2 * CAP] * scales[1]
    g_rows[...] = spread[...].astype(BF)
    put(1)
    weights, gate_pre, up_pre = get(18), get(19), get(20)
    for e in (0, 1):
        gate, up, down_a, down_b = expert_weights(weights, e)
        own = slice(e * SLOTS, (e + 1) * SLOTS)
        g_act = dot(g_rows[own, 0:512], down_a, 1, 1)
        g_act += dot(g_rows[own, 512:1024], down_b, 1, 1)
        gp, up_value = gate_pre[e].astype(F32), up_pre[e].astype(F32)
        sg = jax.nn.sigmoid(gp)
        gg = (g_act * up_value * sg * (1.0 + gp * (1.0 - sg))).astype(BF)
        gu = (g_act * (gp * sg)).astype(BF)
        g_gate[e] = gg
        g_up[e] = gu
        put(2, (e,))
        put(3, (e,))
        for lane in (0, 512):
            part = dot(gg, gate[lane : lane + 512], 1, 1) + dot(gu, up[lane : lane + 512], 1, 1)
            stage(spread, e, lane, part)
            if e == 1:
                lanes = slice(lane, lane + 512)
                result[:, lanes] = spread[0:SENT, lanes].astype(BF)
                put(0, (slice(None), lanes))


def expert_weight_kernel(rows, g_rows, act, g_gate, g_up, result):
    x, g = rows[...], g_rows[...]
    result[:, 0:128, :] = dot(x, g_gate[0], 0, 0).astype(BF).reshape(8, 128, 512)
    result[:, 128:256, :] = dot(x, g_up[0], 0, 0).astype(BF).reshape(8, 128, 512)
    low = act[0]
    result[:, 256:320, :] = dot(low, g[:, 0:512], 0, 0).astype(BF).reshape(8, 64, 512)
    result[:, 320:384, :] = dot(low, g[:, 512:1024], 0, 0).astype(BF).reshape(8, 64, 512)


HALF = pl.BlockSpec((SLOTS, 1024), lambda e: (e, 0))
INNER = pl.BlockSpec((1, SLOTS, 512), lambda e: (e, 0, 0))
WEIGHTS = pl.BlockSpec((8, 384, 512), lambda e: (0, e, 0))


def expert_call(body, outs, out_specs, args, in_specs, name, flops, scratch=()):
    size = sum(int(np.prod(o.shape)) * o.dtype.itemsize for o in outs)
    size += sum(int(np.prod(a.shape)) * a.dtype.itemsize for a in args)
    return pl.pallas_call(
        body,
        grid=(2,),
        out_shape=outs,
        in_specs=in_specs,
        out_specs=out_specs,
        scratch_shapes=list(scratch),
        compiler_params=pltpu.CompilerParams(vmem_limit_bytes=58 * 2**20),
        cost_estimate=pl.CostEstimate(flops=flops, bytes_accessed=size, transcendentals=0),
        name=name,
    )(*args)


def combine_kernel(get, put, outs):
    result, g_result, g_low, loss_parts = outs
    meta, consts = get(0), get(1)
    moved, high, low, resid, teacher = [get(i) for i in range(2, 7)]
    slot = meta[4, 0]
    tile = meta[0, slot]
    room = meta[3, tile] - (tile - meta[2, tile]) * TILE
    valid = (iota((TILE, 1), 0) < room).astype(F32)
    total = resid[...] + dot(high[...], moved[...], 0, 0) + dot(low[...], moved[...], 0, 0)
    result[...] = total.astype(BF)
    errors = (total - teacher[...].astype(F32)) * valid
    g = errors * consts[0:1, 0:1]
    g_result[...] = g
    g_low[...] = g.astype(BF)
    squared = jnp.sum(jnp.sum(errors * errors, 0, keepdims=True), 1, keepdims=True)
    first = squared.astype(BF).astype(F32)
    second = (squared - first).astype(BF).astype(F32)
    third = squared - first - second
    lane = iota((8, 128), 1)
    loss_parts[...] = jnp.where(
        lane == 0, first, jnp.where(lane == 1, second, jnp.where(lane == 2, third, 0.0))
    )


def router_grad_kernel(moved, place, probs, g_result, post, g_logits, router_grad):
    p = probs[...]
    g_high, g_low = split(g_result[...])
    match = dot(moved[...], g_high, 1, 1) + dot(moved[...], g_low, 1, 1)
    picked = place[...].astype(F32) * match
    g_p = dot(slot_experts().astype(F32), picked, 0, 0, lax.Precision.HIGHEST)
    g_z = (p * (g_p - jnp.sum(p * g_p, 0, keepdims=True))).astype(BF)
    g_logits[...] = g_z
    router_grad[...] = dot(g_z, post[...])


def resid_grad_kernel(get, put, outs):
    g_resid_out, ffn_gain_grad, to_heads = outs
    moved, place, g_logits, packed, resid_in, g_result = [get(i) for i in range(6)]
    core = lax.axis_index("ctx") % 2
    g_post = dot(g_logits[...], packed[208:240, :], 0, 0)
    g_post += dot(place[...], moved[...], 0, 0)
    resid = resid_in[...]
    gain = packed[192:208, :].astype(F32)[1:2, :]
    factor = lax.rsqrt(jnp.mean(resid * resid, -1, keepdims=True) + EPS)
    n = resid * factor
    ffn_gain_grad[...] = jnp.broadcast_to(jnp.sum(g_post * n, 0, keepdims=True), (8, 1024))
    weighted = g_post * gain
    g_resid = g_result[...] + factor * (
        weighted - n * jnp.mean(weighted * n, -1, keepdims=True)
    )
    g_resid_out[...] = g_resid
    low = g_resid.astype(BF)
    near, far = low[:, 0:512], low[:, 512:1024]
    mine, other = jnp.where(core == 0, near, far), jnp.where(core == 0, far, near)
    g_mixed = (dot(get(6)[...], mine, 1, 1) + dot(get(7)[...], other, 1, 1)).astype(BF)
    turned = g_resid.T.astype(BF)
    for head in range(16):
        at = slice(head * 64, (head + 1) * 64)
        to_heads[head, 0:64, :] = g_mixed[at]
        to_heads[head, 64:128, :] = turned[at]


def final_kernel(get, put, outs, gain_rows):
    (
        grad_q, grad_k, grad_v, grad_o, router, q_gain, k_gain, ffn_gain, attn_gain, loss,
    ) = outs
    meta, consts, na = [get(i) for i in range(3)]
    odd_core = meta[4, 0] % 2 == 1
    wq, wk, wv = get(3), get(4), get(5)
    x = meta[4, 0] // 4
    shard = meta[4, 1]
    summed = jnp.zeros((ROWS_OUT - ROW_GR, 128), F32)
    for n, dx in enumerate((0, 3, 1, 2)):
        index = (x + dx) % 4
        mine, other = get(6 + n)[...].astype(F32), get(10 + n)[...].astype(F32)
        low, high = jnp.where(odd_core, other, mine), jnp.where(odd_core, mine, other)
        blocks = jnp.stack([low[0], high[0], low[1], high[1]])
        wide = pl.ds(pl.multiple_of(index * 256, 256), 256)
        slim = pl.ds(pl.multiple_of(index * 128, 128), 128)
        grad_q[:, wide] = blocks[:, 0:64, :].reshape(256, 128).T
        grad_o[:, wide] = blocks[:, 128:192, :].reshape(256, 128).T
        grad_k[:, slim] = jnp.concatenate([blocks[0, 64:128], blocks[2, 64:128]], 0).T
        grad_v[:, slim] = jnp.concatenate([blocks[1, 64:128], blocks[3, 64:128]], 0).T
        tails = blocks[:, ROW_GR:, :]
        summed += tails[0] + tails[1] + tails[2] + tails[3]
        for j in range(4):
            gain_rows[pl.ds(index * 4 + j, 1), :] = tails[j, 33:34, :]
    router[...] = summed[0:32]
    even = gain_rows[pl.ds(2 * shard, 1), :]
    odd = gain_rows[pl.ds(2 * shard + 1, 1), :]
    q_gain[...] = jnp.concatenate([even[:, 0:64], odd[:, 0:64]], 1)
    k_gain[...] = (even + odd)[:, 64:128]
    ffn_gain[...] = summed[32:33]
    folded = (
        jnp.sum(grad_q[...] * wq[...].astype(F32), 1, keepdims=True)
        + jnp.sum(grad_k[...] * wk[...].astype(F32), 1, keepdims=True)
        + jnp.sum(grad_v[...] * wv[...].astype(F32), 1, keepdims=True)
    )
    attn_gain[...] = jnp.broadcast_to(folded, (128, 128)).T[0:1, :] / na[...].astype(F32)
    loss[...] = jnp.sum(summed[34:35, :], 1, keepdims=True) * consts[1:2, 0:1]


def unpack_kernel(get, put, outs):
    grad_gate, grad_up, grad_down = outs
    shard = get(0)
    for e in (0, 1):
        at = e * 384
        grad_gate[e] = shard[at : at + 128, :].astype(F32)
        grad_up[e] = shard[at + 128 : at + 256, :].astype(F32)
        grad_down[e, :, 0:512] = shard[at + 256 : at + 320, :].astype(F32)
        grad_down[e, :, 512:1024] = shard[at + 320 : at + 384, :].astype(F32)


def gather_rows(rows, y_again=True):
    across = ctx_move(rows, YHI)
    up, down = ctx_move(rows, XUP), ctx_move(rows, XDOWN)
    across_up = ctx_move(up, YHI) if y_again else ctx_move(across, XUP)
    across_down = ctx_move(across, XDOWN)
    far, across_far = ctx_move(up, XUP), ctx_move(across_down, XDOWN)
    mine = [rows, across, up, down, across_up, across_down, far, across_far]
    return mine + [ctx_move(piece, CORE) for piece in mine]


def sum_ctx(value, beside=()):
    value = value + ctx_move(value, CORE)
    moved, *beside = lax.optimization_barrier((ctx_move(value, YHI), *beside))
    value = value + moved
    up, down, far = ctx_move(value, XUP), ctx_move(value, XDOWN), ctx_move(value, XTWO)
    return value + up + down + far, *beside


def exchange(value, axis):
    return lax.all_to_all(value, axis, split_axis=0, concat_axis=0, tiled=True)


def on_device(
    hidden,
    teacher,
    lengths,
    tile_perm,
    routes,
    norm_attn,
    w_query,
    w_key,
    w_value,
    w_out,
    q_gain,
    k_gain,
    norm_ffn,
    w_router,
    w_gate,
    w_up,
    w_down,
):
    ctx = lax.axis_index("ctx")
    shard = lax.axis_index("fsdp")
    x_in = hidden[0]
    block, expert_block, meta = kernel_call(
        pack_kernel,
        [
            shape((ROWS_IN + 512, 128), BF),
            shape((768, 512), BF),
            shape((5, 16), jnp.int32),
        ],
        [
            lengths, tile_perm, w_query, w_key, w_value, w_router.T,
            norm_attn.reshape(1, 128), norm_ffn.reshape(1, 128),
            q_gain.reshape(1, 128), k_gain.reshape(1, 64),
            w_out, w_gate, w_up, w_down,
        ],
        smem=(0, 1),
        smem_out=(2,),
        name="pack",
    )
    x_first, block = lax.optimization_barrier((x_in, block))
    pieces = gather_rows(x_first)
    other = fsdp_move(block, YLO)
    first = shard < 4
    pair = jnp.stack([jnp.where(first, block, other), jnp.where(first, other, block)])
    pair_moves = [fsdp_move(pair, ZUP), fsdp_move(pair, ZDOWN)]
    pair_moves.append(fsdp_move(pair_moves[0], ZUP))
    *pair_moves, pieces[3], pieces[7] = lax.optimization_barrier(
        (*pair_moves, pieces[3], pieces[7])
    )
    packed, w_mine, qg, kg, consts = kernel_call(
        assemble_kernel,
        [
            shape((ROWS_IN, 1024), BF),
            shape((1024, 512), BF),
            shape((HD, 1), F32),
            shape((HD, 1), F32),
            shape((8, 128), F32),
        ],
        [meta, pair] + pair_moves,
        smem=(0,),
        name="assemble",
    )
    w_other = ctx_move(w_mine, CORE)
    frequencies = 10000.0 ** (-jnp.arange(32, dtype=F32) / 32)
    angles = frequencies[:, None] * jnp.arange(1024, dtype=F32)[None, :]
    cos_t, sin_t = jnp.cos(angles), jnp.sin(angles)
    routes_t = routes[0].T.astype(BF)

    expert_block, *_ = lax.optimization_barrier((expert_block, packed, *pieces[4:8]))
    experts = lax.all_gather(expert_block, "fsdp", axis=0)
    qkv, squares, normed = streamed_call(
        project_kernel,
        [shape((192, 2048), F32), shape((2, 2048), F32), shape((2048, 1024), BF)],
        [meta, packed] + pieces,
        smem=(0,),
        name="project",
        flops=2 * 2048 * 1024 * 192,
    )
    (squares,) = sum_ctx(squares)
    mixed_low, mixed_full, stats, q_t, k_t, k_rows, v_rows = streamed_call(
        attend_kernel,
        [
            shape((1040, 128), BF),
            shape((64, 2048), F32),
            shape((2, 2048), F32),
            shape((64, 2048), BF),
            shape((64, 2048), BF),
            shape((2048, 64), BF),
            shape((2048, 64), BF),
        ],
        [meta, qkv, squares, qg, kg, cos_t, sin_t, routes_t],
        smem=(0,),
        scratch=[pltpu.VMEM((64, 2048), BF)],
        name="attend",
        flops=54 * 4 * 128 * 128 * 64,
    )
    even = ctx % 2 == 0
    qkv_half = jnp.where(even, w_query, jnp.concatenate([w_key, w_value], 1))
    qkv_half, mixed_low = lax.optimization_barrier((qkv_half, mixed_low))
    qkv_mine = lax.all_gather(qkv_half, "fsdp", axis=0, tiled=True)
    mixed_pieces = gather_rows(mixed_low, False)
    (
        rows, act, expert_out, place_here, gates, resid, post, probs, gate_pre, up_pre,
    ) = streamed_call(
        route_kernel,
        [
            shape((2 * SLOTS, 1024), BF),
            shape((2, SLOTS, 512), BF),
            shape((SENT, 1024), BF),
            shape((2 * SLOTS, 128), F32),
            shape((32, 128), F32),
            shape((128, 1024), F32),
            shape((128, 1024), BF),
            shape((32, 128), F32),
            shape((2, SLOTS, 512), BF),
            shape((2, SLOTS, 512), BF),
        ],
        [meta, packed] + mixed_pieces + pieces + [w_mine, w_other, experts],
        smem=(0,),
        stream=range(2, 37),
        stream_out=range(10),
        scratch=[
            pltpu.VMEM((2 * SLOTS, 1024), F32),
            pltpu.VMEM((32, 128), F32),
            pltpu.VMEM((1024, 1024), BF),
            pltpu.VMEM((2048, 1024), BF),
        ],
        name="route_experts",
        flops=2 * 2048 * 1024 * 1024 + 2 * 2 * SLOTS * 1024 * 1536,
    )
    returned = exchange(expert_out, "ctx")
    place, gate_high, gate_low = kernel_call(
        slots_kernel, [shape((SENT, 128), BF)] * 3, [routes_t, probs], name="slots"
    )
    result, g_result, g_low, loss_parts = streamed_call(
        combine_kernel,
        [
            shape((128, 1024), BF),
            shape((128, 1024), F32),
            shape((128, 1024), BF),
            shape((8, 128), F32),
        ],
        [meta, consts, returned, gate_high, gate_low, resid, teacher[0]],
        smem=(0,),
        stream=range(2, 7),
        name="combine",
        flops=2 * SLOTS * 128 * 1024 * 4,
    )
    g_low, qkv_mine = lax.optimization_barrier((g_low, qkv_mine))
    qkv_other = ctx_move(qkv_mine, CORE)
    g_pieces = gather_rows(g_low)
    g_logits, router_grad = kernel_call(
        router_grad_kernel,
        [shape((32, 128), BF), shape((32, 1024), F32)],
        [returned, place, probs, g_result, post],
        name="router_grad",
        brief=True,
    )
    g_rows, g_slots, g_gate, g_up = streamed_call(
        expert_back_kernel,
        [
            shape((SENT, 1024), BF),
            shape((2 * SLOTS, 1024), BF),
            shape((2, SLOTS, 512), BF),
            shape((2, SLOTS, 512), BF),
        ],
        g_pieces + [place_here, gates, experts, gate_pre, up_pre],
        stream=range(21),
        stream_out=range(4),
        scratch=[pltpu.VMEM((2 * SLOTS, 1024), F32)],
        name="experts_back",
        flops=2 * 2 * SLOTS * 1024 * 1536,
    )
    g_returned = exchange(g_rows, "ctx")
    (expert_grads,) = expert_call(
        expert_weight_kernel,
        [shape((8, 768, 512), BF)],
        [WEIGHTS],
        [rows, g_slots, act, g_gate, g_up],
        [HALF, HALF, INNER, INNER, INNER],
        "experts_weights",
        2 * 2 * SLOTS * 1024 * 1536,
    )
    expert_shard = lax.psum_scatter(
        expert_grads.reshape(8 * 768, 512), "fsdp", scatter_dimension=0, tiled=True
    )

    grad_gate, grad_up, grad_down = streamed_call(
        unpack_kernel,
        [shape((2, 128, 512), F32), shape((2, 128, 512), F32), shape((2, 64, 1024), F32)],
        [expert_shard],
        name="unpack",
    )
    g_resid, ffn_gain_grad, to_heads = streamed_call(
        resid_grad_kernel,
        [shape((128, 1024), F32), shape((8, 1024), F32), shape((16, 128, 128), BF)],
        [g_returned, place, g_logits, packed, resid, g_result, w_mine, w_other],
        stream=(0, 1, 4, 5, 6, 7),
        name="resid_grad",
        flops=2 * 128 * 1024 * 2400,
    )
    norms, factors = streamed_call(
        own_linear_kernel,
        [shape((1536, 128), F32), shape((8, 128), F32)],
        [x_in, packed, qkv_mine, qkv_other],
        name="own_linear",
    )
    to_heads, norms, factors = lax.optimization_barrier((to_heads, norms, factors))
    moved = exchange(to_heads.reshape(2048, 128), "ctx").reshape(16, 128, 128)
    to_tokens, gq_weighted, keep, send, dots, gains = streamed_call(
        attend_back_kernel,
        [
            shape((16, 192, 128), BF),
            shape((64, 2048), F32),
            shape((64, 2048), F32),
            shape((64, 2048), F32),
            shape((2, 2048), F32),
            shape((8, 128), F32),
        ],
        [
            meta, moved, qkv, squares, qg, kg, cos_t, sin_t,
            mixed_full, stats, q_t, k_t, k_rows, v_rows,
        ],
        smem=(0,),
        scratch=[
            pltpu.VMEM((64, 2048), F32),
            pltpu.VMEM((64, 2048), F32),
            pltpu.VMEM((64, 128), F32),
            pltpu.VMEM((64, 128), F32),
        ],
        name="attend_back",
        limit=20,
        flops=10**11,
    )
    (out_grad,) = streamed_call(
        out_grad_kernel,
        [shape((64, 1024), F32)],
        [meta, moved] + mixed_pieces,
        smem=(0,),
        name="out_grad",
        limit=20,
        flops=2 * 2048 * 64 * 1024,
    )
    dots, out_grad, received = sum_ctx(dots, (out_grad, ctx_move(send, CORE)))
    to_tokens, dots = lax.optimization_barrier((to_tokens, dots))
    g_lin = exchange(to_tokens.reshape(16 * 192, 128), "ctx").reshape(16, 192, 128)
    scattered = streamed_call(
        linear_grad_kernel,
        [shape((2, ROWS_OUT, 128), BF)] * 4,
        [
            qkv, squares, dots, gq_weighted, keep, received, kg, normed,
            out_grad, router_grad, ffn_gain_grad, gains, loss_parts,
        ],
        stream=(7,),
        scratch=[pltpu.VMEM((232, 1024), F32)],
        name="linear_grad",
        limit=24,
        flops=2 * 2048 * 128 * 1024,
    )
    came = [fsdp_move(part, pairs) for part, pairs in zip(scattered[1:], (ZUP, ZDOWN, ZTWO))]
    keep_z, send_z = streamed_call(
        sum_z_kernel,
        [shape((ROWS_OUT, 128), F32), shape((ROWS_OUT, 128), BF)],
        [scattered[0]] + came,
        name="sum_z",
        limit=8,
    )
    send_z, g_lin = lax.optimization_barrier((send_z, g_lin))
    came_y = fsdp_move(send_z, YLO)
    (summed,) = streamed_call(
        sum_y_kernel,
        [shape((ROWS_OUT, 128), BF)],
        [keep_z, came_y],
        name="sum_y",
        limit=8,
    )
    across, grad_gate, grad_up, grad_down = lax.optimization_barrier(
        (ctx_move(summed, YHI), grad_gate, grad_up, grad_down)
    )
    low_y = (ctx // 2) % 2 == 0
    both = jnp.stack([jnp.where(low_y, summed, across), jnp.where(low_y, across, summed)])
    shares = [both] + [ctx_move(both, pairs) for pairs in (XUP, XDOWN, XTWO)]
    (input_grad,) = streamed_call(
        input_grad_kernel,
        [shape((128, 1024), F32)],
        [norms, factors, g_lin, qkv_mine, qkv_other, x_in, packed, g_resid],
        stream=(3, 4),
        name="input_grad",
        flops=2 * 128 * 2048 * 1024,
    )
    *shares, input_grad = lax.optimization_barrier((*shares, input_grad))
    shares += [ctx_move(share, CORE) for share in shares]
    (
        grad_q, grad_k, grad_v, grad_o, router, q_gain_grad, k_gain_grad, ffn_gain, attn_gain,
        loss,
    ) = streamed_call(
        final_kernel,
        [
            shape((128, 1024), F32),
            shape((128, 512), F32),
            shape((128, 512), F32),
            shape((128, 1024), F32),
            shape((32, 128), F32),
            shape((1, 128), F32),
            shape((1, 64), F32),
            shape((1, 128), F32),
            shape((1, 128), F32),
            shape((1, 1), F32),
        ],
        [
            meta, consts, norm_attn.reshape(1, 128), w_query, w_key, w_value,
        ]
        + shares,
        smem=(0,),
        scratch=[pltpu.VMEM((16, 128), F32)],
        name="final",
        limit=16,
    )
    return (
        result[None],
        loss.reshape(()),
        input_grad[None],
        attn_gain.reshape(128),
        grad_q,
        grad_k,
        grad_v,
        grad_o,
        q_gain_grad.reshape(128),
        k_gain_grad.reshape(64),
        ffn_gain.reshape(128),
        router.T,
        grad_gate,
        grad_up,
        grad_down,
    )


def solution(mesh):
    return jax.shard_map(
        on_device,
        mesh=mesh,
        in_specs=(
            P("fsdp", "ctx", None),
            P("fsdp", "ctx", None),
            P("fsdp", None),
            P("fsdp", None),
            P("fsdp", "ctx", None),
            P("fsdp"),
            P("fsdp", None),
            P("fsdp", None),
            P("fsdp", None),
            P("fsdp", None),
            P("fsdp"),
            P("fsdp"),
            P("fsdp"),
            P("fsdp", None),
            P("ctx", "fsdp", None),
            P("ctx", "fsdp", None),
            P("ctx", "fsdp", None),
        ),
        out_specs=(
            P("fsdp", "ctx", None),
            P(),
            P("fsdp", "ctx", None),
            P("fsdp"),
            P("fsdp", None),
            P("fsdp", None),
            P("fsdp", None),
            P("fsdp", None),
            P("fsdp"),
            P("fsdp"),
            P("fsdp"),
            P("fsdp", None),
            P("ctx", "fsdp", None),
            P("ctx", "fsdp", None),
            P("ctx", "fsdp", None),
        ),
        check_vma=False,
    )
```

```python
import functools

import jax
import jax.numpy as jnp
import numpy as np
from jax import lax
from jax.experimental import pallas as pl
from jax.experimental.pallas import tpu as pltpu
from jax.sharding import PartitionSpec as P

TILE = 128
HD = 64
FULL = 36
CAP = 40
SLOTS = 16 * CAP
SENT = 32 * FULL
EPS = 1e-05
F32 = jnp.float32
BF = jnp.bfloat16

ROW_GAIN = 192
ROW_ROUTER = 208
ROWS_IN = 240
ROW_OUT = 128
ROW_GR = 192
ROW_NF = 224
ROW_LOSS = 226
ROWS_OUT = 240

CORE = [(i, i ^ 1) for i in range(16)]
YHI = [(i, i ^ 2) for i in range(16)]
XUP = [(i, (i + 4) % 16) for i in range(16)]
XDOWN = [(i, (i - 4) % 16) for i in range(16)]
XTWO = [(i, (i + 8) % 16) for i in range(16)]
YLO = [(i, i ^ 4) for i in range(8)]
ZUP = [(i, (i // 4) * 4 + (i + 1) % 4) for i in range(8)]
ZDOWN = [(i, (i // 4) * 4 + (i - 1) % 4) for i in range(8)]
ZTWO = [(i, (i // 4) * 4 + (i + 2) % 4) for i in range(8)]
PIECES = [
    (dx, dy, dc)
    for dc in (0, 1)
    for dx, dy in ((0, 0), (0, 1), (-1, 0), (1, 0), (-1, 1), (1, 1), (2, 0), (2, 1))
]


def ctx_move(value, pairs):
    return lax.ppermute(value, "ctx", pairs)


def fsdp_move(value, pairs):
    return lax.ppermute(value, "fsdp", pairs)


def dims(left, right):
    return (((left,), (right,)), ((), ()))


def dot(a, b, left=1, right=0, precision=None):
    return lax.dot_general(
        a, b, dims(left, right), preferred_element_type=F32, precision=precision
    )


def split(value):
    high = value.astype(BF)
    return high, (value - high.astype(F32)).astype(BF)


def iota(shape, axis):
    return lax.broadcasted_iota(jnp.int32, shape, axis)


def kernel_call(
    body, outs, args, smem=(), smem_out=(), anywhere=(), scratch=(), name=None, flops=0, brief=False
):
    specs = [
        pl.BlockSpec(
            memory_space=pltpu.SMEM if i in smem else pl.ANY if i in anywhere else pltpu.VMEM
        )
        for i in range(len(args))
    ]
    size = sum(int(np.prod(o.shape)) * o.dtype.itemsize for o in outs)
    size += sum(int(np.prod(a.shape)) * a.dtype.itemsize for a in args)
    if brief:
        size = 0
    return pl.pallas_call(
        body,
        out_shape=outs,
        in_specs=specs,
        out_specs=[
            pl.BlockSpec(memory_space=pltpu.SMEM if i in smem_out else pltpu.VMEM)
            for i in range(len(outs))
        ],
        scratch_shapes=list(scratch),
        compiler_params=pltpu.CompilerParams(
            vmem_limit_bytes=58 * 2**20
        ),
        cost_estimate=pl.CostEstimate(flops=flops, bytes_accessed=size, transcendentals=0),
        name=name,
    )(*args)


def streamed_call(
    body, outs, args, smem=(), stream=(), stream_out=(), scratch=(), name=None, flops=0, limit=58
):
    count, results = len(args), len(outs)
    moved, pushed = list(stream), list(stream_out)
    auto = [i for i in range(count) if i not in smem and i not in moved]
    auto_out = [j for j in range(results) if j not in pushed]
    puts = 40

    def kernel(*refs):
        ins, targets = refs[:count], refs[count : count + results]
        rest = refs[count + results :]
        held = dict(zip(moved, rest[: len(moved)]))
        staged = list(targets)
        for j, ref in zip(pushed, rest[len(moved) : len(moved) + len(pushed)]):
            staged[j] = ref
        own = rest[len(moved) + len(pushed) : -2]
        in_sems, out_sems = rest[-2:]
        copies = {}
        for n, i in enumerate(moved):
            copies[i] = pltpu.make_async_copy(ins[i], held[i], in_sems.at[n])
            copies[i].start()
        arrived, sent, started = set(), [], set()

        def get(i):
            if i not in copies:
                return ins[i]
            if i not in arrived:
                copies[i].wait()
                arrived.add(i)
            return held[i]

        def put(j, index=None):
            source = staged[j] if index is None else staged[j].at[index]
            target = targets[j] if index is None else targets[j].at[index]
            copy = pltpu.make_async_copy(source, target, out_sems.at[len(sent)])
            copy.start()
            sent.append(copy)
            started.add(j)

        body(get, put, staged, *own)
        for i in moved:
            get(i)
        for j in pushed:
            if j not in started:
                put(j)
        for copy in sent:
            copy.wait()

    specs = [
        pl.BlockSpec(
            memory_space=pltpu.SMEM if i in smem else pltpu.VMEM if i in auto else pltpu.HBM
        )
        for i in range(count)
    ]
    size = sum(int(np.prod(o.shape)) * o.dtype.itemsize for o in outs)
    size += sum(int(np.prod(a.shape)) * a.dtype.itemsize for a in args)
    buffers = [pltpu.VMEM(args[i].shape, args[i].dtype) for i in moved]
    buffers += [pltpu.VMEM(outs[j].shape, outs[j].dtype) for j in pushed]
    return pl.pallas_call(
        kernel,
        out_shape=outs,
        in_specs=specs,
        out_specs=[
            pl.BlockSpec(memory_space=pltpu.VMEM if j in auto_out else pltpu.HBM)
            for j in range(results)
        ],
        scratch_shapes=buffers
        + list(scratch)
        + [pltpu.SemaphoreType.DMA((max(1, len(moved)),)), pltpu.SemaphoreType.DMA((puts,))],
        compiler_params=pltpu.CompilerParams(vmem_limit_bytes=limit * 2**20),
        cost_estimate=pl.CostEstimate(flops=flops, bytes_accessed=size, transcendentals=0),
        name=name,
    )(*args)


def shape(dims_, dtype):
    return jax.ShapeDtypeStruct(dims_, dtype)


def pack_kernel(
    lens, perm, wq, wk, wv, wr, na, nf, qg, kg, wo, w_gate, w_up, w_down, out, big, meta
):
    ctx = lax.axis_index("ctx")
    for tile in range(16):
        meta[0, tile] = perm[0, tile]
        meta[1, perm[0, tile]] = tile
    start = jnp.int32(0)
    total = jnp.int32(0)
    begins = []
    for seq in range(5):
        length = lens[0, seq]
        begins.append((start, length))
        start = start + (length + TILE - 1) // TILE
        total = total + length
    for tile in range(16):
        first, length = begins[0]
        for begin, own in begins[1:]:
            later = tile >= begin
            first = jnp.where(later, begin, first)
            length = jnp.where(later, own, length)
        meta[2, tile] = first
        meta[3, tile] = length
        meta[4, tile] = ctx if tile == 0 else lax.axis_index("fsdp")
    head = ctx // 2

    def rows_of(ref, pair, half):
        block = ref[:, pl.ds(pl.multiple_of(pair * 128, 128), 128)]
        pick = (iota((HD, 128), 1) == iota((HD, 128), 0) + half * HD).astype(BF)
        return dot(pick, block, 1, 1).astype(BF)

    out[0:64, :] = rows_of(wq, ctx // 2, ctx % 2)
    out[64:128, :] = rows_of(wk, head // 2, head % 2)
    out[128:192, :] = rows_of(wv, head // 2, head % 2)
    lane = iota((1, 128), 1)
    counts = jnp.where(lane == 0, total // 64, jnp.where(lane == 1, total % 64, 0))
    key_gain = jnp.concatenate([kg[...].astype(F32), jnp.zeros((1, 64), F32)], 1)
    out[192:208, :] = jnp.concatenate(
        [
            na[...].astype(F32),
            nf[...].astype(F32),
            qg[...].astype(F32),
            key_gain,
            counts.astype(F32),
            jnp.zeros((11, 128), F32),
        ],
        0,
    ).astype(BF)
    out[208:240, :] = wr[...]
    for e in (0, 1):
        at = e * 384
        big[at : at + 128, :] = w_gate[e]
        big[at + 128 : at + 256, :] = w_up[e]
        big[at + 256 : at + 320, :] = w_down[e, :, 0:512]
        big[at + 320 : at + 384, :] = w_down[e, :, 512:1024]
    for part in range(4):
        lanes = pl.ds(pl.multiple_of((ctx % 2) * 512 + part * 128, 128), 128)
        out[ROWS_IN + part * 128 : ROWS_IN + (part + 1) * 128, :] = wo[:, lanes]


def assemble_kernel(meta, near, up, down, far, packed, w_half, qg, kg, consts):
    ctx, z = meta[4, 0], meta[4, 1] % 4
    for ref, dz in ((near, 0), (up, 3), (down, 1), (far, 2)):
        for y in (0, 1):
            at = pl.ds(pl.multiple_of((y * 4 + (z + dz) % 4) * 128, 128), 128)
            packed[:, at] = ref[y, 0:ROWS_IN]
            for part in range(4):
                first = ROWS_IN + part * 128
                w_half[at, part * 128 : (part + 1) * 128] = ref[y, first : first + 128]
    lanes = pl.ds(pl.multiple_of((ctx // 2) * 128, 128), 128)
    gains = packed[192:208, lanes].astype(F32)
    at, place = iota((HD, 128), 1), iota((HD, 128), 0)
    own = at == place + (ctx % 2) * HD
    qg[...] = jnp.sum(jnp.where(own, gains[2:3, :], 0.0), 1, keepdims=True)
    kg[...] = jnp.sum(jnp.where(at == place, gains[3:4, :], 0.0), 1, keepdims=True)
    counts = packed[192:208, :].astype(F32)[4:5, :]
    lane = iota((1, 1024), 1) % 128
    count = jnp.sum(jnp.where(lane == 0, counts * 64.0, counts), 1, keepdims=True)
    elements = count * 1024.0
    row = iota((8, 128), 0)
    consts[...] = jnp.where(row == 0, 2.0 * 8388608.0 / elements, 1.0 / elements)


def place_rows(named):
    before = (iota((128, 128), 0) < iota((128, 128), 1)).astype(BF)
    rank = jnp.where(named > 0.0, dot(named.astype(BF), before), -1.0)
    place = iota((1, CAP, 1), 1).astype(F32)
    return (rank[:, None, :] == place).astype(F32).reshape(32 * CAP, 128)


def slot_of(ctx, piece):
    dx, dy, dc = piece
    return ((ctx // 4 + dx + 4) % 4) * 4 + (((ctx // 2) % 2 + dy) % 2) * 2 + (ctx + dc) % 2


def slot_experts():
    row, first = iota((SENT, 32), 0), iota((SENT, 32), 1) * FULL
    return (row >= first) & (row < first + FULL)


def slots_kernel(routes_t, probs, out, out_t, high_out, low_out):
    expert = iota((32, 128), 0).astype(F32)
    routes = routes_t[...].astype(F32)
    named = jnp.zeros((32, 128), F32)
    for k in range(8):
        named = jnp.where(routes[k : k + 1, :] == expert, 1.0, named)
    before = (iota((128, 128), 0) < iota((128, 128), 1)).astype(BF)
    rank = jnp.where(named > 0.0, dot(named.astype(BF), before), -1.0)
    of_expert = slot_experts()
    spread = of_expert.astype(F32).astype(BF)
    first = jnp.sum(jnp.where(of_expert, iota((SENT, 32), 1) * FULL, 0), 1, keepdims=True)
    place = (iota((SENT, 1), 0) - first).astype(F32)
    match = dot(spread, rank.astype(BF)) == place
    found = match.astype(F32)
    out[...] = found.astype(BF)
    out_t[...] = found.T.astype(BF)
    p = probs[...]
    p_high = p.astype(BF)
    p_rest = p - p_high.astype(F32)
    p_low = p_rest.astype(BF)
    p_last = (p_rest - p_low.astype(F32)).astype(BF)
    gate = dot(spread, p_high) + dot(spread, p_low) + dot(spread, p_last)
    high, low = split(jnp.where(match, gate, 0.0).T)
    high_out[...] = high
    low_out[...] = low


def project_kernel(get, put, outs):
    qkv, squares, normed = outs
    meta, packed = get(0), get(1)
    ctx = lax.axis_index("ctx")
    weight = packed[0:192, :]
    gain = packed[192:208, :].astype(F32)[0:1, :]
    for n, where in enumerate(PIECES):
        slot = slot_of(ctx, where)
        at = pl.ds(pl.multiple_of(meta[0, slot] * TILE, TILE), TILE)
        rows = get(2 + n)[...].astype(F32)
        factor = lax.rsqrt(jnp.mean(rows * rows, -1, keepdims=True) + EPS)
        low = (rows * factor * gain).astype(BF)
        normed[at, :] = low
        lin = dot(weight, low, 1, 1)
        qkv[:, at] = lin
        squares[0:1, at] = jnp.sum(lin[0:64] * lin[0:64], 0, keepdims=True)
        squares[1:2, at] = 0.5 * jnp.sum(lin[64:128] * lin[64:128], 0, keepdims=True)


def rotate(value, cos, sin):
    a, b = value[0:32], value[32:64]
    return jnp.concatenate([a * cos - b * sin, b * cos + a * sin], 0)


def diagonal_mask(meta, tile):
    room = meta[3, tile] - (tile - meta[2, tile]) * TILE
    key = iota((TILE, TILE), 0)
    return (key <= iota((TILE, TILE), 1)) & (key < room)


def strip_scores(meta, keys, query, tile, first):
    scores = dot(keys, query)
    parts = []
    for other in range(first, tile):
        shift = jnp.where(other >= meta[2, tile], 0.0, -1000000000.0)
        parts.append(scores[(other - first) * TILE : (other - first + 1) * TILE] + shift)
    parts.append(jnp.where(diagonal_mask(meta, tile), scores[-TILE:], -1000000000.0))
    return jnp.concatenate(parts, 0) if len(parts) > 1 else parts[0]


def attend_kernel(get, put, outs, v_t):
    out_low, out_full, stats, q_t, k_t, k_rows, v_rows = outs
    meta, qg, kg = get(0), get(3)[...], get(4)[...]
    routes_t, squares, cos_t, sin_t, qkv = get(7), get(2), get(5), get(6), get(1)
    for tile in range(16):
        at = slice(tile * TILE, (tile + 1) * TILE)
        base = pl.ds(pl.multiple_of((tile - meta[2, tile]) * TILE, TILE), TILE)
        cos, sin = cos_t[:, base], sin_t[:, base]
        q_factor = lax.rsqrt(squares[0:1, at] * (1.0 / 1024) + EPS)
        k_factor = lax.rsqrt(squares[1:2, at] * (1.0 / 512) + EPS)
        query = rotate(qkv[0:64, at] * q_factor * qg, cos, sin)
        key = rotate(qkv[64:128, at] * k_factor * kg, cos, sin)
        value = qkv[128:192, at]
        q_t[:, at] = (query * 0.125).astype(BF)
        k_t[:, at] = key.astype(BF)
        v_t[:, at] = value.astype(BF)
        k_rows[at, :] = key.T.astype(BF)
        v_rows[at, :] = value.T.astype(BF)

    out_low[1024:1040, :] = jnp.concatenate(
        [routes_t[...].astype(F32), jnp.zeros((8, 128), F32)], 0
    ).astype(BF)

    for tile in range(16):
        first = max(0, tile - 7)
        mine = slice(tile * TILE, (tile + 1) * TILE)
        keys = slice(first * TILE, (tile + 1) * TILE)
        scores = strip_scores(meta, k_rows[keys, :], q_t[:, mine], tile, first)
        top = jnp.max(scores, 0, keepdims=True)
        weights = jnp.exp(scores - top)
        total = jnp.sum(weights, 0, keepdims=True)
        mixed = dot(v_t[:, keys], weights.astype(BF)) / total
        out_full[:, mine] = mixed
        half = tile // 8
        rows = slice((tile % 8) * TILE, (tile % 8 + 1) * TILE)
        out_low[rows, half * HD : (half + 1) * HD] = mixed.T.astype(BF)
        stats[0:1, mine] = top
        stats[1:2, mine] = total


def attend_back_kernel(get, put, outs, gk, gv, gain_q, gain_k):
    to_tokens, gq_weighted, keep, send, dots, gains = outs
    meta, qg, kg = get(0), get(4)[...], get(5)[...]
    qkv, squares, cos_t, sin_t, out_full, stats = [get(i) for i in (2, 3, 6, 7, 8, 9)]
    q_t, k_t, k_rows, v_rows, moved = [get(i) for i in (10, 11, 12, 13, 1)]
    gk[...] = jnp.zeros_like(gk)
    gv[...] = jnp.zeros_like(gv)
    gain_q[...] = jnp.zeros_like(gain_q)
    gain_k[...] = jnp.zeros_like(gain_k)

    def turned_back(tile, value):
        base = pl.ds(pl.multiple_of((tile - meta[2, tile]) * TILE, TILE), TILE)
        return rotate(value, cos_t[:, base], -sin_t[:, base])

    for tile in range(16):
        first = max(0, tile - 7)
        mine = slice(tile * TILE, (tile + 1) * TILE)
        keys = slice(first * TILE, (tile + 1) * TILE)
        g_out = moved[pl.ds(meta[1, tile], 1), 0:64, :][0].astype(F32)
        inverse = 1.0 / stats[1:2, mine]
        g_acc = (g_out * inverse).astype(BF)
        shift = jnp.sum(g_out * out_full[:, mine], 0, keepdims=True) * inverse
        query = q_t[:, mine]
        scores = strip_scores(meta, k_rows[keys, :], query, tile, first)
        weights = jnp.exp(scores - stats[0:1, mine])
        g_weights = dot(v_rows[keys, :], g_acc)
        g_scores = (weights * (g_weights - shift)).astype(BF)
        gk[:, keys] += dot(query, g_scores, 1, 1)
        gv[:, keys] += dot(g_acc, weights.astype(BF), 1, 1)
        g_query = turned_back(tile, dot(k_t[:, keys], g_scores) * 0.125)
        factor = lax.rsqrt(squares[0:1, mine] * (1.0 / 1024) + EPS)
        q_norm = qkv[0:64, mine] * factor
        weighted = g_query * qg
        gq_weighted[:, mine] = weighted
        dots[0:1, mine] = jnp.sum(weighted * q_norm, 0, keepdims=True)
        gain_q[...] += g_query * q_norm

    odd = meta[4, 0] % 2 == 1
    for tile in range(16):
        at = slice(tile * TILE, (tile + 1) * TILE)
        g_key = turned_back(tile, gk[:, at])
        k_norm = qkv[64:128, at] * lax.rsqrt(squares[1:2, at] * (1.0 / 512) + EPS)
        weighted = g_key * kg
        dots[1:2, at] = jnp.sum(weighted * k_norm, 0, keepdims=True)
        gain_k[...] += g_key * k_norm
        g_value = gv[:, at]
        to_tokens[pl.ds(meta[1, tile], 1), :, :] = jnp.concatenate(
            [gq_weighted[:, at], weighted, g_value], 0
        ).astype(BF)[None]
        keep[:, at] = jnp.where(odd, g_value, g_key)
        send[:, at] = jnp.where(odd, g_key, g_value)
    ones = jnp.ones((8, TILE), F32)
    gains[...] = jnp.concatenate(
        [
            dot(ones, gain_q[...], 1, 1, lax.Precision.HIGHEST),
            dot(ones, gain_k[...], 1, 1, lax.Precision.HIGHEST),
        ],
        1,
    )


def out_grad_kernel(get, put, outs):
    (result,) = outs
    meta, moved = get(0), get(1)
    ctx = lax.axis_index("ctx")
    turned = jnp.concatenate(
        [
            jnp.concatenate(
                [moved[pl.ds(meta[1, tile + 8 * half], 1), 64:128, :][0] for tile in range(8)], 1
            )
            for half in (0, 1)
        ],
        0,
    )
    for i in range(8):
        lanes = pl.ds(pl.multiple_of((slot_of(ctx, PIECES[i]) // 2) * 128, 128), 128)
        parts = []
        for piece in (i, i + 8):
            both = dot(turned, get(2 + piece)[0:1024, :])
            parts.append(both[0:64, 0:64] + both[64:128, 64:128])
        mine, other = parts
        odd = ctx % 2 == 1
        result[:, lanes] = jnp.concatenate(
            [jnp.where(odd, other, mine), jnp.where(odd, mine, other)], 1
        )


def linear_grad_kernel(get, put, outs, whole):
    z = lax.axis_index("fsdp") % 4
    odd = lax.axis_index("ctx") % 2 == 1
    kg = get(6)[...]
    qkv, squares, dots, gq_weighted, keep, other = [get(i) for i in range(6)]
    lows = []
    for tile in range(16):
        at = slice(tile * TILE, (tile + 1) * TILE)
        q_factor = lax.rsqrt(squares[0:1, at] * (1.0 / 1024) + EPS)
        k_factor = lax.rsqrt(squares[1:2, at] * (1.0 / 512) + EPS)
        q_norm = qkv[0:64, at] * q_factor
        k_norm = qkv[64:128, at] * k_factor
        g_q = q_factor * (gq_weighted[:, at] - q_norm * (dots[0:1, at] * (1.0 / 1024)))
        both = keep[:, at] + other[:, at]
        g_k = k_factor * (both * kg - k_norm * (dots[1:2, at] * (1.0 / 512)))
        lows.append(jnp.concatenate([g_q, jnp.where(odd, both, g_k)], 0).astype(BF))
    whole[0:128, :] = dot(jnp.concatenate(lows, 1), get(7)[...])
    out_grad, router_grad, ffn_gain_grad, gains, loss_parts = [get(i) for i in range(8, 13)]
    lane = iota((1, 128), 1)
    tail_rows = jnp.zeros((ROWS_OUT - ROW_LOSS - 1, 128), F32)
    loss = loss_parts[0:1, :]
    whole[128:192, :] = out_grad[...]
    whole[192:224, :] = router_grad[...]
    whole[224:232, :] = jnp.where(iota((8, 1024), 0) == 0, ffn_gain_grad[...], 0.0)
    tail = jnp.concatenate([gains[0:1, :], loss, tail_rows], 0)
    for out, dz in zip(outs, (0, 1, 3, 2)):
        for y in (0, 1):
            at = pl.ds(pl.multiple_of((y * 4 + (z + dz) % 4) * 128, 128), 128)
            out[y] = jnp.concatenate([whole[0:225, at], tail], 0).astype(BF)


def loss_again(total):
    parts = jnp.sum(total[ROW_LOSS : ROW_LOSS + 1, :], 1, keepdims=True)
    first = parts.astype(BF).astype(F32)
    second = (parts - first).astype(BF).astype(F32)
    third = parts - first - second
    lane = iota(total.shape, 1)
    pieces = jnp.where(lane == 0, first, jnp.where(lane == 1, second, third))
    use = (iota(total.shape, 0) == ROW_LOSS) & (lane < 3)
    return jnp.where(use, pieces, total)


def sum_z_kernel(get, put, outs):
    keep, send = outs
    low = lax.axis_index("fsdp") < 4
    parts = [get(i)[...].astype(F32) for i in range(4)]
    total = parts[0] + parts[1] + parts[2] + parts[3]
    keep[...] = jnp.where(low, total[0], total[1])
    send[...] = loss_again(jnp.where(low, total[1], total[0])).astype(BF)


def sum_y_kernel(get, put, outs):
    total = get(0)[...] + get(1)[...].astype(F32)
    outs[0][...] = loss_again(total).astype(BF)


def own_linear_kernel(get, put, outs):
    norms, factors = outs
    hidden, packed, mine, other = [get(i) for i in range(4)]
    even = lax.axis_index("ctx") % 2 == 0
    w_q = jnp.where(even, mine[...], other[...])
    w_k = jnp.where(even, other[:, 0:512], mine[:, 0:512])
    rows = hidden[...].astype(F32)
    factor = lax.rsqrt(jnp.mean(rows * rows, -1, keepdims=True) + EPS)
    gain = packed[192:208, :].astype(F32)[0:1, :]
    low = (rows * factor * gain).astype(BF)
    q_lin = dot(low, w_q).T
    k_lin = dot(low, w_k).T
    q_factor = lax.rsqrt(jnp.mean(q_lin * q_lin, 0, keepdims=True) + EPS)
    k_factor = lax.rsqrt(jnp.mean(k_lin * k_lin, 0, keepdims=True) + EPS)
    norms[0:1024, :] = q_lin * q_factor
    norms[1024:1536, :] = k_lin * k_factor
    factors[...] = jnp.where(iota((8, 128), 0) == 0, q_factor, k_factor)


def input_grad_kernel(get, put, outs):
    (result,) = outs
    norms, factors, moved = get(0), get(1), get(2)
    q = jnp.concatenate([moved[h, 0:64, :] for h in range(16)], 0).astype(F32)

    def key_rows(at):
        pairs = [
            moved[h, at : at + 64, :].astype(F32) + moved[h + 1, at : at + 64, :].astype(F32)
            for h in range(0, 16, 2)
        ]
        return jnp.concatenate(pairs, 0)

    k, v = key_rows(64), key_rows(128)
    q_norm, k_norm = norms[0:1024, :], norms[1024:1536, :]
    g_q = factors[0:1, :] * (q - q_norm * jnp.mean(q * q_norm, 0, keepdims=True))
    g_k = factors[1:2, :] * (k - k_norm * jnp.mean(k * k_norm, 0, keepdims=True))
    g_lin = jnp.concatenate([g_q, g_k, v], 0).astype(BF)
    even = lax.axis_index("ctx") % 2 == 0
    near, far = g_lin[0:1024], g_lin[1024:2048]
    g_normed = dot(jnp.where(even, near, far), get(3)[...], 0, 1)
    g_normed += dot(jnp.where(even, far, near), get(4)[...], 0, 1)
    hidden, packed, g_resid = get(5), get(6), get(7)
    rows = hidden[...].astype(F32)
    factor = lax.rsqrt(jnp.mean(rows * rows, -1, keepdims=True) + EPS)
    n = rows * factor
    gain = packed[192:208, :].astype(F32)[0:1, :]
    weighted = g_normed * gain
    result[...] = g_resid[...] + factor * (
        weighted - n * jnp.mean(weighted * n, -1, keepdims=True)
    )


def stage(target, e, lane, values):
    for slot in range(16):
        at = (2 * slot + e) * FULL
        target[at : at + FULL, lane : lane + 512] = values[slot * CAP : slot * CAP + FULL]


def route_kernel(get, put, outs, spread, named, w_full, out_rows):
    rows, act, result, place, gates, resid_out, post_out, probs = outs[:8]
    gate_pre, up_pre = outs[8:]
    meta, packed = get(0), get(1)
    ctx = lax.axis_index("ctx")
    odd = ctx % 2 == 1
    for n in range(2, 18):
        get(n)
    first_x, first_out, first_w, experts = 18, 2, 34, 36
    for i in range(8):
        lanes = pl.ds(pl.multiple_of((slot_of(ctx, PIECES[i]) // 2) * 128, 128), 128)
        mine = get(first_out + i)[0:1024, :]
        other = get(first_out + i + 8)[0:1024, :]
        low, high = jnp.where(odd, other, mine), jnp.where(odd, mine, other)
        out_rows[0:1024, lanes] = jnp.concatenate([low[:, 0:64], high[:, 0:64]], 1)
        out_rows[1024:2048, lanes] = jnp.concatenate([low[:, 64:128], high[:, 64:128]], 1)
    for n, piece in enumerate(PIECES):
        slot = slot_of(ctx, piece)
        routes = get(first_out + n)[1024:1040, :].astype(F32)[0:8, :]
        for e in (0, 1):
            expert = (2 * ctx + e).astype(F32)
            hit = jnp.max(jnp.where(routes == expert, 1.0, 0.0), 0, keepdims=True)
            named[pl.ds(e * 16 + slot, 1), :] = hit
    place[...] = place_rows(named[...])
    xs = [get(first_x + n) for n in range(16)]
    for core in (0, 1):
        columns = pl.ds(pl.multiple_of(((ctx + core) % 2) * 512, 512), 512)
        w_full[:, columns] = get(first_w + core)[...]
    gain = packed[192:208, :].astype(F32)[1:2, :]
    router = packed[208:240, :]
    for group in range(4):
        slots = [slot_of(ctx, PIECES[group * 4 + j]) for j in range(4)]
        tiles = [pl.ds(pl.multiple_of(meta[0, slot] * TILE, TILE), TILE) for slot in slots]
        mixed = jnp.concatenate([out_rows[at, :] for at in tiles], 0)
        x = jnp.concatenate([xs[group * 4 + j][...] for j in range(4)], 0)
        resid = x.astype(F32) + dot(mixed, w_full[...])
        factor = lax.rsqrt(jnp.mean(resid * resid, -1, keepdims=True) + EPS)
        post = (resid * factor * gain).astype(BF)
        logits = dot(router, post, 1, 1)
        shifted = jnp.exp(logits - jnp.max(logits, 0, keepdims=True))
        p = shifted / jnp.sum(shifted, 0, keepdims=True)
        if group == 0:
            resid_out[...] = resid[0:TILE]
            post_out[...] = post[0:TILE]
            probs[...] = p[:, 0:TILE]
        gate = [
            jnp.sum(jnp.where(iota(p.shape, 0) == 2 * ctx + e, p, 0.0), 0, keepdims=True)
            for e in (0, 1)
        ]
        for j, slot in enumerate(slots):
            own = slice(j * TILE, (j + 1) * TILE)
            at = pl.ds(pl.multiple_of(slot * CAP, 8), CAP)
            picks = []
            for e in (0, 1):
                gates[pl.ds(e * 16 + slot, 1), :] = gate[e][:, own]
                picks.append(place[pl.ds(pl.multiple_of(e * SLOTS + slot * CAP, 8), CAP), :])
            both = dot(jnp.concatenate(picks, 0).astype(BF), post[own])
            spread[at, :] = both[0:CAP]
            spread[pl.ds(pl.multiple_of(SLOTS + slot * CAP, 8), CAP), :] = both[CAP : 2 * CAP]
    rows[...] = spread[...].astype(BF)
    for j in (3, 4, 5, 6, 7, 0):
        put(j)
    weights = get(experts)
    for e in (0, 1):
        gate_w, up_w, down_a, down_b = expert_weights(weights, e)
        x = rows[e * SLOTS : (e + 1) * SLOTS, :]
        gp, up = dot(x, gate_w), dot(x, up_w)
        gate_pre[e] = gp.astype(BF)
        up_pre[e] = up.astype(BF)
        low = (gp * jax.nn.sigmoid(gp) * up).astype(BF)
        act[e] = low
        for j in (8, 9, 1):
            put(j, (e,))
        for lane, down in ((0, down_a), (512, down_b)):
            stage(spread, e, lane, dot(low, down))
            if e == 1:
                lanes = slice(lane, lane + 512)
                result[:, lanes] = spread[0:SENT, lanes].astype(BF)
                put(2, (slice(None), lanes))


def expert_weights(ref, e):
    at = e * 384
    gate = ref[:, at : at + 128, :].reshape(1024, 512)
    up = ref[:, at + 128 : at + 256, :].reshape(1024, 512)
    down_a = ref[:, at + 256 : at + 320, :].reshape(512, 512)
    down_b = ref[:, at + 320 : at + 384, :].reshape(512, 512)
    return gate, up, down_a, down_b


def expert_back_kernel(get, put, outs, spread):
    result, g_rows, g_gate, g_up = outs
    ctx = lax.axis_index("ctx")
    place, gates = get(16), get(17)
    for n in range(16):
        get(n)
    for n, piece in enumerate(PIECES):
        slot = slot_of(ctx, piece)
        at = pl.ds(pl.multiple_of(slot * CAP, 8), CAP)
        picks, scales = [], []
        for e in (0, 1):
            pick = place[pl.ds(pl.multiple_of(e * SLOTS + slot * CAP, 8), CAP), :]
            gate = gates[pl.ds(e * 16 + slot, 1), :]
            scales.append(jnp.sum(pick * gate, 1, keepdims=True))
            picks.append(pick)
        both = dot(jnp.concatenate(picks, 0).astype(BF), get(n)[...])
        spread[at, :] = both[0:CAP] * scales[0]
        second = pl.ds(pl.multiple_of(SLOTS + slot * CAP, 8), CAP)
        spread[second, :] = both[CAP : 2 * CAP] * scales[1]
    g_rows[...] = spread[...].astype(BF)
    put(1)
    weights, gate_pre, up_pre = get(18), get(19), get(20)
    for e in (0, 1):
        gate, up, down_a, down_b = expert_weights(weights, e)
        own = slice(e * SLOTS, (e + 1) * SLOTS)
        g_act = dot(g_rows[own, 0:512], down_a, 1, 1)
        g_act += dot(g_rows[own, 512:1024], down_b, 1, 1)
        gp, up_value = gate_pre[e].astype(F32), up_pre[e].astype(F32)
        sg = jax.nn.sigmoid(gp)
        gg = (g_act * up_value * sg * (1.0 + gp * (1.0 - sg))).astype(BF)
        gu = (g_act * (gp * sg)).astype(BF)
        g_gate[e] = gg
        g_up[e] = gu
        put(2, (e,))
        put(3, (e,))
        for lane in (0, 512):
            part = dot(gg, gate[lane : lane + 512], 1, 1) + dot(gu, up[lane : lane + 512], 1, 1)
            stage(spread, e, lane, part)
            if e == 1:
                lanes = slice(lane, lane + 512)
                result[:, lanes] = spread[0:SENT, lanes].astype(BF)
                put(0, (slice(None), lanes))


def expert_weight_kernel(rows, g_rows, act, g_gate, g_up, result):
    x, g = rows[...].astype(F32).T.astype(BF), g_rows[...]
    result[:, 0:128, :] = dot(x, g_gate[0]).astype(BF).reshape(8, 128, 512)
    result[:, 128:256, :] = dot(x, g_up[0]).astype(BF).reshape(8, 128, 512)
    low = act[0]
    result[:, 256:320, :] = dot(low, g[:, 0:512], 0, 0).astype(BF).reshape(8, 64, 512)
    result[:, 320:384, :] = dot(low, g[:, 512:1024], 0, 0).astype(BF).reshape(8, 64, 512)


HALF = pl.BlockSpec((SLOTS, 1024), lambda e: (e, 0))
INNER = pl.BlockSpec((1, SLOTS, 512), lambda e: (e, 0, 0))
WEIGHTS = pl.BlockSpec((8, 384, 512), lambda e: (0, e, 0))


def expert_call(body, outs, out_specs, args, in_specs, name, flops, scratch=()):
    size = sum(int(np.prod(o.shape)) * o.dtype.itemsize for o in outs)
    size += sum(int(np.prod(a.shape)) * a.dtype.itemsize for a in args)
    return pl.pallas_call(
        body,
        grid=(2,),
        out_shape=outs,
        in_specs=in_specs,
        out_specs=out_specs,
        scratch_shapes=list(scratch),
        compiler_params=pltpu.CompilerParams(vmem_limit_bytes=58 * 2**20),
        cost_estimate=pl.CostEstimate(flops=flops, bytes_accessed=size, transcendentals=0),
        name=name,
    )(*args)


def combine_kernel(get, put, outs):
    result, g_result, g_low, loss_parts = outs
    meta, consts = get(0), get(1)
    moved, high, low, resid, teacher = [get(i) for i in range(2, 7)]
    slot = meta[4, 0]
    tile = meta[0, slot]
    room = meta[3, tile] - (tile - meta[2, tile]) * TILE
    valid = (iota((TILE, 1), 0) < room).astype(F32)
    total = resid[...] + dot(high[...], moved[...]) + dot(low[...], moved[...])
    result[...] = total.astype(BF)
    errors = (total - teacher[...].astype(F32)) * valid
    g = errors * consts[0:1, 0:1]
    g_result[...] = g
    g_low[...] = g.astype(BF)
    squared = jnp.sum(jnp.sum(errors * errors, 0, keepdims=True), 1, keepdims=True)
    first = squared.astype(BF).astype(F32)
    second = (squared - first).astype(BF).astype(F32)
    third = squared - first - second
    lane = iota((8, 128), 1)
    loss_parts[...] = jnp.where(
        lane == 0, first, jnp.where(lane == 1, second, jnp.where(lane == 2, third, 0.0))
    )


def router_grad_kernel(moved, place, probs, g_result, post, g_logits, router_grad):
    p = probs[...]
    g_high, g_low = split(g_result[...])
    match = dot(moved[...], g_high, 1, 1) + dot(moved[...], g_low, 1, 1)
    picked = place[...].astype(F32) * match
    g_p = dot(slot_experts().astype(F32), picked, 0, 0, lax.Precision.HIGHEST)
    g_z = (p * (g_p - jnp.sum(p * g_p, 0, keepdims=True))).astype(BF)
    g_logits[...] = g_z
    router_grad[...] = dot(g_z, post[...])


def resid_grad_kernel(get, put, outs):
    g_resid_out, ffn_gain_grad, to_heads = outs
    moved, place, g_logits, packed, resid_in, g_result = [get(i) for i in range(6)]
    core = lax.axis_index("ctx") % 2
    g_post = dot(g_logits[...], packed[208:240, :], 0, 0)
    g_post += dot(place[...], moved[...])
    resid = resid_in[...]
    gain = packed[192:208, :].astype(F32)[1:2, :]
    factor = lax.rsqrt(jnp.mean(resid * resid, -1, keepdims=True) + EPS)
    n = resid * factor
    ffn_gain_grad[...] = jnp.broadcast_to(jnp.sum(g_post * n, 0, keepdims=True), (8, 1024))
    weighted = g_post * gain
    g_resid = g_result[...] + factor * (
        weighted - n * jnp.mean(weighted * n, -1, keepdims=True)
    )
    g_resid_out[...] = g_resid
    low = g_resid.astype(BF)
    near, far = low[:, 0:512], low[:, 512:1024]
    mine, other = jnp.where(core == 0, near, far), jnp.where(core == 0, far, near)
    g_mixed = (dot(get(6)[...], mine, 1, 1) + dot(get(7)[...], other, 1, 1)).astype(BF)
    turned = g_resid.T.astype(BF)
    for head in range(16):
        at = slice(head * 64, (head + 1) * 64)
        to_heads[head, 0:64, :] = g_mixed[at]
        to_heads[head, 64:128, :] = turned[at]


def final_kernel(get, put, outs, gain_rows):
    (
        grad_q, grad_k, grad_v, grad_o, router, q_gain, k_gain, ffn_gain, attn_gain, loss,
    ) = outs
    meta, consts, na = [get(i) for i in range(3)]
    odd_core = meta[4, 0] % 2 == 1
    wq, wk, wv = get(3), get(4), get(5)
    x = meta[4, 0] // 4
    shard = meta[4, 1]
    summed = jnp.zeros((ROWS_OUT - ROW_GR, 128), F32)
    for n, dx in enumerate((0, 3, 1, 2)):
        index = (x + dx) % 4
        mine, other = get(6 + n)[...].astype(F32), get(10 + n)[...].astype(F32)
        low, high = jnp.where(odd_core, other, mine), jnp.where(odd_core, mine, other)
        blocks = jnp.stack([low[0], high[0], low[1], high[1]])
        wide = pl.ds(pl.multiple_of(index * 256, 256), 256)
        slim = pl.ds(pl.multiple_of(index * 128, 128), 128)
        grad_q[:, wide] = blocks[:, 0:64, :].reshape(256, 128).T
        grad_o[:, wide] = blocks[:, 128:192, :].reshape(256, 128).T
        grad_k[:, slim] = jnp.concatenate([blocks[0, 64:128], blocks[2, 64:128]], 0).T
        grad_v[:, slim] = jnp.concatenate([blocks[1, 64:128], blocks[3, 64:128]], 0).T
        tails = blocks[:, ROW_GR:, :]
        summed += tails[0] + tails[1] + tails[2] + tails[3]
        for j in range(4):
            gain_rows[pl.ds(index * 4 + j, 1), :] = tails[j, 33:34, :]
    router[...] = summed[0:32]
    even = gain_rows[pl.ds(2 * shard, 1), :]
    odd = gain_rows[pl.ds(2 * shard + 1, 1), :]
    q_gain[...] = jnp.concatenate([even[:, 0:64], odd[:, 0:64]], 1)
    k_gain[...] = (even + odd)[:, 64:128]
    ffn_gain[...] = summed[32:33]
    folded = (
        jnp.sum(grad_q[...] * wq[...].astype(F32), 1, keepdims=True)
        + jnp.sum(grad_k[...] * wk[...].astype(F32), 1, keepdims=True)
        + jnp.sum(grad_v[...] * wv[...].astype(F32), 1, keepdims=True)
    )
    attn_gain[...] = jnp.broadcast_to(folded, (128, 128)).T[0:1, :] / na[...].astype(F32)
    loss[...] = jnp.sum(summed[34:35, :], 1, keepdims=True) * consts[1:2, 0:1]


def unpack_kernel(get, put, outs):
    grad_gate, grad_up, grad_down = outs
    shard = get(0)
    for e in (0, 1):
        at = e * 384
        grad_gate[e] = shard[at : at + 128, :].astype(F32)
        grad_up[e] = shard[at + 128 : at + 256, :].astype(F32)
        grad_down[e, :, 0:512] = shard[at + 256 : at + 320, :].astype(F32)
        grad_down[e, :, 512:1024] = shard[at + 320 : at + 384, :].astype(F32)


def gather_rows(rows, y_again=True):
    across = ctx_move(rows, YHI)
    up, down = ctx_move(rows, XUP), ctx_move(rows, XDOWN)
    across_up = ctx_move(up, YHI) if y_again else ctx_move(across, XUP)
    across_down = ctx_move(across, XDOWN)
    far, across_far = ctx_move(up, XUP), ctx_move(across_down, XDOWN)
    mine = [rows, across, up, down, across_up, across_down, far, across_far]
    return mine + [ctx_move(piece, CORE) for piece in mine]


def sum_ctx(value, beside=()):
    value = value + ctx_move(value, CORE)
    moved, *beside = lax.optimization_barrier((ctx_move(value, YHI), *beside))
    value = value + moved
    up, down, far = ctx_move(value, XUP), ctx_move(value, XDOWN), ctx_move(value, XTWO)
    return value + up + down + far, *beside


def exchange(value, axis):
    return lax.all_to_all(value, axis, split_axis=0, concat_axis=0, tiled=True)


def on_device(
    hidden,
    teacher,
    lengths,
    tile_perm,
    routes,
    norm_attn,
    w_query,
    w_key,
    w_value,
    w_out,
    q_gain,
    k_gain,
    norm_ffn,
    w_router,
    w_gate,
    w_up,
    w_down,
):
    ctx = lax.axis_index("ctx")
    shard = lax.axis_index("fsdp")
    x_in = hidden[0]
    block, expert_block, meta = kernel_call(
        pack_kernel,
        [
            shape((ROWS_IN + 512, 128), BF),
            shape((768, 512), BF),
            shape((5, 16), jnp.int32),
        ],
        [
            lengths, tile_perm, w_query, w_key, w_value, w_router.T,
            norm_attn.reshape(1, 128), norm_ffn.reshape(1, 128),
            q_gain.reshape(1, 128), k_gain.reshape(1, 64),
            w_out, w_gate, w_up, w_down,
        ],
        smem=(0, 1),
        smem_out=(2,),
        name="pack",
    )
    x_first, block = lax.optimization_barrier((x_in, block))
    pieces = gather_rows(x_first)
    other = fsdp_move(block, YLO)
    first = shard < 4
    pair = jnp.stack([jnp.where(first, block, other), jnp.where(first, other, block)])
    pair_moves = [fsdp_move(pair, ZUP), fsdp_move(pair, ZDOWN)]
    pair_moves.append(fsdp_move(pair_moves[0], ZUP))
    *pair_moves, pieces[3], pieces[7] = lax.optimization_barrier(
        (*pair_moves, pieces[3], pieces[7])
    )
    packed, w_mine, qg, kg, consts = kernel_call(
        assemble_kernel,
        [
            shape((ROWS_IN, 1024), BF),
            shape((1024, 512), BF),
            shape((HD, 1), F32),
            shape((HD, 1), F32),
            shape((8, 128), F32),
        ],
        [meta, pair] + pair_moves,
        smem=(0,),
        name="assemble",
    )
    w_other = ctx_move(w_mine, CORE)
    frequencies = 10000.0 ** (-jnp.arange(32, dtype=F32) / 32)
    angles = frequencies[:, None] * jnp.arange(1024, dtype=F32)[None, :]
    cos_t, sin_t = jnp.cos(angles), jnp.sin(angles)
    routes_t = routes[0].T.astype(BF)

    expert_block, *_ = lax.optimization_barrier((expert_block, packed, *pieces[4:8]))
    experts = lax.all_gather(expert_block, "fsdp", axis=0)
    qkv, squares, normed = streamed_call(
        project_kernel,
        [shape((192, 2048), F32), shape((2, 2048), F32), shape((2048, 1024), BF)],
        [meta, packed] + pieces,
        smem=(0,),
        name="project",
        flops=2 * 2048 * 1024 * 192,
    )
    (squares,) = sum_ctx(squares)
    mixed_low, mixed_full, stats, q_t, k_t, k_rows, v_rows = streamed_call(
        attend_kernel,
        [
            shape((1040, 128), BF),
            shape((64, 2048), F32),
            shape((2, 2048), F32),
            shape((64, 2048), BF),
            shape((64, 2048), BF),
            shape((2048, 64), BF),
            shape((2048, 64), BF),
        ],
        [meta, qkv, squares, qg, kg, cos_t, sin_t, routes_t],
        smem=(0,),
        scratch=[pltpu.VMEM((64, 2048), BF)],
        name="attend",
        flops=54 * 4 * 128 * 128 * 64,
    )
    even = ctx % 2 == 0
    qkv_half = jnp.where(even, w_query, jnp.concatenate([w_key, w_value], 1))
    qkv_half, mixed_low = lax.optimization_barrier((qkv_half, mixed_low))
    qkv_mine = lax.all_gather(qkv_half, "fsdp", axis=0, tiled=True)
    mixed_pieces = gather_rows(mixed_low, False)
    (
        rows, act, expert_out, place_here, gates, resid, post, probs, gate_pre, up_pre,
    ) = streamed_call(
        route_kernel,
        [
            shape((2 * SLOTS, 1024), BF),
            shape((2, SLOTS, 512), BF),
            shape((SENT, 1024), BF),
            shape((2 * SLOTS, 128), F32),
            shape((32, 128), F32),
            shape((128, 1024), F32),
            shape((128, 1024), BF),
            shape((32, 128), F32),
            shape((2, SLOTS, 512), BF),
            shape((2, SLOTS, 512), BF),
        ],
        [meta, packed] + mixed_pieces + pieces + [w_mine, w_other, experts],
        smem=(0,),
        stream=range(2, 37),
        stream_out=range(10),
        scratch=[
            pltpu.VMEM((2 * SLOTS, 1024), F32),
            pltpu.VMEM((32, 128), F32),
            pltpu.VMEM((1024, 1024), BF),
            pltpu.VMEM((2048, 1024), BF),
        ],
        name="route_experts",
        flops=2 * 2048 * 1024 * 1024 + 2 * 2 * SLOTS * 1024 * 1536,
    )
    returned = exchange(expert_out, "ctx")
    place, place_t, gate_high, gate_low = kernel_call(
        slots_kernel,
        [shape((SENT, 128), BF)] + [shape((128, SENT), BF)] * 3,
        [routes_t, probs],
        name="slots",
    )
    result, g_result, g_low, loss_parts = streamed_call(
        combine_kernel,
        [
            shape((128, 1024), BF),
            shape((128, 1024), F32),
            shape((128, 1024), BF),
            shape((8, 128), F32),
        ],
        [meta, consts, returned, gate_high, gate_low, resid, teacher[0]],
        smem=(0,),
        stream=range(2, 7),
        name="combine",
        flops=2 * SLOTS * 128 * 1024 * 4,
    )
    g_low, qkv_mine = lax.optimization_barrier((g_low, qkv_mine))
    qkv_other = ctx_move(qkv_mine, CORE)
    g_pieces = gather_rows(g_low)
    g_logits, router_grad = kernel_call(
        router_grad_kernel,
        [shape((32, 128), BF), shape((32, 1024), F32)],
        [returned, place, probs, g_result, post],
        name="router_grad",
        brief=True,
    )
    g_rows, g_slots, g_gate, g_up = streamed_call(
        expert_back_kernel,
        [
            shape((SENT, 1024), BF),
            shape((2 * SLOTS, 1024), BF),
            shape((2, SLOTS, 512), BF),
            shape((2, SLOTS, 512), BF),
        ],
        g_pieces + [place_here, gates, experts, gate_pre, up_pre],
        stream=range(21),
        stream_out=range(4),
        scratch=[pltpu.VMEM((2 * SLOTS, 1024), F32)],
        name="experts_back",
        flops=2 * 2 * SLOTS * 1024 * 1536,
    )
    g_returned = exchange(g_rows, "ctx")
    (expert_grads,) = expert_call(
        expert_weight_kernel,
        [shape((8, 768, 512), BF)],
        [WEIGHTS],
        [rows, g_slots, act, g_gate, g_up],
        [HALF, HALF, INNER, INNER, INNER],
        "experts_weights",
        2 * 2 * SLOTS * 1024 * 1536,
    )
    expert_shard = lax.psum_scatter(
        expert_grads.reshape(8 * 768, 512), "fsdp", scatter_dimension=0, tiled=True
    )

    grad_gate, grad_up, grad_down = streamed_call(
        unpack_kernel,
        [shape((2, 128, 512), F32), shape((2, 128, 512), F32), shape((2, 64, 1024), F32)],
        [expert_shard],
        name="unpack",
    )
    g_resid, ffn_gain_grad, to_heads = streamed_call(
        resid_grad_kernel,
        [shape((128, 1024), F32), shape((8, 1024), F32), shape((16, 128, 128), BF)],
        [g_returned, place_t, g_logits, packed, resid, g_result, w_mine, w_other],
        stream=(0, 1, 4, 5, 6, 7),
        name="resid_grad",
        flops=2 * 128 * 1024 * 2400,
    )
    norms, factors = streamed_call(
        own_linear_kernel,
        [shape((1536, 128), F32), shape((8, 128), F32)],
        [x_in, packed, qkv_mine, qkv_other],
        name="own_linear",
    )
    to_heads, norms, factors = lax.optimization_barrier((to_heads, norms, factors))
    moved = exchange(to_heads.reshape(2048, 128), "ctx").reshape(16, 128, 128)
    to_tokens, gq_weighted, keep, send, dots, gains = streamed_call(
        attend_back_kernel,
        [
            shape((16, 192, 128), BF),
            shape((64, 2048), F32),
            shape((64, 2048), F32),
            shape((64, 2048), F32),
            shape((2, 2048), F32),
            shape((8, 128), F32),
        ],
        [
            meta, moved, qkv, squares, qg, kg, cos_t, sin_t,
            mixed_full, stats, q_t, k_t, k_rows, v_rows,
        ],
        smem=(0,),
        scratch=[
            pltpu.VMEM((64, 2048), F32),
            pltpu.VMEM((64, 2048), F32),
            pltpu.VMEM((64, 128), F32),
            pltpu.VMEM((64, 128), F32),
        ],
        name="attend_back",
        limit=20,
        flops=10**11,
    )
    (out_grad,) = streamed_call(
        out_grad_kernel,
        [shape((64, 1024), F32)],
        [meta, moved] + mixed_pieces,
        smem=(0,),
        name="out_grad",
        limit=20,
        flops=2 * 2048 * 64 * 1024,
    )
    dots, out_grad, received = sum_ctx(dots, (out_grad, ctx_move(send, CORE)))
    to_tokens, dots = lax.optimization_barrier((to_tokens, dots))
    g_lin = exchange(to_tokens.reshape(16 * 192, 128), "ctx").reshape(16, 192, 128)
    scattered = streamed_call(
        linear_grad_kernel,
        [shape((2, ROWS_OUT, 128), BF)] * 4,
        [
            qkv, squares, dots, gq_weighted, keep, received, kg, normed,
            out_grad, router_grad, ffn_gain_grad, gains, loss_parts,
        ],
        stream=(7,),
        scratch=[pltpu.VMEM((232, 1024), F32)],
        name="linear_grad",
        limit=24,
        flops=2 * 2048 * 128 * 1024,
    )
    came = [fsdp_move(part, pairs) for part, pairs in zip(scattered[1:], (ZUP, ZDOWN, ZTWO))]
    keep_z, send_z = streamed_call(
        sum_z_kernel,
        [shape((ROWS_OUT, 128), F32), shape((ROWS_OUT, 128), BF)],
        [scattered[0]] + came,
        name="sum_z",
        limit=8,
    )
    send_z, g_lin = lax.optimization_barrier((send_z, g_lin))
    came_y = fsdp_move(send_z, YLO)
    (summed,) = streamed_call(
        sum_y_kernel,
        [shape((ROWS_OUT, 128), BF)],
        [keep_z, came_y],
        name="sum_y",
        limit=8,
    )
    across, grad_gate, grad_up, grad_down = lax.optimization_barrier(
        (ctx_move(summed, YHI), grad_gate, grad_up, grad_down)
    )
    low_y = (ctx // 2) % 2 == 0
    both = jnp.stack([jnp.where(low_y, summed, across), jnp.where(low_y, across, summed)])
    shares = [both] + [ctx_move(both, pairs) for pairs in (XUP, XDOWN, XTWO)]
    (input_grad,) = streamed_call(
        input_grad_kernel,
        [shape((128, 1024), F32)],
        [norms, factors, g_lin, qkv_mine, qkv_other, x_in, packed, g_resid],
        stream=(3, 4),
        name="input_grad",
        flops=2 * 128 * 2048 * 1024,
    )
    *shares, input_grad = lax.optimization_barrier((*shares, input_grad))
    shares += [ctx_move(share, CORE) for share in shares]
    (
        grad_q, grad_k, grad_v, grad_o, router, q_gain_grad, k_gain_grad, ffn_gain, attn_gain,
        loss,
    ) = streamed_call(
        final_kernel,
        [
            shape((128, 1024), F32),
            shape((128, 512), F32),
            shape((128, 512), F32),
            shape((128, 1024), F32),
            shape((32, 128), F32),
            shape((1, 128), F32),
            shape((1, 64), F32),
            shape((1, 128), F32),
            shape((1, 128), F32),
            shape((1, 1), F32),
        ],
        [
            meta, consts, norm_attn.reshape(1, 128), w_query, w_key, w_value,
        ]
        + shares,
        smem=(0,),
        scratch=[pltpu.VMEM((16, 128), F32)],
        name="final",
        limit=16,
    )
    return (
        result[None],
        loss.reshape(()),
        input_grad[None],
        attn_gain.reshape(128),
        grad_q,
        grad_k,
        grad_v,
        grad_o,
        q_gain_grad.reshape(128),
        k_gain_grad.reshape(64),
        ffn_gain.reshape(128),
        router.T,
        grad_gate,
        grad_up,
        grad_down,
    )


def solution(mesh):
    return jax.shard_map(
        on_device,
        mesh=mesh,
        in_specs=(
            P("fsdp", "ctx", None),
            P("fsdp", "ctx", None),
            P("fsdp", None),
            P("fsdp", None),
            P("fsdp", "ctx", None),
            P("fsdp"),
            P("fsdp", None),
            P("fsdp", None),
            P("fsdp", None),
            P("fsdp", None),
            P("fsdp"),
            P("fsdp"),
            P("fsdp"),
            P("fsdp", None),
            P("ctx", "fsdp", None),
            P("ctx", "fsdp", None),
            P("ctx", "fsdp", None),
        ),
        out_specs=(
            P("fsdp", "ctx", None),
            P(),
            P("fsdp", "ctx", None),
            P("fsdp"),
            P("fsdp", None),
            P("fsdp", None),
            P("fsdp", None),
            P("fsdp", None),
            P("fsdp"),
            P("fsdp"),
            P("fsdp"),
            P("fsdp", None),
            P("ctx", "fsdp", None),
            P("ctx", "fsdp", None),
            P("ctx", "fsdp", None),
        ),
        check_vma=False,
    )
```
